256 devices in a mesh: seq: 64 (over z, x, core), head: 4 (over y).
Axes of the slice: x: 4, y: 4, z: 8, core: 2. Of those that a mesh axis runs over, the one named last changes fastest.
Arguments:
- queries: bfloat16 [8704, 1024], P('seq', 'head'), may hold values from -5 to 5
- key_rows: bfloat16 [8704, 1024], P('seq', 'head'), may hold values from -5 to 5
- value_rows: bfloat16 [8704, 1024], P('seq', 'head'), may hold values from -6 to 6
- scale_of: int32 [8704], P('seq'), may hold values from -1 to 12, as said below
- wo: bfloat16 [1024, 2048], P('head'), may hold values from -0.1875 to 0.1875
- dy: bfloat16 [8704, 2048], P('seq', 'head'), may hold values from -16 to 16
Outputs:
- block_out: bfloat16 [8704, 2048], P('seq', 'head')
- dq: bfloat16 [8704, 1024], P('seq', 'head')
- dk: bfloat16 [8704, 1024], P('seq', 'head')
- dv: bfloat16 [8704, 1024], P('seq', 'head')
- dwo: float32 [1024, 2048], P('head', 'seq')
The draws below stay inside these ranges and needn't reach their ends.
Inputs may be any that keep to these rules, and one draw needn't show every extreme that they name: `scale_of`: in each aligned block of 136 rows (one index of seq) the first 128 rows hold ids 13 - 3 to 12, not falling over these rows of all blocks taken in order, each of the three ids present; the last 8 rows of a block are all -1 except in exactly 4 blocks, whose last rows hold ids 0 to 9, not falling within the block.
All inputs are finite; a program needn't handle non-finite values.
Results may differ from the reference program's by a relative error of at most 0.035.
Values may be sent and summed in bfloat16 or wider, within the bound.
No kernel may reach another device: no remote copies, remote signals or barrier semaphores. Data moves between devices by JAX's collectives and lax.ppermute only.
A program may use at most 192 MiB of HBM per device.

```python
import jax
import jax.numpy as jnp
from jax import lax

D = 2048
HEADS = 8
DH = 128
TOK_DEV = 128
CSLOT = 8
OWNERS = 4
NSCALE = 13
ROWS_DEV = 136
NTOK = 8704


def draw_queries(key, part):
    key = jax.random.fold_in(key, 3)
    first = jax.random.fold_in(key, 0)
    values = jnp.clip(1.6 * jax.random.normal(first, (NTOK, HEADS * DH), jnp.float32), -5.0, 5.0)
    return values.astype(jnp.bfloat16)


def draw_key_rows(key, part):
    key = jax.random.fold_in(key, 5)
    first = jax.random.fold_in(key, 0)
    values = jnp.clip(1.6 * jax.random.normal(first, (NTOK, HEADS * DH), jnp.float32), -5.0, 5.0)
    return values.astype(jnp.bfloat16)


def draw_scale_of(key, part):
    key = jax.random.fold_in(key, 11)
    key_one, key_two, key_three, key_four = jax.random.split(key, 4)
    blocks = NTOK // ROWS_DEV
    nfine = blocks * TOK_DEV
    bound_one = jax.random.randint(key_one, (), nfine // 6, nfine // 4)
    bound_two = jax.random.randint(key_two, (), 2 * nfine // 5, nfine // 2)
    place = jnp.arange(nfine, dtype=jnp.int32)
    fine_ids = NSCALE - 3 + (place >= bound_one).astype(jnp.int32) + (place >= bound_two).astype(jnp.int32)
    ncoarse = OWNERS * CSLOT
    cuts = jnp.sort(jax.random.randint(key_three, (NSCALE - 4,), 0, ncoarse + 1))
    slots = jnp.arange(ncoarse, dtype=jnp.int32)
    coarse_ids = jnp.sum((slots[:, None] >= cuts[None, :]).astype(jnp.int32), axis=1).reshape(OWNERS, CSLOT)
    shuffle = jax.random.permutation(key_four, blocks)
    rank = jnp.argsort(shuffle).astype(jnp.int32)
    owned = rank < OWNERS
    coarse_rows = coarse_ids[jnp.minimum(rank, OWNERS - 1)]
    coarse_rows = jnp.where(owned[:, None], coarse_rows, -1)
    merged = jnp.concatenate([fine_ids.reshape(blocks, TOK_DEV), coarse_rows], axis=1)
    return merged.reshape(NTOK).astype(jnp.int32)


def with_spikes(values, key, source, target, parts, factor):
    owner, partner = [(jnp.arange(values.shape[axis_at]) // (values.shape[axis_at] // parts)).reshape([-1 if axis == axis_at else 1 for axis in range(values.ndim)]) for axis_at in (source, target)]
    chosen = jax.random.permutation(key, parts)[partner]
    strong = (owner == chosen) | (owner == (partner + parts // 2) % parts)
    return jnp.where(strong, factor * values, values)


def levels(stream_key, shape, shards, least, top_value):
    gain, own = 1.0, jax.random.fold_in(stream_key, 6)
    for position, shards_of in shards:
        draws = jnp.exp(jax.random.uniform(jax.random.fold_in(own, position), (shards_of,), jnp.float32, least / len(shards), top_value / len(shards)))
        gain = gain * jnp.repeat(draws, shape[position] // shards_of).reshape([-1 if axis == position else 1 for axis in range(len(shape))])
    return gain


def scatter_about(rng, dims, width, limit, pieces=(), held_as=jnp.bfloat16):
    entries = jax.random.normal(rng, dims, jnp.float32) * width
    if len(pieces) > 0:
        entries = levels(rng, dims, pieces, -0.22, 0.18) * entries
    return jnp.clip(entries, min=-limit, max=limit).astype(held_as)


def bell_draw_with(rng, dims, width, limit, cuts, heavy, kind=jnp.bfloat16):
    entries = width * jax.random.normal(rng, dims, jnp.float32)
    if cuts:
        entries = entries * levels(rng, dims, cuts, -0.22, 0.18)
    return jnp.clip(with_spikes(entries, jax.random.fold_in(rng, 3), *heavy), -limit, limit).astype(kind)


def setup_inputs(seed: int = 0) -> dict:
    key_list = jax.random.split(jax.random.key(seed), 7)
    return {
        "queries": draw_queries(jax.random.fold_in(key_list[6], 71), 0),
        "key_rows": draw_key_rows(jax.random.fold_in(key_list[6], 71), 0),
        "value_rows": scatter_about(key_list[2], (NTOK, HEADS * DH), 1.0, 6.0, ((0, 64), (1, 4))),
        "scale_of": draw_scale_of(jax.random.fold_in(key_list[6], 71), 0),
        "wo": scatter_about(key_list[4], (HEADS * DH, D), (HEADS * DH) ** -0.5, 0.1875, ((0, 4),)),
        "dy": bell_draw_with(key_list[5], (NTOK, D), 1.0, 16.0, ((0, 64), (1, 4)), (0, 1, 64, 4.0)),
    }


def reference(queries, key_rows, value_rows, scale_of, wo, dy):
    scale = DH ** -0.5
    seen = (scale_of[None, :] >= 0) & (scale_of[None, :] <= scale_of[:, None])
    valid = (scale_of >= 0).astype(jnp.float32)

    def split(x):
        return x.reshape(NTOK, HEADS, DH).transpose(1, 0, 2)

    def merge(x):
        return x.transpose(1, 0, 2).reshape(NTOK, HEADS * DH)

    q_heads, k_heads, v_heads = split(queries), split(key_rows), split(value_rows)

    def logits(q_one, k_one):
        s = jnp.dot(q_one, k_one.T, preferred_element_type=jnp.float32) * scale
        return jnp.where(seen, s, -1e30)

    def forward_head(items):
        q_one, k_one, v_one = items
        s = logits(q_one, k_one)
        top = jnp.max(s, axis=1, keepdims=True)
        lse = top + jnp.log(jnp.sum(jnp.exp(s - top), axis=1, keepdims=True))
        weights = jnp.exp(s - lse).astype(jnp.bfloat16)
        out = jnp.dot(weights, v_one, preferred_element_type=jnp.float32) * valid[:, None]
        return out.astype(jnp.bfloat16), lse[:, 0]

    attn_heads, lse = lax.map(forward_head, (q_heads, k_heads, v_heads))
    attn = merge(attn_heads)
    block_out = jnp.dot(attn, wo, preferred_element_type=jnp.float32).astype(jnp.bfloat16)
    dattn = (jnp.dot(dy, wo.T, preferred_element_type=jnp.float32) * valid[:, None]).astype(jnp.bfloat16)
    dattn_heads = split(dattn)
    delta = jnp.sum(dattn_heads.astype(jnp.float32) * attn_heads.astype(jnp.float32), axis=2)

    def backward_head(items):
        q_one, k_one, v_one, d_one, lse_one, delta_one = items
        s = logits(q_one, k_one)
        prob = jnp.exp(s - lse_one[:, None])
        dprob = jnp.dot(d_one, v_one.T, preferred_element_type=jnp.float32)
        dscore = (prob * (dprob - delta_one[:, None]) * scale).astype(jnp.bfloat16)
        dq_one = jnp.dot(dscore, k_one, preferred_element_type=jnp.float32).astype(jnp.bfloat16)
        dk_one = jnp.dot(dscore.T, q_one, preferred_element_type=jnp.float32).astype(jnp.bfloat16)
        dv_one = jnp.dot(prob.astype(jnp.bfloat16).T, d_one, preferred_element_type=jnp.float32).astype(jnp.bfloat16)
        return dq_one, dk_one, dv_one

    dq_h, dk_h, dv_h = lax.map(backward_head, (q_heads, k_heads, v_heads, dattn_heads, lse, delta))
    dwo = jnp.dot(attn.T, dy, preferred_element_type=jnp.float32)
    return (block_out, merge(dq_h), merge(dk_h), merge(dv_h), dwo)
```

```python
import functools
import math

import jax
import jax.numpy as jnp
from jax import lax
from jax.experimental import pallas as pl
from jax.experimental.pallas import tpu as pltpu
from jax.sharding import Mesh, PartitionSpec as P

DH = 128
BIG = -1e30
SCALE = DH ** (-0.5)
UNIT = SCALE * math.log2(math.e)
F32 = jnp.float32
BF16 = jnp.bfloat16
LAST = (((1,), (1,)), ((), ()))


def forward_kernel(q_ref, qm_ref, kv_ref, km_ref, da_ref, o_ref, stat_ref):
    rows = q_ref.shape[0]
    lane = lax.broadcasted_iota(jnp.int32, (rows, DH), 1)
    stat = jnp.zeros((rows, DH), F32)
    for head in range(2):
        cols = slice(head * DH, (head + 1) * DH)
        q_ext = jnp.concatenate([q_ref[:, cols], qm_ref[...]], axis=1)
        k_ext = jnp.concatenate([kv_ref[:, cols], km_ref[...]], axis=1)
        s = lax.dot_general(q_ext, k_ext, LAST, preferred_element_type=F32)
        top = jnp.max(s, axis=1, keepdims=True)
        p = jnp.exp2((s - top) * UNIT)
        total = jnp.sum(p, axis=1, keepdims=True)
        v = kv_ref[:, 2 * DH + head * DH : 2 * DH + (head + 1) * DH]
        o = jnp.dot(p.astype(BF16), v, preferred_element_type=F32) / total
        o_ref[:, cols] = o.astype(BF16)
        lse = top * UNIT + jnp.log2(total)
        share = jnp.sum(o * da_ref[:, cols].astype(F32), axis=1, keepdims=True)
        stat = jnp.where(lane == head, lse, stat)
        stat = jnp.where(lane == 2 + head, share, stat)
    stat_ref[...] = stat.T[:8]


def backward_kernel(q_ref, qm_ref, da_ref, kv_ref, km_ref, stat_ref, dq_ref, dkv_ref, ds_ref, row_ref):
    step = pl.program_id(0)
    block = kv_ref.shape[0]

    @pl.when(step == 0)
    def _():
        stat = stat_ref[...]
        lse_each = stat[:, 0:2]
        top = jnp.max(lse_each, axis=0)
        weight = jnp.exp2(lse_each - top[None])
        total = jnp.sum(weight, axis=0)
        lse = top + jnp.log2(total)
        row_ref[0:2] = jnp.where(lse < -1e28, 1e30, lse)
        row_ref[2:4] = jnp.sum(weight * stat[:, 2:4], axis=0) / total

    for head in range(2):
        cols = slice(head * DH, (head + 1) * DH)
        vcols = slice(2 * DH + head * DH, 2 * DH + (head + 1) * DH)
        q = q_ref[:, cols]
        da = da_ref[:, cols]
        q_ext = jnp.concatenate([q, qm_ref[...]], axis=1)
        k_ext = jnp.concatenate([kv_ref[:, cols], km_ref[...]], axis=1)
        s = lax.dot_general(k_ext, q_ext, LAST, preferred_element_type=F32)
        p = jnp.exp2(s * UNIT - row_ref[head : head + 1, :])
        dp = lax.dot_general(kv_ref[:, vcols], da, LAST, preferred_element_type=F32)
        ds = (p * (dp - row_ref[2 + head : 3 + head, :])).astype(BF16)
        dkv_ref[:, vcols] = jnp.dot(p.astype(BF16), da, preferred_element_type=F32).astype(BF16)
        dkv_ref[:, cols] = (jnp.dot(ds, q, preferred_element_type=F32) * SCALE).astype(BF16)
        ds_ref[head, pl.ds(pl.multiple_of(step * block, block), block), :] = ds


def query_kernel(ds_ref, kv_ref, dq_ref):
    for head in range(2):
        cols = slice(head * DH, (head + 1) * DH)
        dq = lax.dot_general(ds_ref[head], kv_ref[:, cols], (((0,), (0,)), ((), ())), preferred_element_type=F32)
        dq_ref[:, cols] = (dq * SCALE).astype(BF16)


def backward(q_ref, qm_ref, da_ref, kv_ref, km_ref, kv_all_ref, stat_ref, dq_ref, dkv_ref, ds_ref, row_ref):
    backward_kernel(q_ref, qm_ref, da_ref, kv_ref, km_ref, stat_ref, dq_ref, dkv_ref, ds_ref, row_ref)

    @pl.when(pl.program_id(0) == pl.num_programs(0) - 1)
    def _():
        query_kernel(ds_ref, kv_all_ref, dq_ref)


def local(queries, key_rows, value_rows, scale_of, wo, dy):
    rows, feats = queries.shape
    valid = (scale_of >= 0).astype(F32)
    kv = lax.all_gather(jnp.concatenate([key_rows, value_rows], axis=1), "z", axis=0, tiled=True)
    q = lax.all_gather(queries, "xc", axis=0, tiled=True)
    q_ids = lax.all_gather(scale_of, "xc", axis=0, tiled=True)
    k_ids = lax.all_gather(scale_of, "z", axis=0, tiled=True)
    dy_full = lax.all_gather(dy, "head", axis=1, tiled=True)
    da_own = (
        jnp.einsum("td,fd->tf", dy_full, wo, preferred_element_type=F32) * valid[:, None]
    ).astype(BF16)
    da = lax.all_gather(da_own, "xc", axis=0, tiled=True)

    lane = jnp.arange(DH, dtype=jnp.int32)[None, :]
    hidden = ((lane > q_ids[:, None]) & (lane < 13)) | (lane == 13)
    qm = jnp.where(hidden, BIG, 0.0).astype(BF16)
    km = (lane == jnp.where(k_ids < 0, 13, k_ids)[:, None]).astype(BF16)

    nq, nk = q.shape[0], kv.shape[0]
    blocks = 4
    qb, kb = nq // blocks, nk // blocks
    qpad = 384

    def whole(shape):
        return pl.BlockSpec(shape, lambda i: (0,) * len(shape))

    o, stat = pl.pallas_call(
        forward_kernel,
        grid=(blocks,),
        in_specs=[
            pl.BlockSpec((qb, feats), lambda i: (i, 0)),
            pl.BlockSpec((qb, DH), lambda i: (i, 0)),
            whole((nk, 2 * feats)),
            whole((nk, DH)),
            pl.BlockSpec((qb, feats), lambda i: (i, 0)),
        ],
        out_specs=[
            pl.BlockSpec((qb, feats), lambda i: (i, 0)),
            pl.BlockSpec((None, 8, qb), lambda i: (i, 0, 0)),
        ],
        out_shape=[
            jax.ShapeDtypeStruct((nq, feats), BF16),
            jax.ShapeDtypeStruct((blocks, 8, qb), F32),
        ],
        compiler_params=pltpu.CompilerParams(vmem_limit_bytes=48 << 20),
    )(q, qm, kv, km, da)
    stat = stat[:, :4].transpose(1, 0, 2).reshape(4, nq)
    stats = lax.all_gather(stat, "xc", axis=0, tiled=False)

    dq_part, dkv_part = pl.pallas_call(
        backward,
        grid=(blocks,),
        in_specs=[
            whole((nq, feats)),
            whole((nq, DH)),
            whole((nq, feats)),
            pl.BlockSpec((kb, 2 * feats), lambda i: (i, 0)),
            pl.BlockSpec((kb, DH), lambda i: (i, 0)),
            whole((nk, 2 * feats)),
            whole(stats.shape),
        ],
        out_specs=[
            whole((nq, feats)),
            pl.BlockSpec((kb, 2 * feats), lambda i: (i, 0)),
        ],
        out_shape=[
            jax.ShapeDtypeStruct((nq, feats), BF16),
            jax.ShapeDtypeStruct((nk, 2 * feats), BF16),
        ],
        scratch_shapes=[
            pltpu.VMEM((2, nk, nq), BF16),
            pltpu.VMEM((4, nq), F32),
        ],
        compiler_params=pltpu.CompilerParams(vmem_limit_bytes=48 << 20),
    )(q, qm, da, kv, km, kv, stats)

    lse_each = stats[:, 0:2]
    weight = jax.nn.softmax(lse_each * math.log(2.0), axis=0)
    mine = jnp.take(weight, lax.axis_index("xc"), axis=0)
    o_part = (o.reshape(nq, 2, DH).astype(F32) * mine.T[:, :, None]).reshape(nq, feats).astype(BF16)
    attn = lax.psum_scatter(o_part, "xc", scatter_dimension=0, tiled=True)
    attn = (attn.astype(F32) * valid[:, None]).astype(BF16)
    partial_out = jnp.dot(attn, wo, preferred_element_type=F32).astype(BF16)
    block_out = lax.psum_scatter(partial_out, "head", scatter_dimension=1, tiled=True)
    dwo = lax.psum_scatter(
        jnp.einsum("tf,td->fd", attn, dy_full, preferred_element_type=F32),
        ("z", "xc"),
        scatter_dimension=1,
        tiled=True,
    )
    dq = lax.psum_scatter(dq_part, "xc", scatter_dimension=0, tiled=True)
    dkv = lax.psum_scatter(dkv_part, "z", scatter_dimension=0, tiled=True)
    return (block_out, dq, dkv[:, :feats], dkv[:, feats:], dwo)


def solution(mesh):
    fine = Mesh(mesh.devices.reshape(8, 8, 4), ("z", "xc", "head"))
    seq = ("z", "xc")
    placed = (
        P(seq, "head"),
        P(seq, "head"),
        P(seq, "head"),
        P(seq),
        P("head", None),
        P(seq, "head"),
    )
    return jax.shard_map(
        local,
        mesh=fine,
        in_specs=placed,
        out_specs=(
            P(seq, "head"),
            P(seq, "head"),
            P(seq, "head"),
            P(seq, "head"),
            P("head", seq),
        ),
        check_vma=False,
    )
```

```python
import math

import jax
import jax.numpy as jnp
from jax import lax
from jax.experimental import pallas as pl
from jax.experimental.pallas import tpu as pltpu
from jax.sharding import Mesh, PartitionSpec as P

DH = 128
ROWS = 136
PAD = 144
FINE = 128
REST = PAD - FINE
PAIR = 2 * PAD
NH = 4
QHALF = 8
KHALF = 16
NQ = QHALF * PAD
NK = KHALF * PAD
QREST = QHALF * FINE
KREST = KHALF * FINE
FEATS = 2 * DH
MODEL = 2048
WIDE = MODEL // NH
COLS = 32
BLOCK = 384
BIG = -1e30
SCALE = DH ** (-0.5)
UNIT = SCALE * math.log2(math.e)
F32 = jnp.float32
BF16 = jnp.bfloat16
LAST = (((1,), (1,)), ((), ()))
FIRST = (((0,), (0,)), ((), ()))
PARAMS = pltpu.CompilerParams(vmem_limit_bytes=48 << 20)
VMEM = pl.BlockSpec(memory_space=pltpu.VMEM)
SMEM = pl.BlockSpec(memory_space=pltpu.SMEM)


def shape(dims, kind=BF16):
    return jax.ShapeDtypeStruct(dims, kind)


def call(kernel, name, ins, outs, scratch=(), scalars=0):
    return pl.pallas_call(
        kernel,
        in_specs=[SMEM] * scalars + [VMEM] * (len(ins) - scalars),
        out_shape=outs,
        scratch_shapes=list(scratch),
        compiler_params=PARAMS,
        name=name,
    )(*ins)


def to_and_from(e, first, second, keep_ref, send_ref):
    @pl.when(e == 0)
    def _():
        keep_ref[...] = first
        send_ref[...] = second

    @pl.when(e == 1)
    def _():
        keep_ref[...] = second
        send_ref[...] = first


def pack_kernel(e_ref, q_ref, k_ref, v_ref, ids_ref, keep_ref, send_ref):
    ids = ids_ref[...].astype(BF16)
    zero = jnp.zeros((8, DH), BF16)
    heads = []
    for head in range(2):
        cols = slice(head * DH, (head + 1) * DH)
        top = jnp.concatenate([q_ref[:, cols], k_ref[:, cols], v_ref[:, cols]], axis=1)
        heads.append(jnp.concatenate([top, jnp.concatenate([ids, ids, zero], axis=1)], axis=0))
    to_and_from(e_ref[0], heads[0], heads[1], keep_ref, send_ref)


def dattn_kernel(at_ref, dy0_ref, dy1_ref, dy2_ref, dy3_ref, wo_ref, ids_ref, keep_ref, send_ref):
    h = at_ref[1]
    acc = jnp.zeros((ROWS, FEATS), F32)
    for s, ref in enumerate((dy0_ref, dy1_ref, dy2_ref, dy3_ref)):
        start = pl.multiple_of(lax.rem(h - s + NH, NH) * WIDE, WIDE)
        acc = acc + lax.dot_general(ref[...], wo_ref[:, pl.ds(start, WIDE)], LAST, preferred_element_type=F32)
    ids = ids_ref[...].T
    keep = jnp.concatenate([ids[:, 0:1], ids[0:8, 1:2]], axis=0) >= 0.0
    acc = jnp.where(keep, acc, 0.0).astype(BF16)
    acc = jnp.concatenate([acc, jnp.zeros((PAD - ROWS, FEATS), BF16)], axis=0)
    to_and_from(at_ref[0], acc[:, 0:DH], acc[:, DH:FEATS], keep_ref, send_ref)


def assemble(pair_refs, all_ref, rest):
    for j, ref in enumerate(pair_refs):
        for k in range(2):
            half = 2 * j + k
            all_ref[half * FINE : (half + 1) * FINE] = ref[k * PAD : k * PAD + FINE]
            all_ref[rest + half * REST : rest + (half + 1) * REST] = ref[k * PAD + FINE : (k + 1) * PAD]


def take_pair(value, j, rest):
    pieces = []
    for half in (2 * j, 2 * j + 1):
        pieces.append(value[half * FINE : (half + 1) * FINE])
        pieces.append(value[rest + half * REST : rest + (half + 1) * REST])
    return jnp.concatenate(pieces, axis=0)


def masks(pair_refs, mask_ref, rest, is_query):
    fine, last = [], []
    for ref in pair_refs:
        for k in range(2):
            rows = ref[k * PAD + FINE : (k + 1) * PAD, 0:DH].astype(F32)
            fine.append(rows[8:9])
            last.append(rows[9:10])
    fine = jnp.concatenate(fine, axis=0).T
    last = jnp.concatenate(last, axis=0).T

    def encode(column):
        lane = lax.broadcasted_iota(jnp.int32, (column.shape[0], DH), 1).astype(F32)
        if is_query:
            hidden = ((lane > column) & (lane < 13.0)) | (lane == 13.0)
            return jnp.where(hidden, BIG, 0.0).astype(BF16)
        return jnp.where(lane == jnp.where(column < 0.0, 13.0, column), 1.0, 0.0).astype(BF16)

    for half in range(2 * len(pair_refs)):
        mask_ref[half * FINE : (half + 1) * FINE] = encode(fine[:, half : half + 1])
        mask_ref[rest + half * REST : rest + (half + 1) * REST] = encode(last[0:REST, half : half + 1])


def forward_kernel(*refs):
    q_parts, da_parts, kv_parts = refs[0:4], refs[4:8], refs[8:16]
    o_refs, stat_ref, q_ref, qm_ref, kv_ref, km_ref, da_ref, oall_ref = refs[16:20], *refs[20:27]
    assemble(q_parts, q_ref, QREST)
    assemble(da_parts, da_ref, QREST)
    assemble(kv_parts, kv_ref, KREST)
    masks(q_parts, qm_ref, QREST, True)
    masks(kv_parts, km_ref, KREST, False)
    k_ext = jnp.concatenate([kv_ref[:, 0:DH], km_ref[...]], axis=1)
    lane = lax.broadcasted_iota(jnp.int32, (BLOCK, DH), 1)
    for block in range(NQ // BLOCK):
        rows = slice(block * BLOCK, (block + 1) * BLOCK)
        q_ext = jnp.concatenate([q_ref[rows], qm_ref[rows]], axis=1)
        s = lax.dot_general(q_ext, k_ext, LAST, preferred_element_type=F32)
        top = jnp.max(s, axis=1, keepdims=True)
        p = jnp.exp2((s - top) * UNIT)
        total = jnp.sum(p, axis=1, keepdims=True)
        o = jnp.dot(p.astype(BF16), kv_ref[:, DH:FEATS], preferred_element_type=F32) / total
        oall_ref[rows] = o.astype(BF16)
        lse = top * UNIT + jnp.log2(total)
        share = jnp.sum(o * da_ref[rows].astype(F32), axis=1, keepdims=True)
        stat = jnp.where(lane == 0, lse, jnp.where(lane == 1, share, 0.0))
        stat_ref[:, rows] = stat.T[0:8]
    for j in range(4):
        o_refs[j][...] = take_pair(oall_ref, j, QREST)


def backward_kernel(q_ref, qm_ref, da_ref, kv_ref, km_ref, s0_ref, s1_ref, s2_ref, s3_ref, *refs):
    dq_refs, keep_ref, send_ref, dkv_ref, ds_ref = refs[0:4], *refs[4:8]
    each = [s0_ref[...]]
    for t, ref in ((1, s1_ref), (2, s2_ref), (3, s3_ref)):
        tiles = [ref[:, 2 * FINE * ((j - t) % 4) : 2 * FINE * ((j - t) % 4 + 1)] for j in range(4)]
        tiles.append(pltpu.roll(ref[:, QREST:NQ], 2 * REST * t, 1))
        each.append(jnp.concatenate(tiles, axis=1))
    lses = [one[0:1] for one in each]
    top = jnp.maximum(jnp.maximum(lses[0], lses[1]), jnp.maximum(lses[2], lses[3]))
    weights = [jnp.exp2(one - top) for one in lses]
    total = weights[0] + weights[1] + weights[2] + weights[3]
    delta = sum(weights[t] * each[t][1:2] for t in range(4)) / total
    lse = top + jnp.log2(total)
    lse = jnp.where(lse < -1e28, 1e30, lse)
    q = q_ref[...]
    da = da_ref[...]
    q_ext = jnp.concatenate([q, qm_ref[...]], axis=1)
    for block in range(NK // BLOCK):
        rows = slice(block * BLOCK, (block + 1) * BLOCK)
        k_ext = jnp.concatenate([kv_ref[rows, 0:DH], km_ref[rows]], axis=1)
        s = lax.dot_general(k_ext, q_ext, LAST, preferred_element_type=F32)
        p = jnp.exp2(s * UNIT - lse)
        dp = lax.dot_general(kv_ref[rows, DH:FEATS], da, LAST, preferred_element_type=F32)
        ds = (p * (dp - delta)).astype(BF16)
        dkv_ref[rows, DH:FEATS] = jnp.dot(p.astype(BF16), da, preferred_element_type=F32).astype(BF16)
        dkv_ref[rows, 0:DH] = (jnp.dot(ds, q, preferred_element_type=F32) * SCALE).astype(BF16)
        ds_ref[rows] = ds
    for j in range(4):
        keep_ref[j] = take_pair(dkv_ref, j, KREST)
        send_ref[j] = take_pair(dkv_ref, 4 + j, KREST)
    dq = lax.dot_general(ds_ref[...], kv_ref[:, 0:DH], FIRST, preferred_element_type=F32)
    dq = (dq * SCALE).astype(BF16)
    for j in range(4):
        dq_refs[j][...] = take_pair(dq, j, QREST)


def merge_kernel(o0_ref, o1_ref, o2_ref, o3_ref, s0_ref, s1_ref, s2_ref, s3_ref, keep_ref, send_ref):
    o_refs = (o0_ref, o3_ref, o2_ref, o1_ref)
    fine, last = [], []
    for t, ref in enumerate((s0_ref, s1_ref, s2_ref, s3_ref)):
        j = -t % 4
        fine += [ref[0:1, FINE * (2 * j + k) : FINE * (2 * j + k + 1)] for k in range(2)]
        last.append(pltpu.roll(ref[0:1, QREST:NQ], (FINE - 2 * REST * j) % FINE, 1))
    fine = jnp.concatenate(fine, axis=0).T
    last = jnp.concatenate(last + last, axis=0).T
    for k, out_ref in ((0, keep_ref), (1, send_ref)):
        for rows, columns in (
            (slice(0, FINE), [fine[:, 2 * t + k : 2 * t + k + 1] for t in range(4)]),
            (slice(FINE, PAD), [last[k * REST : (k + 1) * REST, t : t + 1] for t in range(4)]),
        ):
            source = slice(k * PAD + rows.start, k * PAD + rows.stop)
            top = jnp.maximum(jnp.maximum(columns[0], columns[1]), jnp.maximum(columns[2], columns[3]))
            weights = [jnp.exp2(one - top) for one in columns]
            total = weights[0] + weights[1] + weights[2] + weights[3]
            acc = sum(weights[t] * o_refs[t][source].astype(F32) for t in range(4))
            out_ref[rows] = (acc * jnp.where(top < -1e28, 0.0, 1.0 / total)).astype(BF16)


def project_kernel(at_ref, mine_ref, other_ref, wo_ref, dy0_ref, dy1_ref, dy2_ref, dy3_ref, *refs):
    out_refs, keep_ref, send_ref, dwo_ref = refs[0:4], *refs[4:7]
    e, h, zr, x, c = (at_ref[i] for i in range(5))
    mine, other = mine_ref[...], other_ref[...]
    even = e == 0
    attn = jnp.concatenate([jnp.where(even, mine, other), jnp.where(even, other, mine)], axis=1)
    for s in range(NH):
        start = pl.multiple_of(lax.rem(h + s, NH) * WIDE, WIDE)
        part = jnp.dot(attn, wo_ref[:, pl.ds(start, WIDE)], preferred_element_type=F32)
        out_refs[s][...] = part[0:ROWS].astype(BF16)
    for s, ref in enumerate((dy0_ref, dy1_ref, dy2_ref, dy3_ref)):
        dwo_ref[s] = lax.dot_general(ref[...], attn[0:ROWS], FIRST, preferred_element_type=F32).astype(BF16)
    for xt in range(4):
        for et in range(2):
            for t in range(4):
                s = lax.rem(h - zr - t + 2 * NH, NH)
                x_to = lax.rem(x + xt, 4)
                e_to = lax.rem(e + et, 2)
                row = e_to * 256 + x_to * 64
                keep_ref[xt, et, t] = dwo_ref[s, pl.ds(pl.multiple_of(row + c * COLS, COLS), COLS)]
                send_ref[xt, et, t] = dwo_ref[s, pl.ds(pl.multiple_of(row + (1 - c) * COLS, COLS), COLS)]


def add_kernel(keep_ref, got_ref, mine_ref, *out_refs):
    total = keep_ref[...].astype(F32) + got_ref[...].astype(F32)
    mine_ref[...] = total[0]
    for j, ref in enumerate(out_refs):
        ref[...] = total[j + 1].astype(BF16)


def total_kernel(k0_ref, k1_ref, k2_ref, k3_ref, q0_ref, q1_ref, q2_ref, q3_ref, keep_ref, send_ref):
    dkv = k0_ref[...] + sum(ref[...].astype(F32) for ref in (k1_ref, k2_ref, k3_ref))
    dq = sum(ref[...].astype(F32) for ref in (q0_ref, q1_ref, q2_ref, q3_ref))
    both = jnp.concatenate([dq, dkv], axis=1).astype(BF16)
    keep_ref[...] = both[0:PAD]
    send_ref[...] = both[PAD:PAIR]


def place_kernel(e_ref, mine_ref, other_ref, dq_ref, dk_ref, dv_ref):
    even = e_ref[0] == 0
    mine, other = mine_ref[0:ROWS], other_ref[0:ROWS]
    first, second = jnp.where(even, mine, other), jnp.where(even, other, mine)
    for j, ref in enumerate((dq_ref, dk_ref, dv_ref)):
        ref[:, 0:DH] = first[:, j * DH : (j + 1) * DH]
        ref[:, DH:FEATS] = second[:, j * DH : (j + 1) * DH]


def shifted(value, axis, size, by):
    return lax.ppermute(value, axis, [(i, (i + by) % size) for i in range(size)])


def around(value, axis):
    return [value] + [shifted(value, axis, 4, s) for s in (1, 2, 3)]


def local(queries, key_rows, value_rows, scale_of, wo, dy):
    axes = ("e", "head", "zr", "x", "c")
    at = jnp.stack([lax.axis_index(name) for name in axes]).astype(jnp.int32)
    ids = jnp.pad(scale_of, (0, 8 * DH - ROWS), constant_values=-1).reshape(8, DH).astype(F32)

    keep, send = call(
        pack_kernel, "pack", [at, queries, key_rows, value_rows, ids], [shape((PAD, 3 * DH))] * 2, scalars=1
    )
    got = shifted(send, "e", 2, 1)
    dys = around(dy, "head")
    pair = jnp.concatenate([keep, got], axis=0)
    kvs = around(pair[:, DH : 3 * DH], "x")
    qs = around(pair[:, 0:DH], "zr")
    kvs = kvs + [shifted(one, "c", 2, 1) for one in kvs]
    keep, send = call(
        dattn_kernel, "dattn", [at, *dys, wo, ids], [shape((PAD, DH))] * 2, scalars=1
    )
    das = around(jnp.concatenate([keep, shifted(send, "e", 2, 1)], axis=0), "zr")

    *os, stat, q, qm, kv, km, da = call(
        forward_kernel,
        "forward",
        [*qs, *das, *kvs],
        [shape((PAIR, DH))] * 4
        + [
            shape((8, NQ), F32),
            shape((NQ, DH)),
            shape((NQ, DH)),
            shape((NK, FEATS)),
            shape((NK, DH)),
            shape((NQ, DH)),
        ],
        [pltpu.VMEM((NQ, DH), BF16)],
    )
    stats = around(stat, "zr")
    os = [os[0]] + [shifted(os[s], "zr", 4, -s) for s in (1, 2, 3)]

    *dqs, keep, send = call(
        backward_kernel,
        "backward",
        [q, qm, da, kv, km, *stats],
        [shape((PAIR, DH))] * 4 + [shape((4, PAIR, FEATS))] * 2,
        [pltpu.VMEM((NK, FEATS), BF16), pltpu.VMEM((NK, NQ), BF16)],
    )
    dkvs = call(
        add_kernel,
        "add",
        [keep, shifted(send, "c", 2, 1)],
        [shape((PAIR, FEATS), F32)] + [shape((PAIR, FEATS))] * 3,
    )
    dkvs = [dkvs[0]] + [shifted(dkvs[s], "x", 4, -s) for s in (1, 2, 3)]
    dqs = [dqs[0]] + [shifted(dqs[s], "zr", 4, -s) for s in (1, 2, 3)]

    keep, send = call(merge_kernel, "merge", [*os, *stats], [shape((PAD, DH))] * 2)
    *outs, keep, send = call(
        project_kernel,
        "project",
        [at, keep, shifted(send, "e", 2, 1), wo, *dys],
        [shape((ROWS, WIDE))] * 4 + [shape((4, 2, 4, COLS, FEATS))] * 2,
        [pltpu.VMEM((4, WIDE, FEATS), BF16)],
        scalars=1,
    )
    block_out = sum(
        [outs[0].astype(F32)] + [shifted(outs[s], "head", NH, s).astype(F32) for s in (1, 2, 3)]
    ).astype(BF16)
    dwo = keep.astype(F32) + shifted(send, "c", 2, 1).astype(F32)
    dwo = dwo[0] + sum(shifted(dwo[s].astype(BF16), "x", 4, s).astype(F32) for s in (1, 2, 3))
    dwo = dwo[0] + shifted(dwo[1].astype(BF16), "e", 2, 1).astype(F32)
    dwo = dwo[0] + sum(shifted(dwo[s].astype(BF16), "zr", 4, s).astype(F32) for s in (1, 2, 3))

    keep, send = call(total_kernel, "total", [*dkvs, *dqs], [shape((PAD, 3 * DH))] * 2)
    dq, dk, dv = call(
        place_kernel, "place", [at, keep, shifted(send, "e", 2, 1)], [shape((ROWS, FEATS))] * 3, scalars=1
    )
    return (block_out, dq, dk, dv, dwo.T)


def solution(mesh):
    fine = Mesh(mesh.devices.reshape(4, 2, 4, 2, NH), ("zr", "e", "x", "c", "head"))
    seq = ("zr", "e", "x", "c")
    placed = (
        P(seq, "head"),
        P(seq, "head"),
        P(seq, "head"),
        P(seq),
        P("head", None),
        P(seq, "head"),
    )
    return jax.shard_map(
        local,
        mesh=fine,
        in_specs=placed,
        out_specs=(
            P(seq, "head"),
            P(seq, "head"),
            P(seq, "head"),
            P(seq, "head"),
            P("head", seq),
        ),
        check_vma=False,
    )
```

```python
import functools
import math

import jax
import jax.numpy as jnp
from jax import lax
from jax.experimental import pallas as pl
from jax.experimental.pallas import tpu as pltpu
from jax.sharding import Mesh, PartitionSpec as P

DH = 128
ROWS = 136
PAD = 144
FINE = 128
REST = PAD - FINE
PAIR = 2 * PAD
NH = 4
QHALF = 8
NQ = QHALF * PAD
NK = 2 * NQ
QREST = QHALF * FINE
SUMS = 80
LOAD = PAIR + SUMS
FEATS = 2 * DH
MODEL = 2048
WIDE = MODEL // NH
COLS = 32
BLOCK = 384
BIG = -1e30
SCALE = DH ** (-0.5)
UNIT = SCALE * math.log2(math.e)
F32 = jnp.float32
BF16 = jnp.bfloat16
LAST = (((1,), (1,)), ((), ()))
FIRST = (((0,), (0,)), ((), ()))
PARAMS = pltpu.CompilerParams(vmem_limit_bytes=48 << 20)
VMEM = pl.BlockSpec(memory_space=pltpu.VMEM)
SMEM = pl.BlockSpec(memory_space=pltpu.SMEM)


def shape(dims, kind=BF16):
    return jax.ShapeDtypeStruct(dims, kind)


def call(kernel, name, ins, outs, scratch=(), scalars=0, far=0, flops=0):
    near = len(ins) - scalars - far
    cost = pl.CostEstimate(flops=flops, bytes_accessed=1 << 20, transcendentals=0) if flops else None
    return pl.pallas_call(
        kernel,
        in_specs=[SMEM] * scalars + [pl.BlockSpec(memory_space=pl.ANY)] * far + [VMEM] * near,
        out_shape=outs,
        scratch_shapes=list(scratch),
        compiler_params=PARAMS,
        cost_estimate=cost,
        name=name,
    )(*ins)


def by_parity(e, first, second, keep_ref, send_ref):
    @pl.when(e == 0)
    def _():
        keep_ref[...] = first
        send_ref[...] = second

    @pl.when(e == 1)
    def _():
        keep_ref[...] = second
        send_ref[...] = first


def pack_kernel(at_ref, q_hbm, k_hbm, v_hbm, ids_ref, keep_ref, send_ref, qkeep_ref, qsend_ref, here_ref, sems):
    copies = [
        pltpu.make_async_copy(ref, here_ref.at[i], sems.at[i]) for i, ref in enumerate((q_hbm, k_hbm, v_hbm))
    ]
    for copy in copies:
        copy.start()
    ids = ids_ref[...].astype(BF16)
    zero = jnp.zeros((8, DH), BF16)
    for copy in copies:
        copy.wait()
    kvs, qs = [], []
    for head in range(2):
        cols = slice(head * DH, (head + 1) * DH)
        k = jnp.concatenate([here_ref[1, :, cols], ids], axis=0)
        v = jnp.concatenate([here_ref[2, :, cols], zero], axis=0)
        kvs.append(jnp.concatenate([k, v], axis=1))
        qs.append(jnp.concatenate([here_ref[0, :, cols], ids], axis=0))
    by_parity(at_ref[0], kvs[0], kvs[1], keep_ref, send_ref)
    by_parity(at_ref[0], qs[0], qs[1], qkeep_ref, qsend_ref)


def dattn_kernel(at_ref, dy0_ref, dy1_ref, dy2_ref, dy3_ref, wo_ref, ids_ref, qkeep_ref, qsend_ref, keep_ref, send_ref):
    h = at_ref[1]
    acc = jnp.zeros((ROWS, FEATS), F32)
    for s, ref in enumerate((dy0_ref, dy1_ref, dy2_ref, dy3_ref)):
        start = pl.multiple_of(lax.rem(h - s + NH, NH) * WIDE, WIDE)
        acc = acc + lax.dot_general(ref[...], wo_ref[:, pl.ds(start, WIDE)], LAST, preferred_element_type=F32)
    ids = ids_ref[...].T
    real = jnp.concatenate([ids[:, 0:1], ids[0:8, 1:2]], axis=0) >= 0.0
    acc = jnp.where(real, acc, 0.0).astype(BF16)
    acc = jnp.concatenate([acc, jnp.zeros((PAD - ROWS, FEATS), BF16)], axis=0)
    keep_ref[:, 0:DH] = qkeep_ref[...]
    send_ref[:, 0:DH] = qsend_ref[...]
    by_parity(at_ref[0], acc[:, 0:DH], acc[:, DH:FEATS], keep_ref.at[:, DH:FEATS], send_ref.at[:, DH:FEATS])


def assemble(pair_refs, all_ref, base):
    rest = base + QREST
    for j, ref in enumerate(pair_refs):
        for k in range(2):
            half = 2 * j + k
            all_ref[base + half * FINE : base + (half + 1) * FINE] = ref[k * PAD : k * PAD + FINE]
            all_ref[rest + half * REST : rest + (half + 1) * REST] = ref[k * PAD + FINE : (k + 1) * PAD]


def take_pair(value, j):
    pieces = []
    for half in (2 * j, 2 * j + 1):
        pieces.append(value[half * FINE : (half + 1) * FINE])
        pieces.append(value[QREST + half * REST : QREST + (half + 1) * REST])
    return jnp.concatenate(pieces, axis=0)


def masks(pair_refs, mask_ref, base, is_query):
    fine, last = [], []
    for ref in pair_refs:
        for k in range(2):
            rows = ref[k * PAD + FINE : (k + 1) * PAD, 0:DH].astype(F32)
            fine.append(rows[8:9])
            last.append(rows[9:10])
    fine = jnp.concatenate(fine, axis=0).T
    last = jnp.concatenate(last, axis=0).T
    rest = base + QREST

    def encode(column):
        lane = lax.broadcasted_iota(jnp.int32, (column.shape[0], DH), 1).astype(F32)
        if is_query:
            hidden = ((lane > column) & (lane < 13.0)) | (lane == 13.0)
            return jnp.where(hidden, BIG, 0.0).astype(BF16)
        return jnp.where(lane == jnp.where(column < 0.0, 13.0, column), 1.0, 0.0).astype(BF16)

    for half in range(2 * len(pair_refs)):
        mask_ref[base + half * FINE : base + (half + 1) * FINE] = encode(fine[:, half : half + 1])
        mask_ref[rest + half * REST : rest + (half + 1) * REST] = encode(last[0:REST, half : half + 1])


def in_three(row):
    high = row.astype(BF16).astype(F32)
    middle = (row - high).astype(BF16).astype(F32)
    return [high, middle, row - high - middle]


def forward_kernel(*refs):
    q_parts, kv_parts = refs[0:4], refs[4:12]
    load_refs, q_ref, qm_ref, kv_ref, km_ref, o_ref, stat_ref = refs[12:16], *refs[16:22]
    assemble(q_parts, q_ref, 0)
    masks(q_parts, qm_ref, 0, True)
    for base, parts in ((0, kv_parts[0:4]), (NQ, kv_parts[4:8])):
        assemble(parts, kv_ref, base)
        masks(parts, km_ref, base, False)
    k_ext = jnp.concatenate([kv_ref[:, 0:DH], km_ref[...]], axis=1)
    lane = lax.broadcasted_iota(jnp.int32, (BLOCK, DH), 1)
    for block in range(NQ // BLOCK):
        rows = slice(block * BLOCK, (block + 1) * BLOCK)
        q_ext = jnp.concatenate([q_ref[rows, 0:DH], qm_ref[rows]], axis=1)
        s = lax.dot_general(q_ext, k_ext, LAST, preferred_element_type=F32)
        top = jnp.max(s, axis=1, keepdims=True)
        p = jnp.exp2((s - top) * UNIT)
        total = jnp.sum(p, axis=1, keepdims=True)
        o = jnp.dot(p.astype(BF16), kv_ref[:, DH:FEATS], preferred_element_type=F32) / total
        o_ref[rows] = o.astype(BF16)
        lse = top * UNIT + jnp.log2(total)
        share = jnp.sum(o * q_ref[rows, DH:FEATS].astype(F32), axis=1, keepdims=True)
        stat = jnp.where(lane == 0, lse, jnp.where(lane == 1, share, 0.0))
        stat_ref[:, rows] = stat.T[0:8]
    none = jnp.zeros((2, NQ), F32)
    sums = jnp.concatenate(in_three(stat_ref[0:1]) + in_three(stat_ref[1:2]) + [none], axis=0)
    tiles = [sums[:, i * DH : (i + 1) * DH] for i in range(NQ // DH)] + [jnp.zeros((8, DH), F32)]
    sums = jnp.concatenate(tiles, axis=0).astype(BF16)
    for j in range(4):
        load_refs[j][0:PAIR] = take_pair(o_ref, j)
        load_refs[j][PAIR:LOAD] = sums


def row_sums(load_refs):
    lses, shares = [], []
    for s, ref in enumerate(load_refs):
        sums = ref[PAIR:LOAD].astype(F32)
        tiles = [sums[8 * i : 8 * i + 8] for i in range(9)]
        last = tiles[8] if s == 0 else pltpu.roll(tiles[8], FINE - 2 * REST * s, 1)
        order = [tiles[2 * ((j + s) % 4) + k] for j in range(4) for k in range(2)] + [last]
        rows = jnp.concatenate(order, axis=1)
        lses.append(rows[0:1] + rows[1:2] + rows[2:3])
        shares.append(rows[3:4] + rows[4:5] + rows[5:6])
    top = jnp.maximum(jnp.maximum(lses[0], lses[1]), jnp.maximum(lses[2], lses[3]))
    weights = [jnp.exp2(one - top) for one in lses]
    total = weights[0] + weights[1] + weights[2] + weights[3]
    delta = sum(weights[s] * shares[s] for s in range(4)) / total
    lse = top + jnp.log2(total)
    return jnp.where(lse < -1e28, 1e30, lse), delta


def backward_kernel(base, q_ref, qm_ref, kv_ref, km_ref, *refs):
    load_refs, refs = refs[0:4], refs[4:]
    if base == 0:
        dq_in_ref, refs = refs[0], refs[1:]
    dkv_out_ref, dq_refs, dkv_ref, ds_ref = refs[0], refs[1:-2], refs[-2], refs[-1]
    lse, delta = row_sums(load_refs)
    q = q_ref[:, 0:DH]
    da = q_ref[:, DH:FEATS]
    q_ext = jnp.concatenate([q, qm_ref[...]], axis=1)
    for block in range(NQ // BLOCK):
        rows = slice(block * BLOCK, (block + 1) * BLOCK)
        keys = slice(base + block * BLOCK, base + (block + 1) * BLOCK)
        k_ext = jnp.concatenate([kv_ref[keys, 0:DH], km_ref[keys]], axis=1)
        s = lax.dot_general(k_ext, q_ext, LAST, preferred_element_type=F32)
        p = jnp.exp2(s * UNIT - lse)
        dp = lax.dot_general(kv_ref[keys, DH:FEATS], da, LAST, preferred_element_type=F32)
        ds = (p * (dp - delta)).astype(BF16)
        dkv_ref[rows, DH:FEATS] = jnp.dot(p.astype(BF16), da, preferred_element_type=F32).astype(BF16)
        dkv_ref[rows, 0:DH] = (jnp.dot(ds, q, preferred_element_type=F32) * SCALE).astype(BF16)
        ds_ref[rows] = ds
    for j in range(4):
        dkv_out_ref[j] = take_pair(dkv_ref, j)
    keys = slice(base, base + NQ)
    dq = lax.dot_general(ds_ref[...], kv_ref[keys, 0:DH], FIRST, preferred_element_type=F32)
    if base > 0:
        dq_refs[0][...] = dq
    else:
        dq = ((dq + dq_in_ref[...]) * SCALE).astype(BF16)
        for j in range(4):
            dq_refs[j][...] = take_pair(dq, j)


def merge_kernel(l0_ref, l1_ref, l2_ref, l3_ref, keep_ref, send_ref):
    load_refs = (l0_ref, l1_ref, l2_ref, l3_ref)
    fine, last = [], []
    for s, ref in enumerate(load_refs):
        sums = ref[PAIR:LOAD].astype(F32)
        rows = sums[0:72]
        lse = [rows[8 * i : 8 * i + 1] + rows[8 * i + 1 : 8 * i + 2] + rows[8 * i + 2 : 8 * i + 3] for i in (2 * s, 2 * s + 1, 8)]
        fine += lse[0:2]
        last.append(lse[2] if s == 0 else pltpu.roll(lse[2], FINE - 2 * REST * s, 1))
    fine = jnp.concatenate(fine, axis=0).T
    last = jnp.concatenate(last + last, axis=0).T
    for k, out_ref in ((0, keep_ref), (1, send_ref)):
        for rows, columns in (
            (slice(0, FINE), [fine[:, 2 * s + k : 2 * s + k + 1] for s in range(4)]),
            (slice(FINE, PAD), [last[k * REST : (k + 1) * REST, s : s + 1] for s in range(4)]),
        ):
            source = slice(k * PAD + rows.start, k * PAD + rows.stop)
            top = jnp.maximum(jnp.maximum(columns[0], columns[1]), jnp.maximum(columns[2], columns[3]))
            weights = [jnp.exp2(one - top) for one in columns]
            total = weights[0] + weights[1] + weights[2] + weights[3]
            acc = sum(weights[s] * load_refs[s][source].astype(F32) for s in range(4))
            out_ref[rows] = (acc * jnp.where(top < -1e28, 0.0, 1.0 / total)).astype(BF16)


def project_kernel(at_ref, mine_ref, other_ref, wo_ref, dy0_ref, dy1_ref, dy2_ref, dy3_ref, *refs):
    out_refs, keep_ref, send_ref, dwo_ref = refs[0:4], *refs[4:7]
    e, h, zr, x, c = (at_ref[i] for i in range(5))
    mine, other = mine_ref[...], other_ref[...]
    even = e == 0
    attn = jnp.concatenate([jnp.where(even, mine, other), jnp.where(even, other, mine)], axis=1)
    for s in range(NH):
        start = pl.multiple_of(lax.rem(h + s, NH) * WIDE, WIDE)
        part = jnp.dot(attn, wo_ref[:, pl.ds(start, WIDE)], preferred_element_type=F32)
        out_refs[s][...] = part[0:ROWS].astype(BF16)
    for s, ref in enumerate((dy0_ref, dy1_ref, dy2_ref, dy3_ref)):
        dwo_ref[s] = lax.dot_general(ref[...], attn[0:ROWS], FIRST, preferred_element_type=F32).astype(BF16)
    for xt in range(4):
        for et in range(2):
            for t in range(4):
                s = lax.rem(h - jnp.bitwise_xor(zr, t) + NH, NH)
                row = lax.rem(e + et, 2) * 256 + lax.rem(x + xt, 4) * 64
                to = slice((et * 4 + t) * COLS, (et * 4 + t + 1) * COLS)
                keep_ref[xt, to] = dwo_ref[s, pl.ds(pl.multiple_of(row + c * COLS, COLS), COLS)]
                send_ref[xt, to] = dwo_ref[s, pl.ds(pl.multiple_of(row + (1 - c) * COLS, COLS), COLS)]


def core_kernel(keep_ref, got_ref, wkeep_ref, wgot_ref, dq1_ref, dq2_ref, dq3_ref, *refs):
    mine_ref, z_refs, wmine_ref, x_refs = refs[0], refs[1:4], refs[4], refs[5:8]
    total = keep_ref[...].astype(F32) + got_ref[...].astype(F32)
    mine_ref[...] = total[0]
    weights = wkeep_ref[...].astype(F32) + wgot_ref[...].astype(F32)
    wmine_ref[...] = weights[0]
    for s, dq_ref in ((1, dq1_ref), (2, dq2_ref), (3, dq3_ref)):
        z_refs[s - 1][...] = total[s].astype(BF16)
        piece = weights[4 - s].astype(BF16)
        x_refs[s - 1][0:PAIR] = dq_ref[...]
        x_refs[s - 1][PAIR : PAIR + 256] = piece[:, 0:DH]
        x_refs[s - 1][PAIR + 256 : PAIR + 512] = piece[:, DH:FEATS]


def ring_kernel(dq0_ref, wmine_ref, x1_ref, x2_ref, x3_ref, dq_ref, keep_ref, send_ref):
    got = [ref[...].astype(F32) for ref in (x1_ref, x2_ref, x3_ref)]
    got = got[0] + got[1] + got[2]
    dq_ref[...] = dq0_ref[...].astype(F32) + got[0:PAIR]
    total = wmine_ref[...] + jnp.concatenate([got[PAIR : PAIR + 256], got[PAIR + 256 : PAIR + 512]], axis=1)
    for et in range(2):
        at = et * 4 * COLS
        to = et * 2 * COLS
        keep_ref[to : to + 2 * COLS] = total[at : at + 2 * COLS]
        send_ref[to : to + COLS] = total[at + 3 * COLS : at + 4 * COLS].astype(BF16)
        send_ref[to + COLS : to + 2 * COLS] = total[at + 2 * COLS : at + 3 * COLS].astype(BF16)


def half_kernel(keep_ref, got_ref, out_ref, send_ref):
    total = keep_ref[...] + got_ref[...].astype(F32)
    for et in range(2):
        out_ref[et * COLS : (et + 1) * COLS] = total[et * 2 * COLS : (et * 2 + 1) * COLS]
        send_ref[et * COLS : (et + 1) * COLS] = total[(et * 2 + 1) * COLS : (et * 2 + 2) * COLS].astype(BF16)


def total_kernel(k0_ref, k1_ref, k2_ref, k3_ref, dq_ref, wkeep_ref, wgot_ref, keep_ref, wmine_ref, send_ref):
    dkv = k0_ref[...] + sum(ref[...].astype(F32) for ref in (k1_ref, k2_ref, k3_ref))
    both = jnp.concatenate([dq_ref[...], dkv], axis=1).astype(BF16)
    keep_ref[...] = both[0:PAD]
    for i in range(3):
        send_ref[i * PAD : (i + 1) * PAD] = both[PAD:PAIR, i * DH : (i + 1) * DH]
    weights = wkeep_ref[...] + wgot_ref[...].astype(F32)
    wmine_ref[...] = weights[0:COLS]
    piece = weights[COLS : 2 * COLS].astype(BF16)
    send_ref[3 * PAD : 3 * PAD + COLS] = piece[:, 0:DH]
    send_ref[3 * PAD + COLS : 3 * PAD + 2 * COLS] = piece[:, DH:FEATS]


def place_kernel(at_ref, mine_ref, wmine_ref, got_ref, dq_ref, dk_ref, dv_ref, dwo_ref):
    even = at_ref[0] == 0
    for i, ref in enumerate((dq_ref, dk_ref, dv_ref)):
        mine = mine_ref[0:ROWS, i * DH : (i + 1) * DH]
        other = got_ref[i * PAD : i * PAD + ROWS]
        ref[:, 0:DH] = jnp.where(even, mine, other)
        ref[:, DH:FEATS] = jnp.where(even, other, mine)
    got = got_ref[3 * PAD : 3 * PAD + 2 * COLS].astype(F32)
    dwo_ref[...] = (wmine_ref[...] + jnp.concatenate([got[0:COLS], got[COLS : 2 * COLS]], axis=1)).T


def shifted(value, axis, size, by):
    return lax.ppermute(value, axis, [(i, (i + by) % size) for i in range(size)])


def swapped(value, axis, size, mask):
    return lax.ppermute(value, axis, [(i, i ^ mask) for i in range(size)])


def around(value, axis):
    return [value] + [shifted(value, axis, 4, s) for s in (1, 2, 3)]


def local(queries, key_rows, value_rows, scale_of, wo, dy):
    axes = ("e", "head", "zr", "x", "c")
    at = jnp.stack([lax.axis_index(name) for name in axes]).astype(jnp.int32)
    ids = jnp.pad(scale_of, (0, 8 * DH - ROWS), constant_values=-1).reshape(8, DH).astype(F32)
    pair = (PAIR, FEATS)

    keep, send, qkeep, qsend = call(
        pack_kernel,
        "pack",
        [at, queries, key_rows, value_rows, ids],
        [shape((PAD, FEATS))] * 2 + [shape((PAD, DH))] * 2,
        [pltpu.VMEM((3, ROWS, FEATS), BF16), pltpu.SemaphoreType.DMA((3,))],
        scalars=1,
        far=3,
    )
    kvs = around(jnp.concatenate([keep, swapped(send, "e", 2, 1)], axis=0), "zr")
    dys = around(dy, "head")
    keep, send = call(
        dattn_kernel, "dattn", [at, *dys, wo, ids, qkeep, qsend], [shape((PAD, FEATS))] * 2, scalars=1
    )
    qs = around(jnp.concatenate([keep, swapped(send, "e", 2, 1)], axis=0), "x")
    kvs = kvs + [swapped(one, "c", 2, 1) for one in kvs]

    *loads, q, qm, kv, km = call(
        forward_kernel,
        "forward",
        [*qs, *kvs],
        [shape((LOAD, DH))] * 4 + [shape((NQ, FEATS)), shape((NQ, DH)), shape((NK, FEATS)), shape((NK, DH))],
        [pltpu.VMEM((NQ, DH), BF16), pltpu.VMEM((8, NQ), F32)],
        flops=6 * NQ * NK * DH,
    )
    loads = [loads[0]] + [shifted(loads[s], "x", 4, -s) for s in (1, 2, 3)]

    keep, send = call(merge_kernel, "merge", loads, [shape((PAD, DH))] * 2)
    other = swapped(send, "e", 2, 1)
    scratch = [pltpu.VMEM((NQ, FEATS), BF16), pltpu.VMEM((NQ, NQ), BF16)]
    dkv_send, dq_part = call(
        functools.partial(backward_kernel, NQ),
        "backward_far",
        [q, qm, kv, km, *loads],
        [shape((4, *pair)), shape((NQ, DH), F32)],
        scratch,
        flops=6 * NQ * NK * DH,
    )
    other, dq_part = lax.optimization_barrier((other, dq_part))
    *outs, wkeep, wsend = call(
        project_kernel,
        "project",
        [at, keep, other, wo, *dys],
        [shape((ROWS, WIDE))] * 4 + [shape((4, 256, FEATS))] * 2,
        [pltpu.VMEM((4, WIDE, FEATS), BF16)],
        scalars=1,
    )
    wsend, dq_part = lax.optimization_barrier((wsend, dq_part))
    dkv_keep, *dqs = call(
        functools.partial(backward_kernel, 0),
        "backward_near",
        [q, qm, kv, km, *loads, dq_part],
        [shape((4, *pair))] + [shape((PAIR, DH))] * 4,
        scratch,
        flops=6 * NQ * NK * DH,
    )
    mine, *far = call(
        core_kernel,
        "core",
        [dkv_keep, swapped(dkv_send, "c", 2, 1), wkeep, swapped(wsend, "c", 2, 1), *dqs[1:]],
        [shape(pair, F32)] + [shape(pair)] * 3 + [shape((256, FEATS), F32)] + [shape((PAIR + 512, DH))] * 3,
    )
    dkvs = [mine] + [shifted(far[s - 1], "zr", 4, -s) for s in (1, 2, 3)]
    xs = [shifted(far[3 + s], "x", 4, -s) for s in (1, 2, 3)]
    dq, wkeep, wsend = call(
        ring_kernel,
        "ring",
        [dqs[0], far[3], *xs],
        [shape((PAIR, DH), F32), shape((128, FEATS), F32), shape((128, FEATS))],
    )
    wkeep, wsend = call(
        half_kernel,
        "half",
        [wkeep, swapped(wsend, "zr", 4, 3)],
        [shape((64, FEATS), F32), shape((64, FEATS))],
    )
    block_out = sum(
        [outs[0].astype(F32)] + [shifted(outs[s], "head", NH, s).astype(F32) for s in (1, 2, 3)]
    ).astype(BF16)
    keep, wkeep, send = call(
        total_kernel,
        "total",
        [*dkvs, dq, wkeep, swapped(wsend, "zr", 4, 1)],
        [shape((PAD, 3 * DH)), shape((COLS, FEATS), F32), shape((3 * PAD + 2 * COLS, DH))],
    )
    dq, dk, dv, dwo = call(
        place_kernel,
        "place",
        [at, keep, wkeep, swapped(send, "e", 2, 1)],
        [shape((ROWS, FEATS))] * 3 + [shape((FEATS, COLS), F32)],
        scalars=1,
    )
    return (block_out, dq, dk, dv, dwo)


def solution(mesh):
    fine = Mesh(mesh.devices.reshape(4, 2, 4, 2, NH), ("zr", "e", "x", "c", "head"))
    seq = ("zr", "e", "x", "c")
    placed = (
        P(seq, "head"),
        P(seq, "head"),
        P(seq, "head"),
        P(seq),
        P("head", None),
        P(seq, "head"),
    )
    return jax.shard_map(
        local,
        mesh=fine,
        in_specs=placed,
        out_specs=(
            P(seq, "head"),
            P(seq, "head"),
            P(seq, "head"),
            P(seq, "head"),
            P("head", seq),
        ),
        check_vma=False,
    )
```

```python
import functools
import math

import jax
import jax.numpy as jnp
from jax import lax
from jax.experimental import pallas as pl
from jax.experimental.pallas import tpu as pltpu
from jax.sharding import Mesh, PartitionSpec as P

DH = 128
ROWS = 136
PAD = 144
FINE = 128
REST = PAD - FINE
PAIR = 2 * PAD
NH = 4
QHALF = 8
NQ = QHALF * PAD
NK = 2 * NQ
QREST = QHALF * FINE
SUMS = 80
LOAD = PAIR + SUMS
FEATS = 2 * DH
MODEL = 2048
WIDE = MODEL // NH
COLS = 32
BLOCK = 384
BIG = -1e30
SCALE = DH ** (-0.5)
UNIT = SCALE * math.log2(math.e)
F32 = jnp.float32
BF16 = jnp.bfloat16
LAST = (((1,), (1,)), ((), ()))
FIRST = (((0,), (0,)), ((), ()))
PARAMS = pltpu.CompilerParams(vmem_limit_bytes=48 << 20)
VMEM = pl.BlockSpec(memory_space=pltpu.VMEM)
SMEM = pl.BlockSpec(memory_space=pltpu.SMEM)


def shape(dims, kind=BF16):
    return jax.ShapeDtypeStruct(dims, kind)


def call(kernel, name, ins, outs, scratch=(), scalars=0, flops=0):
    cost = pl.CostEstimate(flops=flops, bytes_accessed=1 << 20, transcendentals=0) if flops else None
    return pl.pallas_call(
        kernel,
        in_specs=[SMEM] * scalars + [VMEM] * (len(ins) - scalars),
        out_shape=outs,
        scratch_shapes=list(scratch),
        compiler_params=PARAMS,
        cost_estimate=cost,
        name=name,
    )(*ins)


def by_parity(e, first, second, keep_ref, send_ref):
    @pl.when(e == 0)
    def _():
        keep_ref[...] = first
        send_ref[...] = second

    @pl.when(e == 1)
    def _():
        keep_ref[...] = second
        send_ref[...] = first


def pack_kernel(at_ref, qkv_ref, ids_ref, keep_ref, send_ref, qkeep_ref, qsend_ref):
    ids = ids_ref[...].astype(BF16)
    zero = jnp.zeros((8, DH), BF16)
    kvs, qs = [], []
    for head in range(2):
        cols = slice(head * DH, (head + 1) * DH)
        k = jnp.concatenate([qkv_ref[1, :, cols], ids], axis=0)
        v = jnp.concatenate([qkv_ref[2, :, cols], zero], axis=0)
        kvs.append(jnp.concatenate([k, v], axis=1))
        qs.append(jnp.concatenate([qkv_ref[0, :, cols], ids], axis=0))
    by_parity(at_ref[0], kvs[0], kvs[1], keep_ref, send_ref)
    by_parity(at_ref[0], qs[0], qs[1], qkeep_ref, qsend_ref)


def dattn_kernel(at_ref, dy0_ref, dy1_ref, dy2_ref, dy3_ref, wo_ref, qkeep_ref, qsend_ref, keep_ref, send_ref):
    acc = jnp.zeros((ROWS, FEATS), F32)
    for s, ref in enumerate((dy0_ref, dy1_ref, dy2_ref, dy3_ref)):
        block = wo_ref[:, s * WIDE : (s + 1) * WIDE]
        acc = acc + lax.dot_general(ref[...], block, LAST, preferred_element_type=F32)
    acc = jnp.concatenate([acc.astype(BF16), jnp.zeros((PAD - ROWS, FEATS), BF16)], axis=0)
    keep_ref[:, 0:DH] = qkeep_ref[...]
    send_ref[:, 0:DH] = qsend_ref[...]
    by_parity(at_ref[0], acc[:, 0:DH], acc[:, DH:FEATS], keep_ref.at[:, DH:FEATS], send_ref.at[:, DH:FEATS])


def assemble(pair_refs, all_ref, base):
    rest = base + QREST
    for j, ref in enumerate(pair_refs):
        for k in range(2):
            half = 2 * j + k
            all_ref[base + half * FINE : base + (half + 1) * FINE] = ref[k * PAD : k * PAD + FINE]
            all_ref[rest + half * REST : rest + (half + 1) * REST] = ref[k * PAD + FINE : (k + 1) * PAD]


def take_pair(value, j):
    pieces = []
    for half in (2 * j, 2 * j + 1):
        pieces.append(value[half * FINE : (half + 1) * FINE])
        pieces.append(value[QREST + half * REST : QREST + (half + 1) * REST])
    return jnp.concatenate(pieces, axis=0)


def masks(pair_refs, mask_ref, base, is_query):
    fine, last = [], []
    for ref in pair_refs:
        for k in range(2):
            rows = ref[k * PAD + FINE : (k + 1) * PAD, 0:DH].astype(F32)
            fine.append(rows[8:9])
            last.append(rows[9:10])
    fine = jnp.concatenate(fine, axis=0).T
    last = jnp.concatenate(last, axis=0).T
    rest = base + QREST

    def encode(column):
        lane = lax.broadcasted_iota(jnp.int32, (column.shape[0], DH), 1).astype(F32)
        if is_query:
            hidden = ((lane > column) & (lane < 13.0)) | (lane == 13.0)
            return jnp.where(hidden, BIG, 0.0).astype(BF16)
        return jnp.where(lane == jnp.where(column < 0.0, 13.0, column), 1.0, 0.0).astype(BF16)

    for half in range(2 * len(pair_refs)):
        mask_ref[base + half * FINE : base + (half + 1) * FINE] = encode(fine[:, half : half + 1])
        mask_ref[rest + half * REST : rest + (half + 1) * REST] = encode(last[0:REST, half : half + 1])


def in_three(row):
    high = row.astype(BF16).astype(F32)
    middle = (row - high).astype(BF16).astype(F32)
    return [high, middle, row - high - middle]


def forward_kernel(*refs):
    q_parts, kv_parts = refs[0:4], refs[4:12]
    load_refs, q_ref, qm_ref, kv_ref, km_ref, o_ref, stat_ref = refs[12:16], *refs[16:22]
    assemble(q_parts, q_ref, 0)
    masks(q_parts, qm_ref, 0, True)
    for base, parts in ((0, kv_parts[0:4]), (NQ, kv_parts[4:8])):
        assemble(parts, kv_ref, base)
        masks(parts, km_ref, base, False)
    k_ext = jnp.concatenate([kv_ref[:, 0:DH], km_ref[...]], axis=1)
    lane = lax.broadcasted_iota(jnp.int32, (BLOCK, DH), 1)
    for block in range(NQ // BLOCK):
        rows = slice(block * BLOCK, (block + 1) * BLOCK)
        q_ext = jnp.concatenate([q_ref[rows, 0:DH], qm_ref[rows]], axis=1)
        s = lax.dot_general(q_ext, k_ext, LAST, preferred_element_type=F32)
        top = jnp.max(s, axis=1, keepdims=True)
        p = jnp.exp2((s - top) * UNIT)
        total = jnp.sum(p, axis=1, keepdims=True)
        o = jnp.dot(p.astype(BF16), kv_ref[:, DH:FEATS], preferred_element_type=F32) / total
        o_ref[rows] = o.astype(BF16)
        lse = top * UNIT + jnp.log2(total)
        share = jnp.sum(o * q_ref[rows, DH:FEATS].astype(F32), axis=1, keepdims=True)
        stat = jnp.where(lane == 0, lse, jnp.where(lane == 1, share, 0.0))
        stat_ref[:, rows] = stat.T[0:8]
    none = jnp.zeros((2, NQ), F32)
    sums = jnp.concatenate(in_three(stat_ref[0:1]) + in_three(stat_ref[1:2]) + [none], axis=0)
    tiles = [sums[:, i * DH : (i + 1) * DH] for i in range(NQ // DH)] + [jnp.zeros((8, DH), F32)]
    sums = jnp.concatenate(tiles, axis=0).astype(BF16)
    for j in range(4):
        load_refs[j][0:PAIR] = take_pair(o_ref, j)
        load_refs[j][PAIR:LOAD] = sums


def row_sums(load_refs):
    lses, shares = [], []
    for s, ref in enumerate(load_refs):
        sums = ref[PAIR:LOAD].astype(F32)
        tiles = [sums[8 * i : 8 * i + 8] for i in range(9)]
        last = tiles[8] if s == 0 else pltpu.roll(tiles[8], FINE - 2 * REST * s, 1)
        order = [tiles[2 * ((j + s) % 4) + k] for j in range(4) for k in range(2)] + [last]
        rows = jnp.concatenate(order, axis=1)
        lses.append(rows[0:1] + rows[1:2] + rows[2:3])
        shares.append(rows[3:4] + rows[4:5] + rows[5:6])
    top = jnp.maximum(jnp.maximum(lses[0], lses[1]), jnp.maximum(lses[2], lses[3]))
    weights = [jnp.exp2(one - top) for one in lses]
    total = weights[0] + weights[1] + weights[2] + weights[3]
    delta = sum(weights[s] * shares[s] for s in range(4)) / total
    lse = top + jnp.log2(total)
    return jnp.where(lse < -1e28, 1e30, lse), delta


def backward_kernel(base, q_ref, qm_ref, kv_ref, km_ref, *refs):
    load_refs, refs = refs[0:4], refs[4:]
    if base == 0:
        dq_in_ref, refs = refs[0], refs[1:]
    dkv_out_ref, dq_refs, dkv_ref, ds_ref = refs[0], refs[1:-2], refs[-2], refs[-1]
    lse, delta = row_sums(load_refs)
    q = q_ref[:, 0:DH]
    da = q_ref[:, DH:FEATS]
    q_ext = jnp.concatenate([q, qm_ref[...]], axis=1)
    for block in range(NQ // BLOCK):
        rows = slice(block * BLOCK, (block + 1) * BLOCK)
        keys = slice(base + block * BLOCK, base + (block + 1) * BLOCK)
        k_ext = jnp.concatenate([kv_ref[keys, 0:DH], km_ref[keys]], axis=1)
        s = lax.dot_general(k_ext, q_ext, LAST, preferred_element_type=F32)
        p = jnp.exp2(s * UNIT - lse)
        dp = lax.dot_general(kv_ref[keys, DH:FEATS], da, LAST, preferred_element_type=F32)
        ds = (p * (dp - delta)).astype(BF16)
        dkv_ref[rows, DH:FEATS] = jnp.dot(p.astype(BF16), da, preferred_element_type=F32).astype(BF16)
        dkv_ref[rows, 0:DH] = (jnp.dot(ds, q, preferred_element_type=F32) * SCALE).astype(BF16)
        ds_ref[rows] = ds
    for j in range(4):
        dkv_out_ref[j] = take_pair(dkv_ref, j)
    keys = slice(base, base + NQ)
    dq = lax.dot_general(ds_ref[...], kv_ref[keys, 0:DH], FIRST, preferred_element_type=F32)
    if base > 0:
        dq_refs[0][...] = dq
    else:
        dq = ((dq + dq_in_ref[...]) * SCALE).astype(BF16)
        for j in range(4):
            dq_refs[j][...] = take_pair(dq, j)


def merge_kernel(l0_ref, l1_ref, l2_ref, l3_ref, keep_ref, send_ref):
    load_refs = (l0_ref, l1_ref, l2_ref, l3_ref)
    fine, last = [], []
    for s, ref in enumerate(load_refs):
        sums = ref[PAIR:LOAD].astype(F32)
        rows = sums[0:72]
        lse = [rows[8 * i : 8 * i + 1] + rows[8 * i + 1 : 8 * i + 2] + rows[8 * i + 2 : 8 * i + 3] for i in (2 * s, 2 * s + 1, 8)]
        fine += lse[0:2]
        last.append(lse[2] if s == 0 else pltpu.roll(lse[2], FINE - 2 * REST * s, 1))
    fine = jnp.concatenate(fine, axis=0).T
    last = jnp.concatenate(last + last, axis=0).T
    for k, out_ref in ((0, keep_ref), (1, send_ref)):
        for rows, columns in (
            (slice(0, FINE), [fine[:, 2 * s + k : 2 * s + k + 1] for s in range(4)]),
            (slice(FINE, PAD), [last[k * REST : (k + 1) * REST, s : s + 1] for s in range(4)]),
        ):
            source = slice(k * PAD + rows.start, k * PAD + rows.stop)
            top = jnp.maximum(jnp.maximum(columns[0], columns[1]), jnp.maximum(columns[2], columns[3]))
            weights = [jnp.exp2(one - top) for one in columns]
            total = weights[0] + weights[1] + weights[2] + weights[3]
            acc = sum(weights[s] * load_refs[s][source].astype(F32) for s in range(4))
            out_ref[rows] = (acc * jnp.where(top < -1e28, 0.0, 1.0 / total)).astype(BF16)


def project_kernel(at_ref, mine_ref, other_ref, wo_ref, dy0_ref, dy1_ref, dy2_ref, dy3_ref, *refs):
    out_refs, keep_ref, send_ref, dwo_ref = refs[0:4], *refs[4:7]
    e, h, zr, x, c = (at_ref[i] for i in range(5))
    mine, other = mine_ref[...], other_ref[...]
    even = e == 0
    attn = jnp.concatenate([jnp.where(even, mine, other), jnp.where(even, other, mine)], axis=1)
    for s in range(NH):
        at = -s % NH * WIDE
        part = jnp.dot(attn, wo_ref[:, at : at + WIDE], preferred_element_type=F32)
        out_refs[s][...] = part[0:ROWS].astype(BF16)
    for s, ref in enumerate((dy0_ref, dy1_ref, dy2_ref, dy3_ref)):
        dwo_ref[s] = lax.dot_general(ref[...], attn[0:ROWS], FIRST, preferred_element_type=F32).astype(BF16)
    for xt in range(4):
        for et in range(2):
            for t in range(4):
                s = lax.rem(h - jnp.bitwise_xor(zr, t) + NH, NH)
                row = lax.rem(e + et, 2) * 256 + lax.rem(x + xt, 4) * 64
                to = slice((et * 4 + t) * COLS, (et * 4 + t + 1) * COLS)
                keep_ref[xt, to] = dwo_ref[s, pl.ds(pl.multiple_of(row + c * COLS, COLS), COLS)]
                send_ref[xt, to] = dwo_ref[s, pl.ds(pl.multiple_of(row + (1 - c) * COLS, COLS), COLS)]


def core_kernel(keep_ref, got_ref, wkeep_ref, wgot_ref, dq1_ref, dq2_ref, dq3_ref, *refs):
    mine_ref, z_refs, wmine_ref, x_refs = refs[0], refs[1:4], refs[4], refs[5:8]
    total = keep_ref[...].astype(F32) + got_ref[...].astype(F32)
    mine_ref[...] = total[0]
    weights = wkeep_ref[...].astype(F32) + wgot_ref[...].astype(F32)
    wmine_ref[...] = weights[0]
    for s, dq_ref in ((1, dq1_ref), (2, dq2_ref), (3, dq3_ref)):
        z_refs[s - 1][...] = total[s].astype(BF16)
        piece = weights[4 - s].astype(BF16)
        x_refs[s - 1][0:PAIR] = dq_ref[...]
        x_refs[s - 1][PAIR : PAIR + 256] = piece[:, 0:DH]
        x_refs[s - 1][PAIR + 256 : PAIR + 512] = piece[:, DH:FEATS]


def ring_kernel(dq0_ref, wmine_ref, x1_ref, x2_ref, x3_ref, dq_ref, keep_ref, send_ref):
    got = [ref[...].astype(F32) for ref in (x1_ref, x2_ref, x3_ref)]
    got = got[0] + got[1] + got[2]
    dq_ref[...] = dq0_ref[...].astype(F32) + got[0:PAIR]
    total = wmine_ref[...] + jnp.concatenate([got[PAIR : PAIR + 256], got[PAIR + 256 : PAIR + 512]], axis=1)
    for et in range(2):
        at = et * 4 * COLS
        to = et * 2 * COLS
        keep_ref[to : to + 2 * COLS] = total[at : at + 2 * COLS]
        send_ref[to : to + COLS] = total[at + 3 * COLS : at + 4 * COLS].astype(BF16)
        send_ref[to + COLS : to + 2 * COLS] = total[at + 2 * COLS : at + 3 * COLS].astype(BF16)


def half_kernel(keep_ref, got_ref, out_ref, send_ref):
    total = keep_ref[...] + got_ref[...].astype(F32)
    for et in range(2):
        out_ref[et * COLS : (et + 1) * COLS] = total[et * 2 * COLS : (et * 2 + 1) * COLS]
        send_ref[et * COLS : (et + 1) * COLS] = total[(et * 2 + 1) * COLS : (et * 2 + 2) * COLS].astype(BF16)


def total_kernel(k0_ref, k1_ref, k2_ref, k3_ref, dq_ref, wkeep_ref, wgot_ref, keep_ref, wmine_ref, send_ref):
    dkv = k0_ref[...] + sum(ref[...].astype(F32) for ref in (k1_ref, k2_ref, k3_ref))
    both = jnp.concatenate([dq_ref[...], dkv], axis=1).astype(BF16)
    keep_ref[...] = both[0:PAD]
    for i in range(3):
        send_ref[i * PAD : (i + 1) * PAD] = both[PAD:PAIR, i * DH : (i + 1) * DH]
    weights = wkeep_ref[...] + wgot_ref[...].astype(F32)
    wmine_ref[...] = weights[0:COLS]
    piece = weights[COLS : 2 * COLS].astype(BF16)
    send_ref[3 * PAD : 3 * PAD + COLS] = piece[:, 0:DH]
    send_ref[3 * PAD + COLS : 3 * PAD + 2 * COLS] = piece[:, DH:FEATS]


def place_kernel(at_ref, mine_ref, wmine_ref, got_ref, dq_ref, dk_ref, dv_ref, dwo_ref):
    even = at_ref[0] == 0
    for i, ref in enumerate((dq_ref, dk_ref, dv_ref)):
        mine = mine_ref[0:ROWS, i * DH : (i + 1) * DH]
        other = got_ref[i * PAD : i * PAD + ROWS]
        ref[:, 0:DH] = jnp.where(even, mine, other)
        ref[:, DH:FEATS] = jnp.where(even, other, mine)
    got = got_ref[3 * PAD : 3 * PAD + 2 * COLS].astype(F32)
    dwo_ref[...] = wmine_ref[...] + jnp.concatenate([got[0:COLS], got[COLS : 2 * COLS]], axis=1)


def shifted(value, axis, size, by):
    return lax.ppermute(value, axis, [(i, (i + by) % size) for i in range(size)])


def swapped(value, axis, size, mask):
    return lax.ppermute(value, axis, [(i, i ^ mask) for i in range(size)])


def around(value, axis):
    return [value] + [shifted(value, axis, 4, s) for s in (1, 2, 3)]


def local(queries, key_rows, value_rows, scale_of, wo, dy):
    axes = ("e", "head", "zr", "x", "c")
    at = jnp.stack([lax.axis_index(name) for name in axes]).astype(jnp.int32)
    ids = jnp.pad(scale_of, (0, 8 * DH - ROWS), constant_values=-1).reshape(8, DH).astype(F32)
    pair = (PAIR, FEATS)

    keep, send, qkeep, qsend = call(
        pack_kernel,
        "pack",
        [at, jnp.stack([queries, key_rows, value_rows]), ids],
        [shape((PAD, FEATS))] * 2 + [shape((PAD, DH))] * 2,
        scalars=1,
    )
    kv = jnp.concatenate([keep, swapped(send, "e", 2, 1)], axis=0)
    dy, send = lax.optimization_barrier((dy, send))
    dys = around(jnp.where(scale_of[:, None] >= 0, dy, 0), "head")
    wo, _ = lax.optimization_barrier((wo, dys[0]))
    at_head = lax.axis_index("head")
    wo = jnp.concatenate(
        [lax.dynamic_slice_in_dim(wo, lax.rem(at_head - s + NH, NH) * WIDE, WIDE, 1) for s in range(NH)], axis=1
    )
    keep, send = call(
        dattn_kernel, "dattn", [at, *dys, wo, qkeep, qsend], [shape((PAD, FEATS))] * 2, scalars=1
    )
    kv_late, send = lax.optimization_barrier((kv, send))
    kvs = [kv, shifted(kv, "zr", 4, 1), shifted(kv_late, "zr", 4, 2), shifted(kv, "zr", 4, 3)]
    qs = around(jnp.concatenate([keep, swapped(send, "e", 2, 1)], axis=0), "x")
    kvs = kvs + [swapped(one, "c", 2, 1) for one in kvs]

    *loads, q, qm, kv, km = call(
        forward_kernel,
        "forward",
        [*qs, *kvs],
        [shape((LOAD, DH))] * 4 + [shape((NQ, FEATS)), shape((NQ, DH)), shape((NK, FEATS)), shape((NK, DH))],
        [pltpu.VMEM((NQ, DH), BF16), pltpu.VMEM((8, NQ), F32)],
        flops=6 * NQ * NK * DH,
    )
    loads = [loads[0]] + [shifted(loads[s], "x", 4, -s) for s in (1, 2, 3)]

    keep, send = call(merge_kernel, "merge", loads, [shape((PAD, DH))] * 2)
    other = swapped(send, "e", 2, 1)
    q, send = lax.optimization_barrier((q, send))
    scratch = [pltpu.VMEM((NQ, FEATS), BF16), pltpu.VMEM((NQ, NQ), BF16)]
    dkv_send, dq_part = call(
        functools.partial(backward_kernel, NQ),
        "backward_far",
        [q, qm, kv, km, *loads],
        [shape((4, *pair)), shape((NQ, DH), F32)],
        scratch,
        flops=6 * NQ * NK * DH,
    )
    other, dq_part = lax.optimization_barrier((other, dq_part))
    *outs, wkeep, wsend = call(
        project_kernel,
        "project",
        [at, keep, other, wo, *dys],
        [shape((ROWS, WIDE))] * 4 + [shape((4, 256, FEATS))] * 2,
        [pltpu.VMEM((4, WIDE, FEATS), BF16)],
        scalars=1,
    )
    wsend, dq_part = lax.optimization_barrier((wsend, dq_part))
    dkv_keep, *dqs = call(
        functools.partial(backward_kernel, 0),
        "backward_near",
        [q, qm, kv, km, *loads, dq_part],
        [shape((4, *pair))] + [shape((PAIR, DH))] * 4,
        scratch,
        flops=6 * NQ * NK * DH,
    )
    mine, *far = call(
        core_kernel,
        "core",
        [dkv_keep, swapped(dkv_send, "c", 2, 1), wkeep, swapped(wsend, "c", 2, 1), *dqs[1:]],
        [shape(pair, F32)] + [shape(pair)] * 3 + [shape((256, FEATS), F32)] + [shape((PAIR + 512, DH))] * 3,
    )
    dkvs = [mine] + [shifted(far[s - 1], "zr", 4, -s) for s in (1, 2, 3)]
    xs = [shifted(far[3 + s], "x", 4, -s) for s in (1, 2, 3)]
    xs, dkvs = lax.optimization_barrier((xs, dkvs))
    dq, wkeep, wsend = call(
        ring_kernel,
        "ring",
        [dqs[0], far[3], *xs],
        [shape((PAIR, DH), F32), shape((128, FEATS), F32), shape((128, FEATS))],
    )
    wkeep, wsend = call(
        half_kernel,
        "half",
        [wkeep, swapped(wsend, "zr", 4, 3)],
        [shape((64, FEATS), F32), shape((64, FEATS))],
    )
    block_out = sum(
        [outs[0].astype(F32)] + [shifted(outs[s], "head", NH, s).astype(F32) for s in (1, 2, 3)]
    ).astype(BF16)
    keep, wkeep, send = call(
        total_kernel,
        "total",
        [*dkvs, dq, wkeep, swapped(wsend, "zr", 4, 1)],
        [shape((PAD, 3 * DH)), shape((COLS, FEATS), F32), shape((3 * PAD + 2 * COLS, DH))],
    )
    dq, dk, dv, dwo = call(
        place_kernel,
        "place",
        [at, keep, wkeep, swapped(send, "e", 2, 1)],
        [shape((ROWS, FEATS))] * 3 + [shape((COLS, FEATS), F32)],
        scalars=1,
    )
    return (block_out, dq, dk, dv, dwo.T)


def solution(mesh):
    fine = Mesh(mesh.devices.reshape(4, 2, 4, 2, NH), ("zr", "e", "x", "c", "head"))
    seq = ("zr", "e", "x", "c")
    placed = (
        P(seq, "head"),
        P(seq, "head"),
        P(seq, "head"),
        P(seq),
        P("head", None),
        P(seq, "head"),
    )
    return jax.shard_map(
        local,
        mesh=fine,
        in_specs=placed,
        out_specs=(
            P(seq, "head"),
            P(seq, "head"),
            P(seq, "head"),
            P(seq, "head"),
            P("head", seq),
        ),
        check_vma=False,
    )
```

```python
import functools
import math

import jax
import jax.numpy as jnp
from jax import lax
from jax.experimental import pallas as pl
from jax.experimental.pallas import tpu as pltpu
from jax.sharding import Mesh, PartitionSpec as P

DH = 128
ROWS = 136
PAD = 144
FINE = 128
REST = PAD - FINE
PAIR = 2 * PAD
NH = 4
QHALF = 8
NQ = QHALF * PAD
NK = 2 * NQ
QREST = QHALF * FINE
SUMS = 80
LOAD = PAIR + SUMS
FEATS = 2 * DH
MODEL = 2048
WIDE = MODEL // NH
COLS = 32
BLOCK = 384
BIG = -1e30
SCALE = DH ** (-0.5)
UNIT = SCALE * math.log2(math.e)
F32 = jnp.float32
BF16 = jnp.bfloat16
LAST = (((1,), (1,)), ((), ()))
FIRST = (((0,), (0,)), ((), ()))
PARAMS = pltpu.CompilerParams(vmem_limit_bytes=48 << 20)
VMEM = pl.BlockSpec(memory_space=pltpu.VMEM)
SMEM = pl.BlockSpec(memory_space=pltpu.SMEM)


def shape(dims, kind=BF16):
    return jax.ShapeDtypeStruct(dims, kind)


def call(kernel, name, ins, outs, scratch=(), scalars=0, flops=0):
    cost = pl.CostEstimate(flops=flops, bytes_accessed=1 << 20, transcendentals=0) if flops else None
    return pl.pallas_call(
        kernel,
        in_specs=[SMEM] * scalars + [VMEM] * (len(ins) - scalars),
        out_shape=outs,
        scratch_shapes=list(scratch),
        compiler_params=PARAMS,
        cost_estimate=cost,
        name=name,
    )(*ins)


def by_parity(e, first, second, keep_ref, send_ref):
    @pl.when(e == 0)
    def _():
        keep_ref[...] = first
        send_ref[...] = second

    @pl.when(e == 1)
    def _():
        keep_ref[...] = second
        send_ref[...] = first


def pack_kernel(at_ref, all_ref, ids_ref, keep_ref, send_ref, qkeep_ref, qsend_ref, dy_ref):
    ids = ids_ref[...].astype(BF16)
    zero = jnp.zeros((8, DH), BF16)
    kvs, qs = [], []
    for head in range(2):
        q, k, v = (all_ref[:, i * FEATS + head * DH : i * FEATS + (head + 1) * DH] for i in range(3))
        kvs.append(jnp.concatenate([k, ids, v, zero], axis=0))
        qs.append(jnp.concatenate([q, ids], axis=0))
    by_parity(at_ref[0], kvs[0], kvs[1], keep_ref, send_ref)
    by_parity(at_ref[0], qs[0], qs[1], qkeep_ref, qsend_ref)
    dy_ref[...] = all_ref[:, 3 * FEATS : 3 * FEATS + WIDE]


def dattn_kernel(at_ref, *refs):
    dy_refs, (wo_ref, ids_ref, qkeep_ref, qsend_ref, keep_ref, send_ref) = refs[0:4], refs[4:]
    acc = jnp.zeros((ROWS, FEATS), F32)
    for s, ref in enumerate(dy_refs):
        block = wo_ref[:, s * WIDE : (s + 1) * WIDE]
        acc = acc + lax.dot_general(ref[...], block, LAST, preferred_element_type=F32)
    ids = ids_ref[...].T
    real = jnp.concatenate([ids[:, 0:1], ids[0:8, 1:2]], axis=0) >= 0.0
    acc = jnp.where(real, acc, 0.0).astype(BF16)
    acc = jnp.concatenate([acc, jnp.zeros((PAD - ROWS, FEATS), BF16)], axis=0)
    keep_ref[0:PAD] = qkeep_ref[...]
    send_ref[0:PAD] = qsend_ref[...]
    by_parity(at_ref[0], acc[:, 0:DH], acc[:, DH:FEATS], keep_ref.at[PAD:PAIR], send_ref.at[PAD:PAIR])


def pairs_of(refs, slots):
    found = [None] * 4
    for i, slot in enumerate(slots):
        found[slot] = (refs[i // 2], i % 2 * PAIR)
    return found


def assemble(pairs, all_ref, base, cols):
    rest = base + QREST
    for j, (ref, at) in enumerate(pairs):
        for k in range(2):
            half = 2 * j + k
            top = at + k * PAD
            all_ref[base + half * FINE : base + (half + 1) * FINE, cols] = ref[top : top + FINE]
            all_ref[rest + half * REST : rest + (half + 1) * REST, cols] = ref[top + FINE : top + PAD]


def take_pair(value, j):
    pieces = []
    for half in (2 * j, 2 * j + 1):
        pieces.append(value[half * FINE : (half + 1) * FINE])
        pieces.append(value[QREST + half * REST : QREST + (half + 1) * REST])
    return jnp.concatenate(pieces, axis=0)


def masks(pairs, mask_ref, base, is_query):
    fine, last = [], []
    for ref, at in pairs:
        for k in range(2):
            rows = ref[at + k * PAD + FINE : at + (k + 1) * PAD].astype(F32)
            fine.append(rows[8:9])
            last.append(rows[9:10])
    fine = jnp.concatenate(fine, axis=0).T
    last = jnp.concatenate(last, axis=0).T
    rest = base + QREST

    def encode(column):
        lane = lax.broadcasted_iota(jnp.int32, (column.shape[0], DH), 1).astype(F32)
        if is_query:
            hidden = ((lane > column) & (lane < 13.0)) | (lane == 13.0)
            return jnp.where(hidden, BIG, 0.0).astype(BF16)
        return jnp.where(lane == jnp.where(column < 0.0, 13.0, column), 1.0, 0.0).astype(BF16)

    for half in range(2 * len(pairs)):
        mask_ref[base + half * FINE : base + (half + 1) * FINE] = encode(fine[:, half : half + 1])
        mask_ref[rest + half * REST : rest + (half + 1) * REST] = encode(last[0:REST, half : half + 1])


def in_three(row):
    high = row.astype(BF16).astype(F32)
    middle = (row - high).astype(BF16).astype(F32)
    return [high, middle, row - high - middle]


def forward_kernel(*refs):
    load_refs, q_ref, qm_ref, kv_ref, km_ref, o_ref, stat_ref = refs[12:16], *refs[16:22]
    left, right = slice(0, DH), slice(DH, FEATS)
    queries = pairs_of(refs[0:2], (0, 1, 3, 2))
    assemble(queries, q_ref, 0, left)
    assemble(pairs_of(refs[2:4], (0, 3, 1, 2)), q_ref, 0, right)
    masks(queries, qm_ref, 0, True)
    for base, parts in ((0, refs[4:8]), (NQ, refs[8:12])):
        keys = pairs_of(parts[0:2], (0, 1, 3, 2))
        assemble(keys, kv_ref, base, left)
        assemble(pairs_of(parts[2:4], (0, 3, 1, 2)), kv_ref, base, right)
        masks(keys, km_ref, base, False)
    k_ext = jnp.concatenate([kv_ref[:, 0:DH], km_ref[...]], axis=1)
    lane = lax.broadcasted_iota(jnp.int32, (BLOCK, DH), 1)
    for block in range(NQ // BLOCK):
        rows = slice(block * BLOCK, (block + 1) * BLOCK)
        q_ext = jnp.concatenate([q_ref[rows, 0:DH], qm_ref[rows]], axis=1)
        s = lax.dot_general(q_ext, k_ext, LAST, preferred_element_type=F32)
        top = jnp.max(s, axis=1, keepdims=True)
        p = jnp.exp2((s - top) * UNIT)
        total = jnp.sum(p, axis=1, keepdims=True)
        o = jnp.dot(p.astype(BF16), kv_ref[:, DH:FEATS], preferred_element_type=F32) / total
        o_ref[rows] = o.astype(BF16)
        lse = top * UNIT + jnp.log2(total)
        share = jnp.sum(o * q_ref[rows, DH:FEATS].astype(F32), axis=1, keepdims=True)
        stat = jnp.where(lane == 0, lse, jnp.where(lane == 1, share, 0.0))
        stat_ref[:, rows] = stat.T[0:8]
    none = jnp.zeros((2, NQ), F32)
    sums = jnp.concatenate(in_three(stat_ref[0:1]) + in_three(stat_ref[1:2]) + [none], axis=0)
    tiles = [sums[:, i * DH : (i + 1) * DH] for i in range(NQ // DH)] + [jnp.zeros((8, DH), F32)]
    sums = jnp.concatenate(tiles, axis=0).astype(BF16)
    for j in range(4):
        load_refs[j][0:PAIR] = take_pair(o_ref, j)
        load_refs[j][PAIR:LOAD] = sums


def row_sums(load_refs):
    lses, shares = [], []
    odd = lax.broadcasted_iota(jnp.int32, (8, DH), 1) % (4 * REST) >= 2 * REST
    for s, ref in enumerate(load_refs):
        sums = ref[PAIR:LOAD].astype(F32)
        tiles = [sums[8 * i : 8 * i + 8] for i in range(9)]
        last = tiles[8]
        if s % 2 == 1:
            last = jnp.where(odd, pltpu.roll(last, 2 * REST, 1), pltpu.roll(last, FINE - 2 * REST, 1))
        if s >= 2:
            last = pltpu.roll(last, FINE // 2, 1)
        rows = jnp.concatenate([tiles[2 * (j ^ s) + k] for j in range(4) for k in range(2)] + [last], axis=1)
        lses.append(rows[0:1] + rows[1:2] + rows[2:3])
        shares.append(rows[3:4] + rows[4:5] + rows[5:6])
    top = jnp.maximum(jnp.maximum(lses[0], lses[1]), jnp.maximum(lses[2], lses[3]))
    weights = [jnp.exp2(one - top) for one in lses]
    total = weights[0] + weights[1] + weights[2] + weights[3]
    delta = sum(weights[s] * shares[s] for s in range(4)) / total
    lse = top + jnp.log2(total)
    return jnp.where(lse < -1e28, 1e30, lse), delta


def backward_kernel(base, q_ref, qm_ref, kv_ref, km_ref, *refs):
    load_refs, refs = refs[0:4], refs[4:]
    if base == 0:
        dq_in_ref, refs = refs[0], refs[1:]
    dkv_out_ref, dq_refs, dkv_ref, ds_ref = refs[0], refs[1:-2], refs[-2], refs[-1]
    lse, delta = row_sums(load_refs)
    q = q_ref[:, 0:DH]
    da = q_ref[:, DH:FEATS]
    q_ext = jnp.concatenate([q, qm_ref[...]], axis=1)
    for block in range(NQ // BLOCK):
        rows = slice(block * BLOCK, (block + 1) * BLOCK)
        keys = slice(base + block * BLOCK, base + (block + 1) * BLOCK)
        k_ext = jnp.concatenate([kv_ref[keys, 0:DH], km_ref[keys]], axis=1)
        s = lax.dot_general(k_ext, q_ext, LAST, preferred_element_type=F32)
        p = jnp.exp2(s * UNIT - lse)
        dp = lax.dot_general(kv_ref[keys, DH:FEATS], da, LAST, preferred_element_type=F32)
        ds = (p * (dp - delta)).astype(BF16)
        dkv_ref[rows, DH:FEATS] = jnp.dot(p.astype(BF16), da, preferred_element_type=F32).astype(BF16)
        dkv_ref[rows, 0:DH] = (jnp.dot(ds, q, preferred_element_type=F32) * SCALE).astype(BF16)
        ds_ref[rows] = ds
    for j in range(4):
        pair = take_pair(dkv_ref, j)
        dkv_out_ref[j] = pair[:, 0:DH]
        dkv_out_ref[4 + j] = pair[:, DH:FEATS]
    keys = slice(base, base + NQ)
    dq = lax.dot_general(ds_ref[...], kv_ref[keys, 0:DH], FIRST, preferred_element_type=F32)
    if base > 0:
        dq_refs[0][...] = dq
    else:
        dq = (dq + dq_in_ref[...]) * SCALE
        for at, (mine, theirs) in enumerate(((0, 1), (3, 2))):
            dq_refs[0][at * PAIR : (at + 1) * PAIR] = take_pair(dq, mine)
            dq_refs[1][at * PAIR : (at + 1) * PAIR] = take_pair(dq, theirs).astype(BF16)


def merge_kernel(l0_ref, l1_ref, l2_ref, l3_ref, keep_ref, send_ref):
    load_refs = (l0_ref, l1_ref, l2_ref, l3_ref)
    fine, last = [], []
    for s, ref in enumerate(load_refs):
        sums = ref[PAIR:LOAD].astype(F32)
        rows = sums[0:72]
        lse = [rows[8 * i : 8 * i + 1] + rows[8 * i + 1 : 8 * i + 2] + rows[8 * i + 2 : 8 * i + 3] for i in (2 * s, 2 * s + 1, 8)]
        fine += lse[0:2]
        last.append(lse[2] if s == 0 else pltpu.roll(lse[2], FINE - 2 * REST * s, 1))
    fine = jnp.concatenate(fine, axis=0).T
    last = jnp.concatenate(last + last, axis=0).T
    for k, out_ref in ((0, keep_ref), (1, send_ref)):
        for rows, columns in (
            (slice(0, FINE), [fine[:, 2 * s + k : 2 * s + k + 1] for s in range(4)]),
            (slice(FINE, PAD), [last[k * REST : (k + 1) * REST, s : s + 1] for s in range(4)]),
        ):
            source = slice(k * PAD + rows.start, k * PAD + rows.stop)
            top = jnp.maximum(jnp.maximum(columns[0], columns[1]), jnp.maximum(columns[2], columns[3]))
            weights = [jnp.exp2(one - top) for one in columns]
            total = weights[0] + weights[1] + weights[2] + weights[3]
            acc = sum(weights[s] * load_refs[s][source].astype(F32) for s in range(4))
            out_ref[rows] = (acc * jnp.where(top < -1e28, 0.0, 1.0 / total)).astype(BF16)


def project_kernel(at_ref, mine_ref, other_ref, wo_ref, dy0_ref, dy1_ref, dy2_ref, dy3_ref, *refs):
    out_refs, keep_ref, send_ref, dwo_ref = refs[0:4], *refs[4:7]
    e, h, zr, x, c = (at_ref[i] for i in range(5))
    mine, other = mine_ref[...], other_ref[...]
    even = e == 0
    attn = jnp.concatenate([jnp.where(even, mine, other), jnp.where(even, other, mine)], axis=1)
    for s in range(NH):
        at = -s % NH * WIDE
        part = jnp.dot(attn, wo_ref[:, at : at + WIDE], preferred_element_type=F32)
        out_refs[s][...] = part[0:ROWS].astype(BF16)
    for s, ref in enumerate((dy0_ref, dy1_ref, dy2_ref, dy3_ref)):
        dwo_ref[s] = lax.dot_general(ref[...], attn[0:ROWS], FIRST, preferred_element_type=F32).astype(BF16)
    for xt in range(4):
        for et in range(2):
            for t in range(4):
                s = lax.rem(h - jnp.bitwise_xor(zr, t) + NH, NH)
                row = lax.rem(e + et, 2) * 256 + jnp.bitwise_xor(x, xt) * 64
                to = slice((et * 4 + t) * COLS, (et * 4 + t + 1) * COLS)
                keep_ref[xt, to] = dwo_ref[s, pl.ds(pl.multiple_of(row + c * COLS, COLS), COLS)]
                send_ref[xt, to] = dwo_ref[s, pl.ds(pl.multiple_of(row + (1 - c) * COLS, COLS), COLS)]


def split_up(total, mine, theirs, keep_ref, send_ref):
    rows = total.shape[1]
    for at in range(len(mine)):
        keep_ref[at * rows : (at + 1) * rows] = total[mine[at]]
        send_ref[at * rows : (at + 1) * rows] = total[theirs[at]].astype(BF16)


def core_kernel(keep_ref, got_ref, wkeep_ref, wgot_ref, *refs):
    total = keep_ref[...].astype(F32) + got_ref[...].astype(F32)
    split_up(total[0:4], (0, 3), (1, 2), refs[0], refs[1])
    split_up(total[4:8], (0, 1), (3, 2), refs[2], refs[3])
    weights = wkeep_ref[...].astype(F32) + wgot_ref[...].astype(F32)
    split_up(weights, (0, 1), (3, 2), refs[4], refs[5])


def middle_kernel(*refs):
    for i in range(4):
        keep_ref, got_ref, mine_ref, send_ref = refs[2 * i], refs[2 * i + 1], refs[8 + 2 * i], refs[9 + 2 * i]
        rows = mine_ref.shape[0]
        total = keep_ref[...] + got_ref[...].astype(F32)
        mine_ref[...] = total[0:rows]
        send_ref[...] = total[rows : 2 * rows].astype(BF16)


def ring_kernel(mine_ref, got_ref, keep_ref, send_ref):
    total = mine_ref[...] + got_ref[...].astype(F32)
    for et in range(2):
        at = et * 4 * COLS
        to = et * 2 * COLS
        keep_ref[to : to + 2 * COLS] = total[at : at + 2 * COLS]
        send_ref[to : to + COLS] = total[at + 3 * COLS : at + 4 * COLS].astype(BF16)
        send_ref[to + COLS : to + 2 * COLS] = total[at + 2 * COLS : at + 3 * COLS].astype(BF16)


def half_kernel(keep_ref, got_ref, out_ref, send_ref):
    total = keep_ref[...] + got_ref[...].astype(F32)
    for et in range(2):
        out_ref[et * COLS : (et + 1) * COLS] = total[et * 2 * COLS : (et * 2 + 1) * COLS]
        send_ref[et * COLS : (et + 1) * COLS] = total[(et * 2 + 1) * COLS : (et * 2 + 2) * COLS].astype(BF16)


def total_kernel(*refs):
    wkeep_ref, wgot_ref, keep_ref, wmine_ref, send_ref = refs[6:11]
    for i in range(3):
        total = (refs[2 * i][...] + refs[2 * i + 1][...].astype(F32)).astype(BF16)
        keep_ref[:, i * DH : (i + 1) * DH] = total[0:PAD]
        send_ref[i * PAD : (i + 1) * PAD] = total[PAD:PAIR]
    weights = wkeep_ref[...] + wgot_ref[...].astype(F32)
    wmine_ref[...] = weights[0:COLS]
    piece = weights[COLS : 2 * COLS].astype(BF16)
    send_ref[3 * PAD : 3 * PAD + COLS] = piece[:, 0:DH]
    send_ref[3 * PAD + COLS : 3 * PAD + 2 * COLS] = piece[:, DH:FEATS]


def place_kernel(at_ref, mine_ref, wmine_ref, got_ref, dq_ref, dk_ref, dv_ref, dwo_ref):
    even = at_ref[0] == 0
    for i, ref in enumerate((dq_ref, dk_ref, dv_ref)):
        mine = mine_ref[0:ROWS, i * DH : (i + 1) * DH]
        other = got_ref[i * PAD : i * PAD + ROWS]
        ref[:, 0:DH] = jnp.where(even, mine, other)
        ref[:, DH:FEATS] = jnp.where(even, other, mine)
    got = got_ref[3 * PAD : 3 * PAD + 2 * COLS].astype(F32)
    dwo_ref[...] = wmine_ref[...] + jnp.concatenate([got[0:COLS], got[COLS : 2 * COLS]], axis=1)


def shifted(value, axis, size, by):
    return lax.ppermute(value, axis, [(i, (i + by) % size) for i in range(size)])


def swapped(value, axis, size, mask):
    return lax.ppermute(value, axis, [(i, i ^ mask) for i in range(size)])


def around(value, axis):
    return [value] + [shifted(value, axis, 4, s) for s in (1, 2, 3)]


def doubled(value, axis, first, second):
    near = jnp.concatenate([value, swapped(value, axis, 4, first)], axis=0)
    return [near, swapped(near, axis, 4, second)]


def local(queries, key_rows, value_rows, scale_of, wo, dy):
    axes = ("e", "head", "zr", "x", "c")
    at = jnp.stack([lax.axis_index(name) for name in axes]).astype(jnp.int32)
    ids = jnp.pad(scale_of, (0, 8 * DH - ROWS), constant_values=-1).reshape(8, DH).astype(F32)
    pair = (PAIR, DH)

    keep, send, qkeep, qsend, dy = call(
        pack_kernel,
        "pack",
        [at, jnp.concatenate([queries, key_rows, value_rows, dy], axis=1), ids],
        [shape(pair)] * 2 + [shape((PAD, DH))] * 2 + [shape((ROWS, WIDE))],
        scalars=1,
    )
    got = swapped(send, "e", 2, 1)
    dy, send = lax.optimization_barrier((dy, send))
    ks = doubled(jnp.concatenate([keep[0:PAD], got[0:PAD]], axis=0), "zr", 1, 3)
    vs = doubled(jnp.concatenate([keep[PAD:PAIR], got[PAD:PAIR]], axis=0), "zr", 3, 1)
    dys = around(dy, "head")
    wo, _ = lax.optimization_barrier((wo, dy))
    at_head = lax.axis_index("head")
    wo = jnp.concatenate(
        [lax.dynamic_slice_in_dim(wo, lax.rem(at_head - s + NH, NH) * WIDE, WIDE, 1) for s in range(NH)], axis=1
    )
    keep, send = call(dattn_kernel, "dattn", [at, *dys, wo, ids, qkeep, qsend], [shape(pair)] * 2, scalars=1)
    got = swapped(send, "e", 2, 1)
    qs = doubled(jnp.concatenate([keep[0:PAD], got[0:PAD]], axis=0), "x", 1, 3)
    das = doubled(jnp.concatenate([keep[PAD:PAIR], got[PAD:PAIR]], axis=0), "x", 3, 1)
    kvs = ks + vs
    kvs = kvs + [swapped(one, "c", 2, 1) for one in kvs]

    *loads, q, qm, kv, km = call(
        forward_kernel,
        "forward",
        [*qs, *das, *kvs],
        [shape((LOAD, DH))] * 4 + [shape((NQ, FEATS)), shape((NQ, DH)), shape((NK, FEATS)), shape((NK, DH))],
        [pltpu.VMEM((NQ, DH), BF16), pltpu.VMEM((8, NQ), F32)],
        flops=6 * NQ * NK * DH,
    )
    loads = [loads[0]] + [swapped(loads[s], "x", 4, s) for s in (1, 2, 3)]

    keep, send = call(merge_kernel, "merge", loads, [shape((PAD, DH))] * 2)
    other = swapped(send, "e", 2, 1)
    q, send = lax.optimization_barrier((q, send))
    scratch = [pltpu.VMEM((NQ, FEATS), BF16), pltpu.VMEM((NQ, NQ), BF16)]
    dkv_send, dq_part = call(
        functools.partial(backward_kernel, NQ),
        "backward_far",
        [q, qm, kv, km, *loads],
        [shape((8, *pair)), shape((NQ, DH), F32)],
        scratch,
        flops=6 * NQ * NK * DH,
    )
    other, dq_part = lax.optimization_barrier((other, dq_part))
    *outs, wkeep, wsend = call(
        project_kernel,
        "project",
        [at, keep, other, wo, *dys],
        [shape((ROWS, WIDE))] * 4 + [shape((4, 256, FEATS))] * 2,
        [pltpu.VMEM((4, WIDE, FEATS), BF16)],
        scalars=1,
    )
    wsend, dq_part = lax.optimization_barrier((wsend, dq_part))
    twice = (2 * PAIR, DH)
    dkv_keep, dq_keep, dq_send = call(
        functools.partial(backward_kernel, 0),
        "backward_near",
        [q, qm, kv, km, *loads, dq_part],
        [shape((8, *pair)), shape(twice, F32), shape(twice)],
        scratch,
        flops=6 * NQ * NK * DH,
    )
    dk_keep, dk_send, dv_keep, dv_send, wkeep, wsend = call(
        core_kernel,
        "core",
        [dkv_keep, swapped(dkv_send, "c", 2, 1), wkeep, swapped(wsend, "c", 2, 1)],
        [shape(twice, F32), shape(twice)] * 2 + [shape((512, FEATS), F32), shape((512, FEATS))],
    )
    wkeep, wsend, dk, dk_send, dv, dv_send, dq, dq_send = call(
        middle_kernel,
        "middle",
        [wkeep, swapped(wsend, "x", 4, 3)]
        + [dk_keep, swapped(dk_send, "zr", 4, 1)]
        + [dv_keep, swapped(dv_send, "zr", 4, 3)]
        + [dq_keep, swapped(dq_send, "x", 4, 1)],
        [shape((256, FEATS), F32), shape((256, FEATS))] + [shape(pair, F32), shape(pair)] * 3,
    )
    landed = [swapped(wsend, "x", 4, 1), swapped(dq_send, "x", 4, 3)]
    landed += [swapped(dk_send, "zr", 4, 3), swapped(dv_send, "zr", 4, 1)]
    wgot, dq_got, dk_got, dv_got = lax.optimization_barrier(landed)
    wkeep, wsend = call(
        ring_kernel,
        "ring",
        [wkeep, wgot],
        [shape((128, FEATS), F32), shape((128, FEATS))],
    )
    wkeep, wsend = call(
        half_kernel,
        "half",
        [wkeep, swapped(wsend, "zr", 4, 3)],
        [shape((64, FEATS), F32), shape((64, FEATS))],
    )
    block_out = sum(
        [outs[0].astype(F32)] + [shifted(outs[s], "head", NH, s).astype(F32) for s in (1, 2, 3)]
    ).astype(BF16)
    keep, wkeep, send = call(
        total_kernel,
        "total",
        [dq, dq_got, dk, dk_got, dv, dv_got]
        + [wkeep, swapped(wsend, "zr", 4, 1)],
        [shape((PAD, 3 * DH)), shape((COLS, FEATS), F32), shape((3 * PAD + 2 * COLS, DH))],
    )
    dq, dk, dv, dwo = call(
        place_kernel,
        "place",
        [at, keep, wkeep, swapped(send, "e", 2, 1)],
        [shape((ROWS, FEATS))] * 3 + [shape((COLS, FEATS), F32)],
        scalars=1,
    )
    return (block_out, dq, dk, dv, dwo.T)


def solution(mesh):
    fine = Mesh(mesh.devices.reshape(4, 2, 4, 2, NH), ("zr", "e", "x", "c", "head"))
    seq = ("zr", "e", "x", "c")
    placed = (
        P(seq, "head"),
        P(seq, "head"),
        P(seq, "head"),
        P(seq),
        P("head", None),
        P(seq, "head"),
    )
    return jax.shard_map(
        local,
        mesh=fine,
        in_specs=placed,
        out_specs=(
            P(seq, "head"),
            P(seq, "head"),
            P(seq, "head"),
            P(seq, "head"),
            P("head", seq),
        ),
        check_vma=False,
    )
```

```python
import functools
import math

import jax
import jax.numpy as jnp
from jax import lax
from jax.experimental import pallas as pl
from jax.experimental.pallas import tpu as pltpu
from jax.sharding import Mesh, PartitionSpec as P

DH = 128
ROWS = 136
PAD = 144
FINE = 128
REST = PAD - FINE
PAIR = 2 * PAD
NH = 4
QHALF = 8
NQ = QHALF * PAD
NK = 2 * NQ
QREST = QHALF * FINE
SUMS = 80
LOAD = PAIR + SUMS
FEATS = 2 * DH
MODEL = 2048
WIDE = MODEL // NH
COLS = 32
BLOCK = 384
BIG = -1e30
SCALE = DH ** (-0.5)
UNIT = SCALE * math.log2(math.e)
F32 = jnp.float32
BF16 = jnp.bfloat16
LAST = (((1,), (1,)), ((), ()))
FIRST = (((0,), (0,)), ((), ()))
PARAMS = pltpu.CompilerParams(vmem_limit_bytes=48 << 20)
VMEM = pl.BlockSpec(memory_space=pltpu.VMEM)
SMEM = pl.BlockSpec(memory_space=pltpu.SMEM)


def shape(dims, kind=BF16):
    return jax.ShapeDtypeStruct(dims, kind)


def call(kernel, name, ins, outs, scratch=(), scalars=0, flops=0):
    cost = pl.CostEstimate(flops=flops, bytes_accessed=1 << 20, transcendentals=0) if flops else None
    return pl.pallas_call(
        kernel,
        in_specs=[SMEM] * scalars + [VMEM] * (len(ins) - scalars),
        out_shape=outs,
        scratch_shapes=list(scratch),
        compiler_params=PARAMS,
        cost_estimate=cost,
        name=name,
    )(*ins)


def by_parity(e, first, second, keep_ref, send_ref):
    @pl.when(e == 0)
    def _():
        keep_ref[...] = first
        send_ref[...] = second

    @pl.when(e == 1)
    def _():
        keep_ref[...] = second
        send_ref[...] = first


def pack_kernel(at_ref, all_ref, ids_ref, keep_ref, send_ref, dy_ref):
    ids = ids_ref[...].astype(BF16)
    zero = jnp.zeros((8, DH), BF16)
    heads = []
    for head in range(2):
        q, k, v = (all_ref[:, i * FEATS + head * DH : i * FEATS + (head + 1) * DH] for i in range(3))
        heads.append(jnp.concatenate([k, ids, v, zero, q, ids], axis=0))
    by_parity(at_ref[0], heads[0], heads[1], keep_ref, send_ref)
    dy_ref[...] = all_ref[:, 3 * FEATS : 3 * FEATS + WIDE]


def dattn_kernel(at_ref, *refs):
    dy_refs, (wo_ref, ids_ref, keep_ref, send_ref) = refs[0:4], refs[4:]
    acc = jnp.zeros((ROWS, FEATS), F32)
    for s, ref in enumerate(dy_refs):
        block = wo_ref[:, s * WIDE : (s + 1) * WIDE]
        acc = acc + lax.dot_general(ref[...], block, LAST, preferred_element_type=F32)
    ids = ids_ref[...].T
    real = jnp.concatenate([ids[:, 0:1], ids[0:8, 1:2]], axis=0) >= 0.0
    acc = jnp.where(real, acc, 0.0).astype(BF16)
    acc = jnp.concatenate([acc, jnp.zeros((PAD - ROWS, FEATS), BF16)], axis=0)
    by_parity(at_ref[0], acc[:, 0:DH], acc[:, DH:FEATS], keep_ref, send_ref)


def pairs_of(refs, slots):
    found = [None] * 4
    for i, slot in enumerate(slots):
        found[slot] = (refs[i // 2], i % 2 * PAIR)
    return found


def assemble(pairs, all_ref, base, cols):
    rest = base + QREST
    for j, (ref, at) in enumerate(pairs):
        for k in range(2):
            half = 2 * j + k
            top = at + k * PAD
            all_ref[base + half * FINE : base + (half + 1) * FINE, cols] = ref[top : top + FINE]
            all_ref[rest + half * REST : rest + (half + 1) * REST, cols] = ref[top + FINE : top + PAD]


def take_pair(value, j):
    pieces = []
    for half in (2 * j, 2 * j + 1):
        pieces.append(value[half * FINE : (half + 1) * FINE])
        pieces.append(value[QREST + half * REST : QREST + (half + 1) * REST])
    return jnp.concatenate(pieces, axis=0)


def masks(pairs, mask_ref, base, is_query):
    fine, last = [], []
    for ref, at in pairs:
        for k in range(2):
            rows = ref[at + k * PAD + FINE : at + (k + 1) * PAD].astype(F32)
            fine.append(rows[8:9])
            last.append(rows[9:10])
    fine = jnp.concatenate(fine, axis=0).T
    last = jnp.concatenate(last, axis=0).T
    rest = base + QREST

    def encode(column):
        lane = lax.broadcasted_iota(jnp.int32, (column.shape[0], DH), 1).astype(F32)
        if is_query:
            hidden = ((lane > column) & (lane < 13.0)) | (lane == 13.0)
            return jnp.where(hidden, BIG, 0.0).astype(BF16)
        return jnp.where(lane == jnp.where(column < 0.0, 13.0, column), 1.0, 0.0).astype(BF16)

    for half in range(2 * len(pairs)):
        mask_ref[base + half * FINE : base + (half + 1) * FINE] = encode(fine[:, half : half + 1])
        mask_ref[rest + half * REST : rest + (half + 1) * REST] = encode(last[0:REST, half : half + 1])


def in_three(row):
    high = row.astype(BF16).astype(F32)
    middle = (row - high).astype(BF16).astype(F32)
    return [high, middle, row - high - middle]


def forward_kernel(*refs):
    o_ref, stat_ref, q_ref, qm_ref, kv_ref, km_ref = refs[12:18]
    left, right = slice(0, DH), slice(DH, FEATS)
    queries = [(ref, 0) for ref in refs[0:4]]
    assemble(queries, q_ref, 0, left)
    masks(queries, qm_ref, 0, True)
    for base, parts in ((0, refs[4:8]), (NQ, refs[8:12])):
        keys = pairs_of(parts[0:2], (0, 1, 3, 2))
        assemble(keys, kv_ref, base, left)
        assemble(pairs_of(parts[2:4], (0, 3, 1, 2)), kv_ref, base, right)
        masks(keys, km_ref, base, False)
    k_ext = jnp.concatenate([kv_ref[:, 0:DH], km_ref[...]], axis=1)
    lane = lax.broadcasted_iota(jnp.int32, (BLOCK, DH), 1)
    for block in range(NQ // BLOCK):
        rows = slice(block * BLOCK, (block + 1) * BLOCK)
        q_ext = jnp.concatenate([q_ref[rows], qm_ref[rows]], axis=1)
        s = lax.dot_general(q_ext, k_ext, LAST, preferred_element_type=F32)
        top = jnp.max(s, axis=1, keepdims=True)
        p = jnp.exp2((s - top) * UNIT)
        total = jnp.sum(p, axis=1, keepdims=True)
        o = jnp.dot(p.astype(BF16), kv_ref[:, DH:FEATS], preferred_element_type=F32) / total
        o_ref[rows] = o
        lse = top * UNIT + jnp.log2(total)
        stat_ref[:, rows] = jnp.where(lane == 0, lse, 0.0).T[0:8]


def share_kernel(*refs):
    o_ref, stat_ref, load_refs, da_ref, delta_ref = refs[4], refs[5], refs[6:10], refs[10], refs[11]
    assemble([(ref, 0) for ref in refs[0:4]], da_ref, 0, slice(0, DH))
    lane = lax.broadcasted_iota(jnp.int32, (BLOCK, DH), 1)
    for block in range(NQ // BLOCK):
        rows = slice(block * BLOCK, (block + 1) * BLOCK)
        share = jnp.sum(o_ref[rows] * da_ref[rows].astype(F32), axis=1, keepdims=True)
        delta_ref[:, rows] = jnp.where(lane == 0, share, 0.0).T[0:8]
    none = jnp.zeros((2, NQ), F32)
    sums = jnp.concatenate(in_three(stat_ref[0:1]) + in_three(delta_ref[0:1]) + [none], axis=0)
    tiles = [sums[:, i * DH : (i + 1) * DH] for i in range(NQ // DH)] + [jnp.zeros((8, DH), F32)]
    sums = jnp.concatenate(tiles, axis=0).astype(BF16)
    for j in range(4):
        load_refs[j][0:PAIR] = take_pair(o_ref, j).astype(BF16)
        load_refs[j][PAIR:LOAD] = sums


def row_sums(load_refs):
    lses, shares = [], []
    odd = lax.broadcasted_iota(jnp.int32, (8, DH), 1) % (4 * REST) >= 2 * REST
    for s, ref in enumerate(load_refs):
        sums = ref[PAIR:LOAD].astype(F32)
        tiles = [sums[8 * i : 8 * i + 8] for i in range(9)]
        last = tiles[8]
        if s % 2 == 1:
            last = jnp.where(odd, pltpu.roll(last, 2 * REST, 1), pltpu.roll(last, FINE - 2 * REST, 1))
        if s >= 2:
            last = pltpu.roll(last, FINE // 2, 1)
        rows = jnp.concatenate([tiles[2 * (j ^ s) + k] for j in range(4) for k in range(2)] + [last], axis=1)
        lses.append(rows[0:1] + rows[1:2] + rows[2:3])
        shares.append(rows[3:4] + rows[4:5] + rows[5:6])
    top = jnp.maximum(jnp.maximum(lses[0], lses[1]), jnp.maximum(lses[2], lses[3]))
    weights = [jnp.exp2(one - top) for one in lses]
    total = weights[0] + weights[1] + weights[2] + weights[3]
    delta = sum(weights[s] * shares[s] for s in range(4)) / total
    lse = top + jnp.log2(total)
    return jnp.where(lse < -1e28, 1e30, lse), delta


def backward_kernel(base, first, last, q_ref, qm_ref, da_ref, kv_ref, km_ref, *refs):
    load_refs, refs = refs[0:4], refs[4:]
    if first > 0 or base == 0:
        dq_in_ref, refs = refs[0], refs[1:]
    if first > 0:
        rows_in_ref, refs = refs[0], refs[1:]
    out_refs, dkv_ref, ds_ref = refs[:-2], refs[-2], refs[-1]
    lse, delta = row_sums(load_refs)
    q = q_ref[...]
    da = da_ref[...]
    q_ext = jnp.concatenate([q, qm_ref[...]], axis=1)
    if first > 0:
        dkv_ref[0 : first * BLOCK] = rows_in_ref[...]
    for block in range(first, last):
        rows = slice(block * BLOCK, (block + 1) * BLOCK)
        keys = slice(base + block * BLOCK, base + (block + 1) * BLOCK)
        k_ext = jnp.concatenate([kv_ref[keys, 0:DH], km_ref[keys]], axis=1)
        s = lax.dot_general(k_ext, q_ext, LAST, preferred_element_type=F32)
        p = jnp.exp2(s * UNIT - lse)
        dp = lax.dot_general(kv_ref[keys, DH:FEATS], da, LAST, preferred_element_type=F32)
        ds = (p * (dp - delta)).astype(BF16)
        dkv_ref[rows, DH:FEATS] = jnp.dot(p.astype(BF16), da, preferred_element_type=F32).astype(BF16)
        dkv_ref[rows, 0:DH] = (jnp.dot(ds, q, preferred_element_type=F32) * SCALE).astype(BF16)
        ds_ref[rows] = ds
    if last * BLOCK < NQ:
        out_refs[0][...] = dkv_ref[0 : last * BLOCK]
    else:
        for j in range(4):
            pair = take_pair(dkv_ref, j)
            out_refs[0][j] = pair[:, 0:DH]
            out_refs[0][4 + j] = pair[:, DH:FEATS]
    rows = slice(first * BLOCK, last * BLOCK)
    keys = slice(base + rows.start, base + rows.stop)
    dq = lax.dot_general(ds_ref[rows], kv_ref[keys, 0:DH], FIRST, preferred_element_type=F32)
    if first > 0 or base == 0:
        dq = dq + dq_in_ref[...]
    if base > 0:
        out_refs[1][...] = dq
    else:
        dq = dq * SCALE
        for at, (mine, theirs) in enumerate(((0, 1), (3, 2))):
            out_refs[1][at * PAIR : (at + 1) * PAIR] = take_pair(dq, mine)
            out_refs[2][at * PAIR : (at + 1) * PAIR] = take_pair(dq, theirs).astype(BF16)


def merge_kernel(l0_ref, l1_ref, l2_ref, l3_ref, keep_ref, send_ref):
    load_refs = (l0_ref, l1_ref, l2_ref, l3_ref)
    fine, last = [], []
    for s, ref in enumerate(load_refs):
        sums = ref[PAIR:LOAD].astype(F32)
        rows = sums[0:72]
        lse = [rows[8 * i : 8 * i + 1] + rows[8 * i + 1 : 8 * i + 2] + rows[8 * i + 2 : 8 * i + 3] for i in (2 * s, 2 * s + 1, 8)]
        fine += lse[0:2]
        last.append(lse[2] if s == 0 else pltpu.roll(lse[2], FINE - 2 * REST * s, 1))
    fine = jnp.concatenate(fine, axis=0).T
    last = jnp.concatenate(last + last, axis=0).T
    for k, out_ref in ((0, keep_ref), (1, send_ref)):
        for rows, columns in (
            (slice(0, FINE), [fine[:, 2 * s + k : 2 * s + k + 1] for s in range(4)]),
            (slice(FINE, PAD), [last[k * REST : (k + 1) * REST, s : s + 1] for s in range(4)]),
        ):
            source = slice(k * PAD + rows.start, k * PAD + rows.stop)
            top = jnp.maximum(jnp.maximum(columns[0], columns[1]), jnp.maximum(columns[2], columns[3]))
            weights = [jnp.exp2(one - top) for one in columns]
            total = weights[0] + weights[1] + weights[2] + weights[3]
            acc = sum(weights[s] * load_refs[s][source].astype(F32) for s in range(4))
            out_ref[rows] = (acc * jnp.where(top < -1e28, 0.0, 1.0 / total)).astype(BF16)


def project_kernel(at_ref, mine_ref, other_ref, wo_ref, dy0_ref, dy1_ref, dy2_ref, dy3_ref, *refs):
    out_refs, keep_ref, send_ref, dwo_ref = refs[0:4], *refs[4:7]
    e, h, zr, x, c = (at_ref[i] for i in range(5))
    mine, other = mine_ref[...], other_ref[...]
    even = e == 0
    attn = jnp.concatenate([jnp.where(even, mine, other), jnp.where(even, other, mine)], axis=1)
    for s in range(NH):
        at = -s % NH * WIDE
        part = jnp.dot(attn, wo_ref[:, at : at + WIDE], preferred_element_type=F32)
        out_refs[s][...] = part[0:ROWS].astype(BF16)
    for s, ref in enumerate((dy0_ref, dy1_ref, dy2_ref, dy3_ref)):
        dwo_ref[s] = lax.dot_general(ref[...], attn[0:ROWS], FIRST, preferred_element_type=F32).astype(BF16)
    for xt in range(4):
        for et in range(2):
            for t in range(4):
                s = lax.rem(h - jnp.bitwise_xor(zr, t) + NH, NH)
                row = lax.rem(e + et, 2) * 256 + jnp.bitwise_xor(x, xt) * 64
                to = slice((et * 4 + t) * COLS, (et * 4 + t + 1) * COLS)
                keep_ref[xt, to] = dwo_ref[s, pl.ds(pl.multiple_of(row + c * COLS, COLS), COLS)]
                send_ref[xt, to] = dwo_ref[s, pl.ds(pl.multiple_of(row + (1 - c) * COLS, COLS), COLS)]


def split_up(total, mine, theirs, keep_ref, send_ref):
    rows = total.shape[1]
    for at in range(len(mine)):
        keep_ref[at * rows : (at + 1) * rows] = total[mine[at]]
        send_ref[at * rows : (at + 1) * rows] = total[theirs[at]].astype(BF16)


def core_kernel(keep_ref, got_ref, *refs):
    total = keep_ref[...].astype(F32) + got_ref[...].astype(F32)
    split_up(total[0:4], (0, 3), (1, 2), refs[0], refs[1])
    split_up(total[4:8], (0, 1), (3, 2), refs[2], refs[3])


def dwo_kernel(keep_ref, got_ref, mine_ref, send_ref):
    total = keep_ref[...].astype(F32) + got_ref[...].astype(F32)
    split_up(total, (0, 1), (3, 2), mine_ref, send_ref)


def middle_kernel(*refs):
    count = len(refs) // 4
    for i in range(count):
        keep_ref, got_ref = refs[2 * i : 2 * i + 2]
        mine_ref, send_ref = refs[2 * (count + i) : 2 * (count + i) + 2]
        rows = mine_ref.shape[0]
        total = keep_ref[...] + got_ref[...].astype(F32)
        mine_ref[...] = total[0:rows]
        send_ref[...] = total[rows : 2 * rows].astype(BF16)


def ring_kernel(mine_ref, got_ref, keep_ref, send_ref):
    total = mine_ref[...] + got_ref[...].astype(F32)
    for et in range(2):
        at = et * 4 * COLS
        to = et * 2 * COLS
        keep_ref[to : to + 2 * COLS] = total[at : at + 2 * COLS]
        send_ref[to : to + COLS] = total[at + 3 * COLS : at + 4 * COLS].astype(BF16)
        send_ref[to + COLS : to + 2 * COLS] = total[at + 2 * COLS : at + 3 * COLS].astype(BF16)


def half_kernel(keep_ref, got_ref, out_ref, send_ref):
    total = keep_ref[...] + got_ref[...].astype(F32)
    for et in range(2):
        out_ref[et * COLS : (et + 1) * COLS] = total[et * 2 * COLS : (et * 2 + 1) * COLS]
        send_ref[et * COLS : (et + 1) * COLS] = total[(et * 2 + 1) * COLS : (et * 2 + 2) * COLS].astype(BF16)


def total_kernel(*refs):
    wkeep_ref, wgot_ref, keep_ref, wmine_ref, send_ref = refs[6:11]
    for i in range(3):
        total = (refs[2 * i][...] + refs[2 * i + 1][...].astype(F32)).astype(BF16)
        keep_ref[:, i * DH : (i + 1) * DH] = total[0:PAD]
        send_ref[i * PAD : (i + 1) * PAD] = total[PAD:PAIR]
    weights = wkeep_ref[...] + wgot_ref[...].astype(F32)
    wmine_ref[...] = weights[0:COLS]
    piece = weights[COLS : 2 * COLS].astype(BF16)
    send_ref[3 * PAD : 3 * PAD + COLS] = piece[:, 0:DH]
    send_ref[3 * PAD + COLS : 3 * PAD + 2 * COLS] = piece[:, DH:FEATS]


def place_kernel(at_ref, mine_ref, wmine_ref, got_ref, dq_ref, dk_ref, dv_ref, dwo_ref):
    even = at_ref[0] == 0
    for i, ref in enumerate((dq_ref, dk_ref, dv_ref)):
        mine = mine_ref[0:ROWS, i * DH : (i + 1) * DH]
        other = got_ref[i * PAD : i * PAD + ROWS]
        ref[:, 0:DH] = jnp.where(even, mine, other)
        ref[:, DH:FEATS] = jnp.where(even, other, mine)
    got = got_ref[3 * PAD : 3 * PAD + 2 * COLS].astype(F32)
    dwo_ref[...] = wmine_ref[...] + jnp.concatenate([got[0:COLS], got[COLS : 2 * COLS]], axis=1)


def shifted(value, axis, size, by):
    return lax.ppermute(value, axis, [(i, (i + by) % size) for i in range(size)])


def swapped(value, axis, size, mask):
    return lax.ppermute(value, axis, [(i, i ^ mask) for i in range(size)])


def around(value, axis):
    return [value] + [shifted(value, axis, 4, s) for s in (1, 2, 3)]


def doubled(value, axis, first, second):
    near = jnp.concatenate([value, swapped(value, axis, 4, first)], axis=0)
    return [near, swapped(near, axis, 4, second)]


def local(queries, key_rows, value_rows, scale_of, wo, dy):
    axes = ("e", "head", "zr", "x", "c")
    at = jnp.stack([lax.axis_index(name) for name in axes]).astype(jnp.int32)
    ids = jnp.pad(scale_of, (0, 8 * DH - ROWS), constant_values=-1).reshape(8, DH).astype(F32)
    pair = (PAIR, DH)

    keep, send, dy = call(
        pack_kernel,
        "pack",
        [at, jnp.concatenate([queries, key_rows, value_rows, dy], axis=1), ids],
        [shape((3 * PAD, DH))] * 2 + [shape((ROWS, WIDE))],
        scalars=1,
    )
    got = swapped(send, "e", 2, 1)
    dy, send = lax.optimization_barrier((dy, send))
    k, v, q = (jnp.concatenate([keep[i : i + PAD], got[i : i + PAD]], axis=0) for i in (0, PAD, 2 * PAD))
    ks = doubled(k, "zr", 1, 3)
    vs = doubled(v, "zr", 3, 1)
    qs = [q] + [swapped(q, "x", 4, s) for s in (1, 2, 3)]
    dys = around(dy, "head")
    wo, _ = lax.optimization_barrier((wo, dy))
    at_head = lax.axis_index("head")
    wo = jnp.concatenate(
        [lax.dynamic_slice_in_dim(wo, lax.rem(at_head - s + NH, NH) * WIDE, WIDE, 1) for s in range(NH)], axis=1
    )
    qs, dys = lax.optimization_barrier((qs, dys))
    keep, send = call(dattn_kernel, "dattn", [at, *dys, wo, ids], [shape((PAD, DH))] * 2, scalars=1)
    da = jnp.concatenate([keep, swapped(send, "e", 2, 1)], axis=0)
    das = [da] + [swapped(da, "x", 4, s) for s in (1, 2, 3)]
    kvs = ks + vs
    kvs = kvs + [swapped(one, "c", 2, 1) for one in kvs]

    rows = (NQ, DH)
    o, stat, q, qm, kv, km = call(
        forward_kernel,
        "forward",
        [*qs, *kvs],
        [shape(rows, F32), shape((8, NQ), F32), shape(rows), shape(rows), shape((NK, FEATS)), shape((NK, DH))],
        flops=6 * NQ * NK * DH,
    )
    *loads, da = call(
        share_kernel, "share", [*das, o, stat], [shape((LOAD, DH))] * 4 + [shape(rows)], [pltpu.VMEM((8, NQ), F32)]
    )
    loads = [loads[0]] + [swapped(loads[s], "x", 4, s) for s in (1, 2, 3)]

    keep, send = call(merge_kernel, "merge", loads, [shape((PAD, DH))] * 2)
    other = swapped(send, "e", 2, 1)
    q, send = lax.optimization_barrier((q, send))
    scratch = [pltpu.VMEM((NQ, FEATS), BF16), pltpu.VMEM((NQ, NQ), BF16)]
    sides = [q, qm, da, kv, km, *loads]
    dkv_part, dq_part = call(
        functools.partial(backward_kernel, NQ, 0, 2),
        "backward_one",
        sides,
        [shape((2 * BLOCK, FEATS)), shape(rows, F32)],
        scratch,
        flops=4 * NQ * NK * DH,
    )
    other, dq_part = lax.optimization_barrier((other, dq_part))
    *outs, wkeep, wsend = call(
        project_kernel,
        "project",
        [at, keep, other, wo, *dys],
        [shape((ROWS, WIDE))] * 4 + [shape((4, 256, FEATS))] * 2,
        [pltpu.VMEM((4, WIDE, FEATS), BF16)],
        scalars=1,
    )
    wsend, dq_part = lax.optimization_barrier((wsend, dq_part))
    dkv_send, dq_part = call(
        functools.partial(backward_kernel, NQ, 2, 3),
        "backward_two",
        [*sides, dq_part, dkv_part],
        [shape((8, *pair)), shape(rows, F32)],
        scratch,
        flops=2 * NQ * NK * DH,
    )
    wgot, dq_part = lax.optimization_barrier((swapped(wsend, "c", 2, 1), dq_part))
    wkeep, wsend = call(
        dwo_kernel, "dwo", [wkeep, wgot], [shape((512, FEATS), F32), shape((512, FEATS))]
    )
    wsend, dq_part = lax.optimization_barrier((wsend, dq_part))
    twice = (2 * PAIR, DH)
    dkv_keep, dq_keep, dq_send = call(
        functools.partial(backward_kernel, 0, 0, 3),
        "backward_three",
        [*sides, dq_part],
        [shape((8, *pair)), shape(twice, F32), shape(twice)],
        scratch,
        flops=6 * NQ * NK * DH,
    )
    dk_keep, dk_send, dv_keep, dv_send = call(
        core_kernel, "core", [dkv_keep, swapped(dkv_send, "c", 2, 1)], [shape(twice, F32), shape(twice)] * 2
    )
    wgot, dk_send = lax.optimization_barrier((swapped(wsend, "x", 4, 3), dk_send))
    wkeep, wsend = call(
        middle_kernel, "middle_dwo", [wkeep, wgot], [shape((256, FEATS), F32), shape((256, FEATS))]
    )
    wkeep, wsend = call(
        ring_kernel,
        "ring",
        [wkeep, swapped(wsend, "x", 4, 1)],
        [shape((128, FEATS), F32), shape((128, FEATS))],
    )
    landed = [swapped(dk_send, "zr", 4, 1), swapped(dv_send, "zr", 4, 3), swapped(dq_send, "x", 4, 1), wsend]
    dk_got, dv_got, dq_got, wsend = lax.optimization_barrier(landed)
    dk, dk_send, dv, dv_send, dq, dq_send = call(
        middle_kernel,
        "middle",
        [dk_keep, dk_got, dv_keep, dv_got, dq_keep, dq_got],
        [shape(pair, F32), shape(pair)] * 3,
    )
    landed = [swapped(wsend, "zr", 4, 3), swapped(dq_send, "x", 4, 3)]
    landed += [swapped(dk_send, "zr", 4, 3), swapped(dv_send, "zr", 4, 1)]
    wgot, dq_got, dk_got, dv_got = lax.optimization_barrier(landed)
    wkeep, wsend = call(half_kernel, "half", [wkeep, wgot], [shape((64, FEATS), F32), shape((64, FEATS))])
    block_out = sum(
        [outs[0].astype(F32)] + [shifted(outs[s], "head", NH, s).astype(F32) for s in (1, 2, 3)]
    ).astype(BF16)
    keep, wkeep, send = call(
        total_kernel,
        "total",
        [dq, dq_got, dk, dk_got, dv, dv_got]
        + [wkeep, swapped(wsend, "zr", 4, 1)],
        [shape((PAD, 3 * DH)), shape((COLS, FEATS), F32), shape((3 * PAD + 2 * COLS, DH))],
    )
    dq, dk, dv, dwo = call(
        place_kernel,
        "place",
        [at, keep, wkeep, swapped(send, "e", 2, 1)],
        [shape((ROWS, FEATS))] * 3 + [shape((COLS, FEATS), F32)],
        scalars=1,
    )
    return (block_out, dq, dk, dv, dwo.T)


def solution(mesh):
    fine = Mesh(mesh.devices.reshape(4, 2, 4, 2, NH), ("zr", "e", "x", "c", "head"))
    seq = ("zr", "e", "x", "c")
    placed = (
        P(seq, "head"),
        P(seq, "head"),
        P(seq, "head"),
        P(seq),
        P("head", None),
        P(seq, "head"),
    )
    return jax.shard_map(
        local,
        mesh=fine,
        in_specs=placed,
        out_specs=(
            P(seq, "head"),
            P(seq, "head"),
            P(seq, "head"),
            P(seq, "head"),
            P("head", seq),
        ),
        check_vma=False,
    )
```

```python
import functools
import math

import jax
import jax.numpy as jnp
from jax import lax
from jax.experimental import pallas as pl
from jax.experimental.pallas import tpu as pltpu
from jax.sharding import Mesh, PartitionSpec as P

DH = 128
ROWS = 136
PAD = 144
FINE = 128
REST = PAD - FINE
PAIR = 2 * PAD
NH = 4
QHALF = 8
NQ = QHALF * PAD
NK = 2 * NQ
QREST = QHALF * FINE
SUMS = 80
LOAD = PAIR + SUMS
FEATS = 2 * DH
MODEL = 2048
WIDE = MODEL // NH
COLS = 32
BLOCK = 384
BIG = -1e30
SCALE = DH ** (-0.5)
UNIT = SCALE * math.log2(math.e)
F32 = jnp.float32
BF16 = jnp.bfloat16
LAST = (((1,), (1,)), ((), ()))
FIRST = (((0,), (0,)), ((), ()))
PARAMS = pltpu.CompilerParams(vmem_limit_bytes=48 << 20)
VMEM = pl.BlockSpec(memory_space=pltpu.VMEM)
SMEM = pl.BlockSpec(memory_space=pltpu.SMEM)


def shape(dims, kind=BF16):
    return jax.ShapeDtypeStruct(dims, kind)


def call(kernel, name, ins, outs, scratch=(), scalars=0, flops=0):
    cost = pl.CostEstimate(flops=flops, bytes_accessed=1 << 20, transcendentals=0) if flops else None
    return pl.pallas_call(
        kernel,
        in_specs=[SMEM] * scalars + [VMEM] * (len(ins) - scalars),
        out_shape=outs,
        scratch_shapes=list(scratch),
        compiler_params=PARAMS,
        cost_estimate=cost,
        name=name,
    )(*ins)


def choose(which, first, second):
    for value, stores in ((0, first), (1, second)):

        @pl.when(which == value)
        def _(stores=stores):
            for ref, what in stores:
                ref[...] = what


def by_parity(e, first, second, keep_ref, send_ref):
    choose(e, [(keep_ref, first), (send_ref, second)], [(keep_ref, second), (send_ref, first)])


def pack_kernel(at_ref, all_ref, ids_ref, xkeep_ref, qkeep_ref, esend_ref, csend_ref, both_ref, dy_ref):
    ids = ids_ref[...].astype(BF16)
    zero = jnp.zeros((8, DH), BF16)
    ks, vs, qs = [], [], []
    for head in range(2):
        q, k, v = (all_ref[:, i * FEATS + head * DH : i * FEATS + (head + 1) * DH] for i in range(3))
        ks.append(jnp.concatenate([k, ids], axis=0))
        vs.append(jnp.concatenate([v, zero], axis=0))
        qs.append(jnp.concatenate([q, ids], axis=0))
    top, low = slice(0, PAD), slice(PAD, PAIR)
    for c, (x, y) in enumerate(((ks, vs), (vs, ks))):

        @pl.when(at_ref[4] == c)
        def _(x=x, y=y):
            by_parity(at_ref[0], x[0], x[1], xkeep_ref, esend_ref.at[top])
            by_parity(at_ref[0], y[0], y[1], csend_ref, both_ref)

    by_parity(at_ref[0], qs[0], qs[1], qkeep_ref, esend_ref.at[low])
    dy_ref[...] = all_ref[:, 3 * FEATS : 3 * FEATS + WIDE]


def dattn_kernel(at_ref, *refs):
    dy_refs, (wo_ref, ids_ref, keep_ref, send_ref) = refs[0:4], refs[4:]
    acc = jnp.zeros((ROWS, FEATS), F32)
    for s, ref in enumerate(dy_refs):
        block = wo_ref[:, s * WIDE : (s + 1) * WIDE]
        acc = acc + lax.dot_general(ref[...], block, LAST, preferred_element_type=F32)
    ids = ids_ref[...].T
    real = jnp.concatenate([ids[:, 0:1], ids[0:8, 1:2]], axis=0) >= 0.0
    acc = jnp.where(real, acc, 0.0).astype(BF16)
    acc = jnp.concatenate([acc, jnp.zeros((PAD - ROWS, FEATS), BF16)], axis=0)
    by_parity(at_ref[0], acc[:, 0:DH], acc[:, DH:FEATS], keep_ref, send_ref)


def assemble(pairs, all_ref, base, cols):
    rest = base + QREST
    for j, (ref, at) in enumerate(pairs):
        for k in range(2):
            half = 2 * j + k
            top = at + k * PAD
            all_ref[base + half * FINE : base + (half + 1) * FINE, cols] = ref[top : top + FINE]
            all_ref[rest + half * REST : rest + (half + 1) * REST, cols] = ref[top + FINE : top + PAD]


def take_pair(value, j):
    pieces = []
    for half in (2 * j, 2 * j + 1):
        pieces.append(value[half * FINE : (half + 1) * FINE])
        pieces.append(value[QREST + half * REST : QREST + (half + 1) * REST])
    return jnp.concatenate(pieces, axis=0)


def masks(all_ref, mask_ref, base, is_query):
    fine, last = [], []
    for half in range(QHALF):
        at = base + QREST + half * REST
        rows = all_ref[at : at + REST, 0:DH].astype(F32)
        fine.append(rows[8:9])
        last.append(rows[9:10])
    fine = jnp.concatenate(fine, axis=0).T
    last = jnp.concatenate(last, axis=0).T
    rest = base + QREST

    def encode(column):
        lane = lax.broadcasted_iota(jnp.int32, (column.shape[0], DH), 1).astype(F32)
        if is_query:
            hidden = ((lane > column) & (lane < 13.0)) | (lane == 13.0)
            return jnp.where(hidden, BIG, 0.0).astype(BF16)
        return jnp.where(lane == jnp.where(column < 0.0, 13.0, column), 1.0, 0.0).astype(BF16)

    for half in range(QHALF):
        mask_ref[base + half * FINE : base + (half + 1) * FINE] = encode(fine[:, half : half + 1])
        mask_ref[rest + half * REST : rest + (half + 1) * REST] = encode(last[0:REST, half : half + 1])


def in_three(row):
    high = row.astype(BF16).astype(F32)
    middle = (row - high).astype(BF16).astype(F32)
    return [high, middle, row - high - middle]


def forward_kernel(at_ref, *refs):
    q_parts, here, there = refs[0:4], refs[4:6], refs[6:8]
    o_ref, stat_ref, q_ref, qm_ref, kv_ref, km_ref = refs[8:14]
    assemble([(ref, 0) for ref in q_parts], q_ref, 0, slice(0, DH))
    masks(q_ref, qm_ref, 0, True)
    for c, (keys, values) in enumerate(((here, there), (there, here))):

        @pl.when(at_ref[4] == c)
        def _(keys=keys, values=values):
            for tokens in range(2):
                k_at, v_at = tokens * PAIR, (1 - tokens) * PAIR
                k_next, v_next = k_at + 2 * PAIR, v_at + 2 * PAIR
                k_pairs = [(keys[0], k_at), (keys[0], k_next), (keys[1], k_next), (keys[1], k_at)]
                v_pairs = [(values[0], v_at), (values[1], v_at), (values[1], v_next), (values[0], v_next)]
                assemble(k_pairs, kv_ref, tokens * NQ, slice(0, DH))
                assemble(v_pairs, kv_ref, tokens * NQ, slice(DH, FEATS))

    for base in (0, NQ):
        masks(kv_ref, km_ref, base, False)
    k_ext = jnp.concatenate([kv_ref[:, 0:DH], km_ref[...]], axis=1)
    lane = lax.broadcasted_iota(jnp.int32, (BLOCK, DH), 1)

    def one(block, _):
        rows = pl.ds(pl.multiple_of(block * BLOCK, BLOCK), BLOCK)
        q_ext = jnp.concatenate([q_ref[rows], qm_ref[rows]], axis=1)
        s = lax.dot_general(q_ext, k_ext, LAST, preferred_element_type=F32)
        top = jnp.max(s, axis=1, keepdims=True)
        p = jnp.exp2((s - top) * UNIT)
        total = jnp.sum(p, axis=1, keepdims=True)
        o = jnp.dot(p.astype(BF16), kv_ref[:, DH:FEATS], preferred_element_type=F32) / total
        o_ref[rows] = o
        lse = top * UNIT + jnp.log2(total)
        stat_ref[:, rows] = jnp.where(lane == 0, lse, 0.0).T[0:8]
        return 0

    lax.fori_loop(0, NQ // BLOCK, one, 0)


def share_kernel(*refs):
    o_ref, stat_ref, load_refs, da_ref, delta_ref = refs[4], refs[5], refs[6:10], refs[10], refs[11]
    assemble([(ref, 0) for ref in refs[0:4]], da_ref, 0, slice(0, DH))
    lane = lax.broadcasted_iota(jnp.int32, (BLOCK, DH), 1)
    for block in range(NQ // BLOCK):
        rows = slice(block * BLOCK, (block + 1) * BLOCK)
        share = jnp.sum(o_ref[rows] * da_ref[rows].astype(F32), axis=1, keepdims=True)
        delta_ref[:, rows] = jnp.where(lane == 0, share, 0.0).T[0:8]
    none = jnp.zeros((2, NQ), F32)
    sums = jnp.concatenate(in_three(stat_ref[0:1]) + in_three(delta_ref[0:1]) + [none], axis=0)
    tiles = [sums[:, i * DH : (i + 1) * DH] for i in range(NQ // DH)] + [jnp.zeros((8, DH), F32)]
    sums = jnp.concatenate(tiles, axis=0).astype(BF16)
    for j in range(4):
        load_refs[j][0:PAIR] = take_pair(o_ref, j).astype(BF16)
        load_refs[j][PAIR:LOAD] = sums


def row_sums(load_refs):
    lses, shares = [], []
    odd = lax.broadcasted_iota(jnp.int32, (8, DH), 1) % (4 * REST) >= 2 * REST
    for s, ref in enumerate(load_refs):
        sums = ref[PAIR:LOAD].astype(F32)
        tiles = [sums[8 * i : 8 * i + 8] for i in range(9)]
        last = tiles[8]
        if s % 2 == 1:
            last = jnp.where(odd, pltpu.roll(last, 2 * REST, 1), pltpu.roll(last, FINE - 2 * REST, 1))
        if s >= 2:
            last = pltpu.roll(last, FINE // 2, 1)
        rows = jnp.concatenate([tiles[2 * (j ^ s) + k] for j in range(4) for k in range(2)] + [last], axis=1)
        lses.append(rows[0:1] + rows[1:2] + rows[2:3])
        shares.append(rows[3:4] + rows[4:5] + rows[5:6])
    top = jnp.maximum(jnp.maximum(lses[0], lses[1]), jnp.maximum(lses[2], lses[3]))
    weights = [jnp.exp2(one - top) for one in lses]
    total = weights[0] + weights[1] + weights[2] + weights[3]
    delta = sum(weights[s] * shares[s] for s in range(4)) / total
    lse = top + jnp.log2(total)
    return jnp.where(lse < -1e28, 1e30, lse), delta


def backward_kernel(base, first, last, at_ref, q_ref, qm_ref, da_ref, kv_ref, km_ref, *refs):
    load_refs, refs = refs[0:4], refs[4:]
    if first > 0 or base > 0:
        dq_in_ref, refs = refs[0], refs[1:]
    if first > 0:
        rows_in_ref, refs = refs[0], refs[1:]
    out_refs, dkv_ref, ds_ref = refs[:-2], refs[-2], refs[-1]
    lse, delta = row_sums(load_refs)
    q = q_ref[...]
    da = da_ref[...]
    q_ext = jnp.concatenate([q, qm_ref[...]], axis=1)
    if first > 0:
        dkv_ref[0 : first * BLOCK] = rows_in_ref[...]

    def one(block, _):
        rows = pl.ds(pl.multiple_of(block * BLOCK, BLOCK), BLOCK)
        keys = pl.ds(pl.multiple_of(base + block * BLOCK, BLOCK), BLOCK)
        k_ext = jnp.concatenate([kv_ref[keys, 0:DH], km_ref[keys]], axis=1)
        s = lax.dot_general(k_ext, q_ext, LAST, preferred_element_type=F32)
        p = jnp.exp2(s * UNIT - lse)
        dp = lax.dot_general(kv_ref[keys, DH:FEATS], da, LAST, preferred_element_type=F32)
        ds = (p * (dp - delta)).astype(BF16)
        dkv_ref[rows, DH:FEATS] = jnp.dot(p.astype(BF16), da, preferred_element_type=F32).astype(BF16)
        dkv_ref[rows, 0:DH] = (jnp.dot(ds, q, preferred_element_type=F32) * SCALE).astype(BF16)
        ds_ref[rows] = ds
        return 0

    lax.fori_loop(first, last, one, 0)
    if last * BLOCK < NQ:
        out_refs[0][...] = dkv_ref[0 : last * BLOCK]
    else:
        for j in range(4):
            pair = take_pair(dkv_ref, j)
            by_parity(at_ref[4], pair[:, 0:DH], pair[:, DH:FEATS], out_refs[0].at[j], out_refs[1].at[j])
    rows = slice(first * BLOCK, last * BLOCK)
    keys = slice(base + rows.start, base + rows.stop)
    dq = lax.dot_general(ds_ref[rows], kv_ref[keys, 0:DH], FIRST, preferred_element_type=F32)
    if first > 0 or base > 0:
        dq = dq + dq_in_ref[...]
    if base == 0:
        out_refs[-1][...] = dq
    else:
        dq = dq * SCALE
        split_up(at_ref[4], [take_pair(dq, j) for j in range(4)], 0, *out_refs[2:4])


def merge_kernel(l0_ref, l1_ref, l2_ref, l3_ref, keep_ref, send_ref):
    load_refs = (l0_ref, l1_ref, l2_ref, l3_ref)
    fine, last = [], []
    for s, ref in enumerate(load_refs):
        sums = ref[PAIR:LOAD].astype(F32)
        rows = sums[0:72]
        lse = [rows[8 * i : 8 * i + 1] + rows[8 * i + 1 : 8 * i + 2] + rows[8 * i + 2 : 8 * i + 3] for i in (2 * s, 2 * s + 1, 8)]
        fine += lse[0:2]
        last.append(lse[2] if s == 0 else pltpu.roll(lse[2], FINE - 2 * REST * s, 1))
    fine = jnp.concatenate(fine, axis=0).T
    last = jnp.concatenate(last + last, axis=0).T
    for k, out_ref in ((0, keep_ref), (1, send_ref)):
        for rows, columns in (
            (slice(0, FINE), [fine[:, 2 * s + k : 2 * s + k + 1] for s in range(4)]),
            (slice(FINE, PAD), [last[k * REST : (k + 1) * REST, s : s + 1] for s in range(4)]),
        ):
            source = slice(k * PAD + rows.start, k * PAD + rows.stop)
            top = jnp.maximum(jnp.maximum(columns[0], columns[1]), jnp.maximum(columns[2], columns[3]))
            weights = [jnp.exp2(one - top) for one in columns]
            total = weights[0] + weights[1] + weights[2] + weights[3]
            acc = sum(weights[s] * load_refs[s][source].astype(F32) for s in range(4))
            out_ref[rows] = (acc * jnp.where(top < -1e28, 0.0, 1.0 / total)).astype(BF16)


def project_kernel(at_ref, mine_ref, other_ref, wo_ref, dy0_ref, dy1_ref, dy2_ref, dy3_ref, *refs):
    out_refs, keep_ref, send_ref, dwo_ref = refs[0:4], *refs[4:7]
    e, h, zr, x, c = (at_ref[i] for i in range(5))
    mine, other = mine_ref[...], other_ref[...]
    even = e == 0
    attn = jnp.concatenate([jnp.where(even, mine, other), jnp.where(even, other, mine)], axis=1)
    for s in range(NH):
        at = -s % NH * WIDE
        part = jnp.dot(attn, wo_ref[:, at : at + WIDE], preferred_element_type=F32)
        out_refs[s][...] = part[0:ROWS].astype(BF16)
    for s, ref in enumerate((dy0_ref, dy1_ref, dy2_ref, dy3_ref)):
        dwo_ref[s] = lax.dot_general(ref[...], attn[0:ROWS], FIRST, preferred_element_type=F32).astype(BF16)
    for xt in range(4):
        for et in range(2):
            for t in range(4):
                s = lax.rem(h - jnp.bitwise_xor(zr, t) + NH, NH)
                row = lax.rem(e + et, 2) * 256 + jnp.bitwise_xor(x, xt) * 64
                to = slice((et * 4 + t) * COLS, (et * 4 + t + 1) * COLS)
                keep_ref[xt, to] = dwo_ref[s, pl.ds(pl.multiple_of(row + c * COLS, COLS), COLS)]
                send_ref[xt, to] = dwo_ref[s, pl.ds(pl.multiple_of(row + (1 - c) * COLS, COLS), COLS)]


def split_up(c, total, flip, keep_ref, send_ref):
    rows = total[0].shape[0]

    def stores(mine, theirs):
        keep = [(keep_ref.at[i * rows : (i + 1) * rows], total[j]) for i, j in enumerate(mine)]
        return keep + [(send_ref.at[i * rows : (i + 1) * rows], total[j].astype(BF16)) for i, j in enumerate(theirs)]

    by_one, by_three = stores((0, 3), (1, 2)), stores((0, 1), (3, 2))
    choose(c, *((by_three, by_one) if flip else (by_one, by_three)))


def core_kernel(at_ref, keep0_ref, got0_ref, keep1_ref, got1_ref, keep_ref, send_ref):
    first = keep0_ref[...].astype(F32) + got0_ref[...].astype(F32)
    second = keep1_ref[...].astype(F32) + got1_ref[...].astype(F32)
    split_up(at_ref[4], [jnp.concatenate([first[j], second[j]], axis=0) for j in range(4)], 0, keep_ref, send_ref)


def dwo_kernel(at_ref, keep_ref, got_ref, mine_ref, send_ref):
    total = keep_ref[...].astype(F32) + got_ref[...].astype(F32)
    split_up(at_ref[4], [total[j] for j in range(4)], 1, mine_ref, send_ref)


def middle_kernel(*refs):
    count = len(refs) // 4
    for i in range(count):
        keep_ref, got_ref = refs[2 * i : 2 * i + 2]
        mine_ref, send_ref = refs[2 * (count + i) : 2 * (count + i) + 2]
        rows = mine_ref.shape[0]
        total = keep_ref[...] + got_ref[...].astype(F32)
        mine_ref[...] = total[0:rows]
        send_ref[...] = total[rows : 2 * rows].astype(BF16)


def ring_kernel(at_ref, mine_ref, got_ref, keep_ref, send_ref):
    total = mine_ref[...] + got_ref[...].astype(F32)
    pieces = []
    for t in range(4):
        pieces.append(jnp.concatenate([total[(et * 4 + t) * COLS : (et * 4 + t + 1) * COLS] for et in range(2)], axis=0))
    split_up(at_ref[4], pieces, 1, keep_ref, send_ref)


def total_kernel(at_ref, *refs):
    sums = [refs[2 * i][...] + refs[2 * i + 1][...].astype(F32) for i in range(3)]
    dq, dx, weights = sums
    qkeep_ref, xkeep_ref, wkeep_ref, esend_ref, csend_ref, both_ref = refs[6:12]
    dq, dx = dq.astype(BF16), dx.astype(BF16)
    qkeep_ref[...] = dq[0:PAD]
    esend_ref[0:PAD] = dq[PAD:PAIR]
    wkeep_ref[...] = weights[0:COLS]
    piece = weights[COLS : 2 * COLS].astype(BF16)
    esend_ref[PAIR : PAIR + COLS] = piece[:, 0:DH]
    esend_ref[PAIR + COLS : PAIR + 2 * COLS] = piece[:, DH:FEATS]
    to = (xkeep_ref, esend_ref.at[PAD:PAIR], csend_ref, both_ref)
    blocks = [dx[i * PAD : (i + 1) * PAD] for i in range(4)]
    choose(at_ref[4], list(zip(to, blocks)), list(zip(to, blocks[2:4] + blocks[0:2])))


def place_kernel(at_ref, dq_ref, dx_ref, wmine_ref, egot_ref, cgot_ref, both_ref, *out_refs):
    rows = slice(0, ROWS)
    even = at_ref[0] == 0
    pairs = [
        (dq_ref[rows], egot_ref[rows]),
        (dx_ref[rows], egot_ref[PAD : PAD + ROWS]),
        (cgot_ref[rows], both_ref[rows]),
    ]
    dq, dx, dy = [
        jnp.concatenate([jnp.where(even, mine, other), jnp.where(even, other, mine)], axis=1) for mine, other in pairs
    ]
    out_refs[0][...] = dq
    by_parity(at_ref[4], dx, dy, out_refs[1], out_refs[2])
    got = egot_ref[PAIR : PAIR + 2 * COLS].astype(F32)
    out_refs[3][...] = wmine_ref[...] + jnp.concatenate([got[0:COLS], got[COLS : 2 * COLS]], axis=1)


def shifted(value, axis, size, by):
    return lax.ppermute(value, axis, [(i, (i + by) % size) for i in range(size)])


def swapped(value, axis, size, mask):
    return lax.ppermute(value, axis, [(i, i ^ mask) for i in range(size)])


def around(value, axis):
    return [value] + [shifted(value, axis, 4, s) for s in (1, 2, 3)]


def by_core(value, axis, flip):
    masks = (3, 1) if flip else (1, 3)
    return lax.ppermute(value, (axis, "c"), [(i, (i // 2 ^ masks[i % 2]) * 2 + i % 2) for i in range(8)])


def crossed(value):
    return lax.ppermute(value, ("e", "c"), [(i, i ^ 3) for i in range(4)])


def local(queries, key_rows, value_rows, scale_of, wo, dy):
    axes = ("e", "head", "zr", "x", "c")
    at = jnp.stack([lax.axis_index(name) for name in axes]).astype(jnp.int32)
    ids = jnp.pad(scale_of, (0, 8 * DH - ROWS), constant_values=-1).reshape(8, DH).astype(F32)
    pair = (PAIR, DH)

    xkeep, qkeep, esend, csend, both, dy = call(
        pack_kernel,
        "pack",
        [at, jnp.concatenate([queries, key_rows, value_rows, dy], axis=1), ids],
        [shape((PAD, DH))] * 2 + [shape(pair)] + [shape((PAD, DH))] * 2 + [shape((ROWS, WIDE))],
        scalars=1,
    )
    egot, cgot, both_got = swapped(esend, "e", 2, 1), swapped(csend, "c", 2, 1), crossed(both)
    dy, esend = lax.optimization_barrier((dy, esend))
    near = jnp.concatenate([xkeep, egot[0:PAD], cgot, both_got], axis=0)
    near_got = by_core(near, "zr", 0)
    q = jnp.concatenate([qkeep, egot[PAD:PAIR]], axis=0)
    qs = [q] + [swapped(q, "x", 4, s) for s in (1, 2, 3)]
    dys = around(dy, "head")
    wo, _ = lax.optimization_barrier((wo, dy))
    at_head = lax.axis_index("head")
    wo = jnp.concatenate(
        [lax.dynamic_slice_in_dim(wo, lax.rem(at_head - s + NH, NH) * WIDE, WIDE, 1) for s in range(NH)], axis=1
    )
    qs, dys, near_got = lax.optimization_barrier((qs, dys, near_got))
    keep, send = call(dattn_kernel, "dattn", [at, *dys, wo, ids], [shape((PAD, DH))] * 2, scalars=1)
    near_got, send = lax.optimization_barrier((near_got, send))
    near = jnp.concatenate([near, near_got], axis=0)
    here = [near, by_core(near, "zr", 1)]
    da = jnp.concatenate([keep, swapped(send, "e", 2, 1)], axis=0)
    das = [da] + [swapped(da, "x", 4, s) for s in (1, 2, 3)]
    here[1], das = lax.optimization_barrier((here[1], das))
    there = [swapped(one, "c", 2, 1) for one in here]

    rows = (NQ, DH)
    o, stat, q, qm, kv, km = call(
        forward_kernel,
        "forward",
        [at, *qs, *here, *there],
        [shape(rows, F32), shape((8, NQ), F32), shape(rows), shape(rows), shape((NK, FEATS)), shape((NK, DH))],
        scalars=1,
        flops=6 * NQ * NK * DH,
    )
    *loads, da = call(
        share_kernel, "share", [*das, o, stat], [shape((LOAD, DH))] * 4 + [shape(rows)], [pltpu.VMEM((8, NQ), F32)]
    )
    loads = [loads[0]] + [swapped(loads[s], "x", 4, s) for s in (1, 2, 3)]

    keep, send = call(merge_kernel, "merge", loads, [shape((PAD, DH))] * 2)
    other = swapped(send, "e", 2, 1)
    q, send = lax.optimization_barrier((q, send))
    scratch = [pltpu.VMEM((NQ, FEATS), BF16), pltpu.VMEM((NQ, NQ), BF16)]
    sides = [at, q, qm, da, kv, km, *loads]
    dkv_part, dq_part = call(
        functools.partial(backward_kernel, 0, 0, 2),
        "backward_one",
        sides,
        [shape((2 * BLOCK, FEATS)), shape(rows, F32)],
        scratch,
        scalars=1,
        flops=4 * NQ * NK * DH,
    )
    other, dq_part = lax.optimization_barrier((other, dq_part))
    *outs, wkeep, wsend = call(
        project_kernel,
        "project",
        [at, keep, other, wo, *dys],
        [shape((ROWS, WIDE))] * 4 + [shape((4, 256, FEATS))] * 2,
        [pltpu.VMEM((4, WIDE, FEATS), BF16)],
        scalars=1,
    )
    wsend, dq_part = lax.optimization_barrier((wsend, dq_part))
    first_keep, first_send, dq_part = call(
        functools.partial(backward_kernel, 0, 2, 3),
        "backward_two",
        [*sides, dq_part, dkv_part],
        [shape((4, *pair))] * 2 + [shape(rows, F32)],
        scratch,
        scalars=1,
        flops=2 * NQ * NK * DH,
    )
    wgot, dq_part = lax.optimization_barrier((swapped(wsend, "c", 2, 1), dq_part))
    wkeep, wsend = call(
        dwo_kernel, "dwo", [at, wkeep, wgot], [shape((512, FEATS), F32), shape((512, FEATS))], scalars=1
    )
    wsend, dq_part = lax.optimization_barrier((wsend, dq_part))
    twice = (2 * PAIR, DH)
    second_keep, second_send, dq_keep, dq_send = call(
        functools.partial(backward_kernel, NQ, 0, 3),
        "backward_three",
        [*sides, dq_part],
        [shape((4, *pair))] * 2 + [shape(twice, F32), shape(twice)],
        scratch,
        scalars=1,
        flops=6 * NQ * NK * DH,
    )
    wgot, second_send = lax.optimization_barrier((by_core(wsend, "x", 1), second_send))
    dx_keep, dx_send = call(
        core_kernel,
        "core",
        [at, first_keep, swapped(first_send, "c", 2, 1), second_keep, swapped(second_send, "c", 2, 1)],
        [shape((4 * PAIR, DH), F32), shape((4 * PAIR, DH))],
        scalars=1,
    )
    wkeep, wsend = call(
        middle_kernel, "middle_dwo", [wkeep, wgot], [shape((256, FEATS), F32), shape((256, FEATS))]
    )
    wkeep, wsend = call(
        ring_kernel,
        "ring",
        [at, wkeep, by_core(wsend, "x", 0)],
        [shape((128, FEATS), F32), shape((128, FEATS))],
        scalars=1,
    )
    dx_got, dq_got, wsend = lax.optimization_barrier((by_core(dx_send, "zr", 0), by_core(dq_send, "x", 0), wsend))
    dx, dx_send, dq, dq_send = call(
        middle_kernel,
        "middle",
        [dx_keep, dx_got, dq_keep, dq_got],
        [shape(twice, F32), shape(twice), shape(pair, F32), shape(pair)],
    )
    landed = [by_core(wsend, "zr", 1), by_core(dq_send, "x", 1), by_core(dx_send, "zr", 1)]
    wgot, dq_got, dx_got = lax.optimization_barrier(landed)
    wkeep, wsend = call(middle_kernel, "half", [wkeep, wgot], [shape((64, FEATS), F32), shape((64, FEATS))])
    block_out = sum(
        [outs[0].astype(F32)] + [shifted(outs[s], "head", NH, s).astype(F32) for s in (1, 2, 3)]
    ).astype(BF16)
    qkeep, xkeep, wkeep, esend, csend, both = call(
        total_kernel,
        "total",
        [at, dq, dq_got, dx, dx_got, wkeep, by_core(wsend, "zr", 0)],
        [shape((PAD, DH))] * 2
        + [shape((COLS, FEATS), F32), shape((PAIR + 2 * COLS, DH))]
        + [shape((PAD, DH))] * 2,
        scalars=1,
    )
    dq, dk, dv, dwo = call(
        place_kernel,
        "place",
        [at, qkeep, xkeep, wkeep, swapped(esend, "e", 2, 1), swapped(csend, "c", 2, 1), crossed(both)],
        [shape((ROWS, FEATS))] * 3 + [shape((COLS, FEATS), F32)],
        scalars=1,
    )
    return (block_out, dq, dk, dv, dwo.T)


def solution(mesh):
    fine = Mesh(mesh.devices.reshape(4, 2, 4, 2, NH), ("zr", "e", "x", "c", "head"))
    seq = ("zr", "e", "x", "c")
    placed = (
        P(seq, "head"),
        P(seq, "head"),
        P(seq, "head"),
        P(seq),
        P("head", None),
        P(seq, "head"),
    )
    return jax.shard_map(
        local,
        mesh=fine,
        in_specs=placed,
        out_specs=(
            P(seq, "head"),
            P(seq, "head"),
            P(seq, "head"),
            P(seq, "head"),
            P("head", seq),
        ),
        check_vma=False,
    )
```

```python
import functools
import math

import jax
import jax.numpy as jnp
from jax import lax
from jax.experimental import pallas as pl
from jax.experimental.pallas import tpu as pltpu
from jax.sharding import Mesh, PartitionSpec as P

DH = 128
ROWS = 136
PAD = 144
FINE = 128
REST = PAD - FINE
PAIR = 2 * PAD
NH = 4
QHALF = 8
NQ = QHALF * PAD
NK = 2 * NQ
QREST = QHALF * FINE
SUMS = 80
LOAD = PAIR + SUMS
FEATS = 2 * DH
MODEL = 2048
WIDE = MODEL // NH
COLS = 32
BLOCK = 384
BIG = -1e30
SCALE = DH ** (-0.5)
UNIT = SCALE * math.log2(math.e)
F32 = jnp.float32
BF16 = jnp.bfloat16
LAST = (((1,), (1,)), ((), ()))
FIRST = (((0,), (0,)), ((), ()))
PARAMS = pltpu.CompilerParams(vmem_limit_bytes=48 << 20)
VMEM = pl.BlockSpec(memory_space=pltpu.VMEM)
SMEM = pl.BlockSpec(memory_space=pltpu.SMEM)


def shape(dims, kind=BF16):
    return jax.ShapeDtypeStruct(dims, kind)


def call(kernel, name, ins, outs, scratch=(), scalars=0, flops=0):
    cost = pl.CostEstimate(flops=flops, bytes_accessed=1 << 20, transcendentals=0) if flops else None
    return pl.pallas_call(
        kernel,
        in_specs=[SMEM] * scalars + [VMEM] * (len(ins) - scalars),
        out_shape=outs,
        scratch_shapes=list(scratch),
        compiler_params=PARAMS,
        cost_estimate=cost,
        name=name,
    )(*ins)


def by_parity(e, first, second, keep_ref, send_ref):
    @pl.when(e == 0)
    def _():
        keep_ref[...] = first
        send_ref[...] = second

    @pl.when(e == 1)
    def _():
        keep_ref[...] = second
        send_ref[...] = first


def pack_kernel(at_ref, all_ref, ids_ref, keep_ref, send_ref, dy_ref):
    ids = ids_ref[...].astype(BF16)
    zero = jnp.zeros((8, DH), BF16)
    heads = []
    for head in range(2):
        q, k, v = (all_ref[:, i * FEATS + head * DH : i * FEATS + (head + 1) * DH] for i in range(3))
        heads.append(jnp.concatenate([k, ids, v, zero, q, ids], axis=0))
    by_parity(at_ref[0], heads[0], heads[1], keep_ref, send_ref)
    dy_ref[...] = all_ref[:, 3 * FEATS : 3 * FEATS + WIDE]


def dattn_kernel(at_ref, *refs):
    dy_refs, (wo_ref, ids_ref, keep_ref, send_ref) = refs[0:4], refs[4:]
    acc = jnp.zeros((ROWS, FEATS), F32)
    for s, ref in enumerate(dy_refs):
        block = wo_ref[:, s * WIDE : (s + 1) * WIDE]
        acc = acc + lax.dot_general(ref[...], block, LAST, preferred_element_type=F32)
    ids = ids_ref[...].T
    real = jnp.concatenate([ids[:, 0:1], ids[0:8, 1:2]], axis=0) >= 0.0
    acc = jnp.where(real, acc, 0.0).astype(BF16)
    acc = jnp.concatenate([acc, jnp.zeros((PAD - ROWS, FEATS), BF16)], axis=0)
    by_parity(at_ref[0], acc[:, 0:DH], acc[:, DH:FEATS], keep_ref, send_ref)


def pairs_of(refs, slots, top):
    found = [None] * 4
    for i, slot in enumerate(slots):
        found[slot] = (refs[i // 2], top + i % 2 * PAIR)
    return found


def assemble(pairs, all_ref, base, cols):
    rest = base + QREST
    for j, (ref, at) in enumerate(pairs):
        for k in range(2):
            half = 2 * j + k
            top = at + k * PAD
            all_ref[base + half * FINE : base + (half + 1) * FINE, cols] = ref[top : top + FINE]
            all_ref[rest + half * REST : rest + (half + 1) * REST, cols] = ref[top + FINE : top + PAD]


def take_pair(value, j):
    pieces = []
    for half in (2 * j, 2 * j + 1):
        pieces.append(value[half * FINE : (half + 1) * FINE])
        pieces.append(value[QREST + half * REST : QREST + (half + 1) * REST])
    return jnp.concatenate(pieces, axis=0)


def masks(pairs, mask_ref, base, is_query):
    fine, last = [], []
    for ref, at in pairs:
        for k in range(2):
            rows = ref[at + k * PAD + FINE : at + (k + 1) * PAD].astype(F32)
            fine.append(rows[8:9])
            last.append(rows[9:10])
    fine = jnp.concatenate(fine, axis=0).T
    last = jnp.concatenate(last, axis=0).T
    rest = base + QREST

    def encode(column):
        lane = lax.broadcasted_iota(jnp.int32, (column.shape[0], DH), 1).astype(F32)
        if is_query:
            hidden = ((lane > column) & (lane < 13.0)) | (lane == 13.0)
            return jnp.where(hidden, BIG, 0.0).astype(BF16)
        return jnp.where(lane == jnp.where(column < 0.0, 13.0, column), 1.0, 0.0).astype(BF16)

    for half in range(2 * len(pairs)):
        mask_ref[base + half * FINE : base + (half + 1) * FINE] = encode(fine[:, half : half + 1])
        mask_ref[rest + half * REST : rest + (half + 1) * REST] = encode(last[0:REST, half : half + 1])


def in_three(row):
    high = row.astype(BF16).astype(F32)
    middle = (row - high).astype(BF16).astype(F32)
    return [high, middle, row - high - middle]


def forward_kernel(*refs):
    o_ref, stat_ref, q_ref, qm_ref, kv_ref, km_ref = refs[8:14]
    left, right = slice(0, DH), slice(DH, FEATS)
    queries = [(ref, 0) for ref in refs[0:4]]
    assemble(queries, q_ref, 0, left)
    masks(queries, qm_ref, 0, True)
    for base, parts in ((0, refs[4:6]), (NQ, refs[6:8])):
        keys = pairs_of(parts, (0, 1, 3, 2), 0)
        assemble(keys, kv_ref, base, left)
        assemble(pairs_of(parts, (0, 3, 1, 2), 2 * PAIR), kv_ref, base, right)
        masks(keys, km_ref, base, False)
    k_ext = jnp.concatenate([kv_ref[:, 0:DH], km_ref[...]], axis=1)
    lane = lax.broadcasted_iota(jnp.int32, (BLOCK, DH), 1)
    for block in range(NQ // BLOCK):
        rows = slice(block * BLOCK, (block + 1) * BLOCK)
        q_ext = jnp.concatenate([q_ref[rows], qm_ref[rows]], axis=1)
        s = lax.dot_general(q_ext, k_ext, LAST, preferred_element_type=F32)
        top = jnp.max(s, axis=1, keepdims=True)
        p = jnp.exp2((s - top) * UNIT)
        total = jnp.sum(p, axis=1, keepdims=True)
        o = jnp.dot(p.astype(BF16), kv_ref[:, DH:FEATS], preferred_element_type=F32) / total
        o_ref[rows] = o
        lse = top * UNIT + jnp.log2(total)
        stat_ref[:, rows] = jnp.where(lane == 0, lse, 0.0).T[0:8]


def share_kernel(*refs):
    o_ref, stat_ref, load_refs, da_ref, delta_ref = refs[4], refs[5], refs[6:10], refs[10], refs[11]
    assemble([(ref, 0) for ref in refs[0:4]], da_ref, 0, slice(0, DH))
    lane = lax.broadcasted_iota(jnp.int32, (BLOCK, DH), 1)
    for block in range(NQ // BLOCK):
        rows = slice(block * BLOCK, (block + 1) * BLOCK)
        share = jnp.sum(o_ref[rows] * da_ref[rows].astype(F32), axis=1, keepdims=True)
        delta_ref[:, rows] = jnp.where(lane == 0, share, 0.0).T[0:8]
    none = jnp.zeros((2, NQ), F32)
    sums = jnp.concatenate(in_three(stat_ref[0:1]) + in_three(delta_ref[0:1]) + [none], axis=0)
    tiles = [sums[:, i * DH : (i + 1) * DH] for i in range(NQ // DH)] + [jnp.zeros((8, DH), F32)]
    sums = jnp.concatenate(tiles, axis=0).astype(BF16)
    for j in range(4):
        load_refs[j][0:PAIR] = take_pair(o_ref, j).astype(BF16)
        load_refs[j][PAIR:LOAD] = sums


def row_sums(load_refs):
    lses, shares = [], []
    odd = lax.broadcasted_iota(jnp.int32, (8, DH), 1) % (4 * REST) >= 2 * REST
    for s, ref in enumerate(load_refs):
        sums = ref[PAIR:LOAD].astype(F32)
        tiles = [sums[8 * i : 8 * i + 8] for i in range(9)]
        last = tiles[8]
        if s % 2 == 1:
            last = jnp.where(odd, pltpu.roll(last, 2 * REST, 1), pltpu.roll(last, FINE - 2 * REST, 1))
        if s >= 2:
            last = pltpu.roll(last, FINE // 2, 1)
        rows = jnp.concatenate([tiles[2 * (j ^ s) + k] for j in range(4) for k in range(2)] + [last], axis=1)
        lses.append(rows[0:1] + rows[1:2] + rows[2:3])
        shares.append(rows[3:4] + rows[4:5] + rows[5:6])
    top = jnp.maximum(jnp.maximum(lses[0], lses[1]), jnp.maximum(lses[2], lses[3]))
    weights = [jnp.exp2(one - top) for one in lses]
    total = weights[0] + weights[1] + weights[2] + weights[3]
    delta = sum(weights[s] * shares[s] for s in range(4)) / total
    lse = top + jnp.log2(total)
    return jnp.where(lse < -1e28, 1e30, lse), delta


def backward_kernel(base, first, last, q_ref, qm_ref, da_ref, kv_ref, km_ref, *refs):
    load_refs, refs = refs[0:4], refs[4:]
    if first > 0 or base == 0:
        dq_in_ref, refs = refs[0], refs[1:]
    if first > 0:
        rows_in_ref, refs = refs[0], refs[1:]
    out_refs, dkv_ref, ds_ref = refs[:-2], refs[-2], refs[-1]
    lse, delta = row_sums(load_refs)
    q = q_ref[...]
    da = da_ref[...]
    q_ext = jnp.concatenate([q, qm_ref[...]], axis=1)
    if first > 0:
        dkv_ref[0 : first * BLOCK] = rows_in_ref[...]
    for block in range(first, last):
        rows = slice(block * BLOCK, (block + 1) * BLOCK)
        keys = slice(base + block * BLOCK, base + (block + 1) * BLOCK)
        k_ext = jnp.concatenate([kv_ref[keys, 0:DH], km_ref[keys]], axis=1)
        s = lax.dot_general(k_ext, q_ext, LAST, preferred_element_type=F32)
        p = jnp.exp2(s * UNIT - lse)
        dp = lax.dot_general(kv_ref[keys, DH:FEATS], da, LAST, preferred_element_type=F32)
        ds = (p * (dp - delta)).astype(BF16)
        dkv_ref[rows, DH:FEATS] = jnp.dot(p.astype(BF16), da, preferred_element_type=F32).astype(BF16)
        dkv_ref[rows, 0:DH] = (jnp.dot(ds, q, preferred_element_type=F32) * SCALE).astype(BF16)
        ds_ref[rows] = ds
    if last * BLOCK < NQ:
        out_refs[0][...] = dkv_ref[0 : last * BLOCK]
    else:
        for j in range(4):
            pair = take_pair(dkv_ref, j)
            out_refs[0][j] = pair[:, 0:DH]
            out_refs[0][4 + j] = pair[:, DH:FEATS]
    rows = slice(first * BLOCK, last * BLOCK)
    keys = slice(base + rows.start, base + rows.stop)
    dq = lax.dot_general(ds_ref[rows], kv_ref[keys, 0:DH], FIRST, preferred_element_type=F32)
    if first > 0 or base == 0:
        dq = dq + dq_in_ref[...]
    if base > 0:
        out_refs[1][...] = dq
    else:
        dq = dq * SCALE
        for at, (mine, theirs) in enumerate(((0, 1), (3, 2))):
            out_refs[1][at * PAIR : (at + 1) * PAIR] = take_pair(dq, mine)
            out_refs[2][at * PAIR : (at + 1) * PAIR] = take_pair(dq, theirs).astype(BF16)


def merge_kernel(l0_ref, l1_ref, l2_ref, l3_ref, keep_ref, send_ref):
    load_refs = (l0_ref, l1_ref, l2_ref, l3_ref)
    fine, last = [], []
    for s, ref in enumerate(load_refs):
        sums = ref[PAIR:LOAD].astype(F32)
        rows = sums[0:72]
        lse = [rows[8 * i : 8 * i + 1] + rows[8 * i + 1 : 8 * i + 2] + rows[8 * i + 2 : 8 * i + 3] for i in (2 * s, 2 * s + 1, 8)]
        fine += lse[0:2]
        last.append(lse[2] if s == 0 else pltpu.roll(lse[2], FINE - 2 * REST * s, 1))
    fine = jnp.concatenate(fine, axis=0).T
    last = jnp.concatenate(last + last, axis=0).T
    for k, out_ref in ((0, keep_ref), (1, send_ref)):
        for rows, columns in (
            (slice(0, FINE), [fine[:, 2 * s + k : 2 * s + k + 1] for s in range(4)]),
            (slice(FINE, PAD), [last[k * REST : (k + 1) * REST, s : s + 1] for s in range(4)]),
        ):
            source = slice(k * PAD + rows.start, k * PAD + rows.stop)
            top = jnp.maximum(jnp.maximum(columns[0], columns[1]), jnp.maximum(columns[2], columns[3]))
            weights = [jnp.exp2(one - top) for one in columns]
            total = weights[0] + weights[1] + weights[2] + weights[3]
            acc = sum(weights[s] * load_refs[s][source].astype(F32) for s in range(4))
            out_ref[rows] = (acc * jnp.where(top < -1e28, 0.0, 1.0 / total)).astype(BF16)


def project_kernel(at_ref, mine_ref, other_ref, wo_ref, dy0_ref, dy1_ref, dy2_ref, dy3_ref, *refs):
    out_refs, keep_ref, send_ref, dwo_ref = refs[0:4], *refs[4:7]
    e, h, zr, x, c = (at_ref[i] for i in range(5))
    mine, other = mine_ref[...], other_ref[...]
    even = e == 0
    attn = jnp.concatenate([jnp.where(even, mine, other), jnp.where(even, other, mine)], axis=1)
    for s in range(NH):
        at = -s % NH * WIDE
        part = jnp.dot(attn, wo_ref[:, at : at + WIDE], preferred_element_type=F32)
        out_refs[s][...] = part[0:ROWS].astype(BF16)
    for s, ref in enumerate((dy0_ref, dy1_ref, dy2_ref, dy3_ref)):
        dwo_ref[s] = lax.dot_general(ref[...], attn[0:ROWS], FIRST, preferred_element_type=F32).astype(BF16)
    for xt in range(4):
        for et in range(2):
            for t in range(4):
                s = lax.rem(h - jnp.bitwise_xor(zr, t) + NH, NH)
                row = lax.rem(e + et, 2) * 256 + jnp.bitwise_xor(x, xt) * 64
                to = slice((et * 4 + t) * COLS, (et * 4 + t + 1) * COLS)
                keep_ref[xt, to] = dwo_ref[s, pl.ds(pl.multiple_of(row + c * COLS, COLS), COLS)]
                send_ref[xt, to] = dwo_ref[s, pl.ds(pl.multiple_of(row + (1 - c) * COLS, COLS), COLS)]


def split_up(total, mine, theirs, keep_ref, send_ref):
    rows = total.shape[1]
    for at in range(len(mine)):
        keep_ref[at * rows : (at + 1) * rows] = total[mine[at]]
        send_ref[at * rows : (at + 1) * rows] = total[theirs[at]].astype(BF16)


def core_kernel(keep_ref, got_ref, *refs):
    total = keep_ref[...].astype(F32) + got_ref[...].astype(F32)
    split_up(total[0:4], (0, 3), (1, 2), refs[0], refs[1])
    split_up(total[4:8], (0, 1), (3, 2), refs[2], refs[3])


def dwo_kernel(keep_ref, got_ref, mine_ref, send_ref):
    total = keep_ref[...].astype(F32) + got_ref[...].astype(F32)
    split_up(total, (0, 1), (3, 2), mine_ref, send_ref)


def middle_kernel(*refs):
    count = len(refs) // 4
    for i in range(count):
        keep_ref, got_ref = refs[2 * i : 2 * i + 2]
        mine_ref, send_ref = refs[2 * (count + i) : 2 * (count + i) + 2]
        rows = mine_ref.shape[0]
        total = keep_ref[...] + got_ref[...].astype(F32)
        mine_ref[...] = total[0:rows]
        send_ref[...] = total[rows : 2 * rows].astype(BF16)


def ring_kernel(mine_ref, got_ref, keep_ref, send_ref):
    total = mine_ref[...] + got_ref[...].astype(F32)
    for et in range(2):
        at = et * 4 * COLS
        to = et * 2 * COLS
        keep_ref[to : to + 2 * COLS] = total[at : at + 2 * COLS]
        send_ref[to : to + COLS] = total[at + 3 * COLS : at + 4 * COLS].astype(BF16)
        send_ref[to + COLS : to + 2 * COLS] = total[at + 2 * COLS : at + 3 * COLS].astype(BF16)


def half_kernel(keep_ref, got_ref, out_ref, send_ref):
    total = keep_ref[...] + got_ref[...].astype(F32)
    for et in range(2):
        out_ref[et * COLS : (et + 1) * COLS] = total[et * 2 * COLS : (et * 2 + 1) * COLS]
        send_ref[et * COLS : (et + 1) * COLS] = total[(et * 2 + 1) * COLS : (et * 2 + 2) * COLS].astype(BF16)


def total_kernel(*refs):
    wkeep_ref, wgot_ref, keep_ref, wmine_ref, send_ref = refs[6:11]
    for i in range(3):
        total = (refs[2 * i][...] + refs[2 * i + 1][...].astype(F32)).astype(BF16)
        keep_ref[:, i * DH : (i + 1) * DH] = total[0:PAD]
        send_ref[i * PAD : (i + 1) * PAD] = total[PAD:PAIR]
    weights = wkeep_ref[...] + wgot_ref[...].astype(F32)
    wmine_ref[...] = weights[0:COLS]
    piece = weights[COLS : 2 * COLS].astype(BF16)
    send_ref[3 * PAD : 3 * PAD + COLS] = piece[:, 0:DH]
    send_ref[3 * PAD + COLS : 3 * PAD + 2 * COLS] = piece[:, DH:FEATS]


def place_kernel(at_ref, mine_ref, wmine_ref, got_ref, dq_ref, dk_ref, dv_ref, dwo_ref):
    even = at_ref[0] == 0
    for i, ref in enumerate((dq_ref, dk_ref, dv_ref)):
        mine = mine_ref[0:ROWS, i * DH : (i + 1) * DH]
        other = got_ref[i * PAD : i * PAD + ROWS]
        ref[:, 0:DH] = jnp.where(even, mine, other)
        ref[:, DH:FEATS] = jnp.where(even, other, mine)
    got = got_ref[3 * PAD : 3 * PAD + 2 * COLS].astype(F32)
    dwo_ref[...] = wmine_ref[...] + jnp.concatenate([got[0:COLS], got[COLS : 2 * COLS]], axis=1)


def shifted(value, axis, size, by):
    return lax.ppermute(value, axis, [(i, (i + by) % size) for i in range(size)])


def swapped(value, axis, size, mask):
    return lax.ppermute(value, axis, [(i, i ^ mask) for i in range(size)])


def around(value, axis):
    return [value] + [shifted(value, axis, 4, s) for s in (1, 2, 3)]


def local(queries, key_rows, value_rows, scale_of, wo, dy):
    axes = ("e", "head", "zr", "x", "c")
    at = jnp.stack([lax.axis_index(name) for name in axes]).astype(jnp.int32)
    ids = jnp.pad(scale_of, (0, 8 * DH - ROWS), constant_values=-1).reshape(8, DH).astype(F32)
    pair = (PAIR, DH)

    keep, send, dy = call(
        pack_kernel,
        "pack",
        [at, jnp.concatenate([queries, key_rows, value_rows, dy], axis=1), ids],
        [shape((3 * PAD, DH))] * 2 + [shape((ROWS, WIDE))],
        scalars=1,
    )
    got = swapped(send, "e", 2, 1)
    dy, send = lax.optimization_barrier((dy, send))
    k, v, q = (jnp.concatenate([keep[i : i + PAD], got[i : i + PAD]], axis=0) for i in (0, PAD, 2 * PAD))
    first = [swapped(k, "zr", 4, 1), swapped(v, "zr", 4, 3), swapped(q, "x", 4, 1), swapped(q, "x", 4, 3)]
    k_got, v_got, q_one, q_three = lax.optimization_barrier(first)
    k, v = jnp.concatenate([k, k_got], axis=0), jnp.concatenate([v, v_got], axis=0)
    dys = around(dy, "head")
    k, v, dys = lax.optimization_barrier((k, v, dys))
    ks, vs = [k, swapped(k, "zr", 4, 3)], [v, swapped(v, "zr", 4, 1)]
    qs = [q, q_one, swapped(q, "x", 4, 2), q_three]
    wo, _ = lax.optimization_barrier((wo, dy))
    at_head = lax.axis_index("head")
    wo = jnp.concatenate(
        [lax.dynamic_slice_in_dim(wo, lax.rem(at_head - s + NH, NH) * WIDE, WIDE, 1) for s in range(NH)], axis=1
    )
    keep, send = call(dattn_kernel, "dattn", [at, *dys, wo, ids], [shape((PAD, DH))] * 2, scalars=1)
    da = jnp.concatenate([keep, swapped(send, "e", 2, 1)], axis=0)
    das = [da] + [swapped(da, "x", 4, s) for s in (1, 2, 3)]
    ks[1], vs[1], das[1], das[3] = lax.optimization_barrier((ks[1], vs[1], das[1], das[3]))
    kvs = [jnp.concatenate([ks[i], vs[i]], axis=0) for i in range(2)]
    kvs = kvs + [swapped(one, "c", 2, 1) for one in kvs]

    rows = (NQ, DH)
    o, stat, q, qm, kv, km = call(
        forward_kernel,
        "forward",
        [*qs, *kvs],
        [shape(rows, F32), shape((8, NQ), F32), shape(rows), shape(rows), shape((NK, FEATS)), shape((NK, DH))],
        flops=6 * NQ * NK * DH,
    )
    *loads, da = call(
        share_kernel, "share", [*das, o, stat], [shape((LOAD, DH))] * 4 + [shape(rows)], [pltpu.VMEM((8, NQ), F32)]
    )
    loads = [loads[0]] + [swapped(loads[s], "x", 4, s) for s in (1, 2, 3)]

    keep, send = call(merge_kernel, "merge", loads, [shape((PAD, DH))] * 2)
    other = swapped(send, "e", 2, 1)
    q, send = lax.optimization_barrier((q, send))
    scratch = [pltpu.VMEM((NQ, FEATS), BF16), pltpu.VMEM((NQ, NQ), BF16)]
    sides = [q, qm, da, kv, km, *loads]
    dkv_part, dq_part = call(
        functools.partial(backward_kernel, NQ, 0, 2),
        "backward_one",
        sides,
        [shape((2 * BLOCK, FEATS)), shape(rows, F32)],
        scratch,
        flops=4 * NQ * NK * DH,
    )
    other, dq_part = lax.optimization_barrier((other, dq_part))
    *outs, wkeep, wsend = call(
        project_kernel,
        "project",
        [at, keep, other, wo, *dys],
        [shape((ROWS, WIDE))] * 4 + [shape((4, 256, FEATS))] * 2,
        [pltpu.VMEM((4, WIDE, FEATS), BF16)],
        scalars=1,
    )
    wsend, dq_part = lax.optimization_barrier((wsend, dq_part))
    dkv_send, dq_part = call(
        functools.partial(backward_kernel, NQ, 2, 3),
        "backward_two",
        [*sides, dq_part, dkv_part],
        [shape((8, *pair)), shape(rows, F32)],
        scratch,
        flops=2 * NQ * NK * DH,
    )
    wgot, dq_part = lax.optimization_barrier((swapped(wsend, "c", 2, 1), dq_part))
    wkeep, wsend = call(
        dwo_kernel, "dwo", [wkeep, wgot], [shape((512, FEATS), F32), shape((512, FEATS))]
    )
    wsend, dq_part = lax.optimization_barrier((wsend, dq_part))
    twice = (2 * PAIR, DH)
    dkv_keep, dq_keep, dq_send = call(
        functools.partial(backward_kernel, 0, 0, 3),
        "backward_three",
        [*sides, dq_part],
        [shape((8, *pair)), shape(twice, F32), shape(twice)],
        scratch,
        flops=6 * NQ * NK * DH,
    )
    dk_keep, dk_send, dv_keep, dv_send = call(
        core_kernel, "core", [dkv_keep, swapped(dkv_send, "c", 2, 1)], [shape(twice, F32), shape(twice)] * 2
    )
    wgot, dk_send = lax.optimization_barrier((swapped(wsend, "x", 4, 3), dk_send))
    wkeep, wsend = call(
        middle_kernel, "middle_dwo", [wkeep, wgot], [shape((256, FEATS), F32), shape((256, FEATS))]
    )
    wkeep, wsend = call(
        ring_kernel,
        "ring",
        [wkeep, swapped(wsend, "x", 4, 1)],
        [shape((128, FEATS), F32), shape((128, FEATS))],
    )
    wsend, outs[1], outs[3] = lax.optimization_barrier((wsend, outs[1], outs[3]))
    landed = [swapped(dk_send, "zr", 4, 1), swapped(dv_send, "zr", 4, 3), swapped(dq_send, "x", 4, 1), wsend]
    landed += [shifted(outs[1], "head", NH, 1), shifted(outs[3], "head", NH, 3)]
    dk_got, dv_got, dq_got, wsend, out_one, out_three = lax.optimization_barrier(landed)
    dk, dk_send, dv, dv_send, dq, dq_send = call(
        middle_kernel,
        "middle",
        [dk_keep, dk_got, dv_keep, dv_got, dq_keep, dq_got],
        [shape(pair, F32), shape(pair)] * 3,
    )
    wgot, dq_got = swapped(wsend, "zr", 4, 3), swapped(dq_send, "x", 4, 3)
    dk_got, dv_got = swapped(dk_send, "zr", 4, 3), swapped(dv_send, "zr", 4, 1)
    wkeep, wsend = call(half_kernel, "half", [wkeep, wgot], [shape((64, FEATS), F32), shape((64, FEATS))])
    out_two = shifted(outs[2], "head", NH, 2)
    block_out = sum(one.astype(F32) for one in (outs[0], out_one, out_two, out_three)).astype(BF16)
    keep, wkeep, send = call(
        total_kernel,
        "total",
        [dq, dq_got, dk, dk_got, dv, dv_got]
        + [wkeep, swapped(wsend, "zr", 4, 1)],
        [shape((PAD, 3 * DH)), shape((COLS, FEATS), F32), shape((3 * PAD + 2 * COLS, DH))],
    )
    dq, dk, dv, dwo = call(
        place_kernel,
        "place",
        [at, keep, wkeep, swapped(send, "e", 2, 1)],
        [shape((ROWS, FEATS))] * 3 + [shape((COLS, FEATS), F32)],
        scalars=1,
    )
    return (block_out, dq, dk, dv, dwo.T)


def solution(mesh):
    fine = Mesh(mesh.devices.reshape(4, 2, 4, 2, NH), ("zr", "e", "x", "c", "head"))
    seq = ("zr", "e", "x", "c")
    placed = (
        P(seq, "head"),
        P(seq, "head"),
        P(seq, "head"),
        P(seq),
        P("head", None),
        P(seq, "head"),
    )
    return jax.shard_map(
        local,
        mesh=fine,
        in_specs=placed,
        out_specs=(
            P(seq, "head"),
            P(seq, "head"),
            P(seq, "head"),
            P(seq, "head"),
            P("head", seq),
        ),
        check_vma=False,
    )
```

```python
import functools
import math

import jax
import jax.numpy as jnp
from jax import lax
from jax.experimental import pallas as pl
from jax.experimental.pallas import tpu as pltpu
from jax.sharding import Mesh, PartitionSpec as P

DH = 128
ROWS = 136
PAD = 144
FINE = 128
REST = PAD - FINE
PAIR = 2 * PAD
NH = 4
QHALF = 8
NQ = QHALF * PAD
NK = 2 * NQ
QREST = QHALF * FINE
SUMS = 80
LOAD = PAIR + SUMS
FEATS = 2 * DH
MODEL = 2048
WIDE = MODEL // NH
COLS = 32
BLOCK = 384
BIG = -1e30
SCALE = DH ** (-0.5)
UNIT = SCALE * math.log2(math.e)
F32 = jnp.float32
BF16 = jnp.bfloat16
LAST = (((1,), (1,)), ((), ()))
FIRST = (((0,), (0,)), ((), ()))
PARAMS = pltpu.CompilerParams(vmem_limit_bytes=48 << 20)
VMEM = pl.BlockSpec(memory_space=pltpu.VMEM)
SMEM = pl.BlockSpec(memory_space=pltpu.SMEM)


def shape(dims, kind=BF16):
    return jax.ShapeDtypeStruct(dims, kind)


def call(kernel, name, ins, outs, scratch=(), scalars=0, flops=0):
    cost = pl.CostEstimate(flops=flops, bytes_accessed=1 << 20, transcendentals=0) if flops else None
    return pl.pallas_call(
        kernel,
        in_specs=[SMEM] * scalars + [VMEM] * (len(ins) - scalars),
        out_shape=outs,
        scratch_shapes=list(scratch),
        compiler_params=PARAMS,
        cost_estimate=cost,
        name=name,
    )(*ins)


def by_parity(e, first, second, keep_ref, send_ref):
    @pl.when(e == 0)
    def _():
        keep_ref[...] = first
        send_ref[...] = second

    @pl.when(e == 1)
    def _():
        keep_ref[...] = second
        send_ref[...] = first


def pack_kernel(at_ref, all_ref, ids_ref, keep_ref, send_ref, dy_ref):
    ids = ids_ref[...].astype(BF16)
    zero = jnp.zeros((8, DH), BF16)
    heads = []
    for head in range(2):
        q, k, v = (all_ref[:, i * FEATS + head * DH : i * FEATS + (head + 1) * DH] for i in range(3))
        heads.append(jnp.concatenate([k, ids, v, zero, q, ids], axis=0))
    by_parity(at_ref[0], heads[0], heads[1], keep_ref, send_ref)
    dy_ref[...] = all_ref[:, 3 * FEATS : 3 * FEATS + WIDE]


def dattn_kernel(at_ref, *refs):
    dy_refs, (wo_ref, ids_ref, keep_ref, send_ref) = refs[0:4], refs[4:]
    acc = jnp.zeros((ROWS, FEATS), F32)
    for s, ref in enumerate(dy_refs):
        block = wo_ref[:, s * WIDE : (s + 1) * WIDE]
        acc = acc + lax.dot_general(ref[...], block, LAST, preferred_element_type=F32)
    ids = ids_ref[...].T
    real = jnp.concatenate([ids[:, 0:1], ids[0:8, 1:2]], axis=0) >= 0.0
    acc = jnp.where(real, acc, 0.0).astype(BF16)
    acc = jnp.concatenate([acc, jnp.zeros((PAD - ROWS, FEATS), BF16)], axis=0)
    by_parity(at_ref[0], acc[:, 0:DH], acc[:, DH:FEATS], keep_ref, send_ref)


def pairs_of(refs, slots, top):
    found = [None] * 4
    for i, slot in enumerate(slots):
        found[slot] = (refs[i // 2], top + i % 2 * PAIR)
    return found


def assemble(pairs, all_ref, base, cols):
    rest = base + QREST
    for j, (ref, at) in enumerate(pairs):
        for k in range(2):
            half = 2 * j + k
            top = at + k * PAD
            all_ref[base + half * FINE : base + (half + 1) * FINE, cols] = ref[top : top + FINE]
            all_ref[rest + half * REST : rest + (half + 1) * REST, cols] = ref[top + FINE : top + PAD]


def take_pair(value, j):
    pieces = []
    for half in (2 * j, 2 * j + 1):
        pieces.append(value[half * FINE : (half + 1) * FINE])
        pieces.append(value[QREST + half * REST : QREST + (half + 1) * REST])
    return jnp.concatenate(pieces, axis=0)


def masks(pairs, mask_ref, base, is_query):
    fine, last = [], []
    for ref, at in pairs:
        for k in range(2):
            rows = ref[at + k * PAD + FINE : at + (k + 1) * PAD].astype(F32)
            fine.append(rows[8:9])
            last.append(rows[9:10])
    fine = jnp.concatenate(fine, axis=0).T
    last = jnp.concatenate(last, axis=0).T
    rest = base + QREST

    def encode(column):
        lane = lax.broadcasted_iota(jnp.int32, (column.shape[0], DH), 1).astype(F32)
        if is_query:
            hidden = ((lane > column) & (lane < 13.0)) | (lane == 13.0)
            return jnp.where(hidden, BIG, 0.0).astype(BF16)
        return jnp.where(lane == jnp.where(column < 0.0, 13.0, column), 1.0, 0.0).astype(BF16)

    for half in range(2 * len(pairs)):
        mask_ref[base + half * FINE : base + (half + 1) * FINE] = encode(fine[:, half : half + 1])
        mask_ref[rest + half * REST : rest + (half + 1) * REST] = encode(last[0:REST, half : half + 1])


def in_three(row):
    high = row.astype(BF16).astype(F32)
    middle = (row - high).astype(BF16).astype(F32)
    return [high, middle, row - high - middle]


def forward_kernel(*refs):
    o_ref, stat_ref, q_ref, qm_ref, kv_ref, km_ref = refs[8:14]
    left, right = slice(0, DH), slice(DH, FEATS)
    queries = [(ref, 0) for ref in refs[0:4]]
    assemble(queries, q_ref, 0, left)
    masks(queries, qm_ref, 0, True)
    for base, parts in ((0, refs[4:6]), (NQ, refs[6:8])):
        keys = pairs_of(parts, (0, 1, 3, 2), 0)
        assemble(keys, kv_ref, base, left)
        assemble(pairs_of(parts, (0, 3, 1, 2), 2 * PAIR), kv_ref, base, right)
        masks(keys, km_ref, base, False)
    k_ext = jnp.concatenate([kv_ref[:, 0:DH], km_ref[...]], axis=1)
    lane = lax.broadcasted_iota(jnp.int32, (BLOCK, DH), 1)
    for block in range(NQ // BLOCK):
        rows = slice(block * BLOCK, (block + 1) * BLOCK)
        q_ext = jnp.concatenate([q_ref[rows], qm_ref[rows]], axis=1)
        s = lax.dot_general(q_ext, k_ext, LAST, preferred_element_type=F32)
        top = jnp.max(s, axis=1, keepdims=True)
        p = jnp.exp2((s - top) * UNIT)
        total = jnp.sum(p, axis=1, keepdims=True)
        o = jnp.dot(p.astype(BF16), kv_ref[:, DH:FEATS], preferred_element_type=F32) / total
        o_ref[rows] = o
        lse = top * UNIT + jnp.log2(total)
        stat_ref[:, rows] = jnp.where(lane == 0, lse, 0.0).T[0:8]


def share_kernel(*refs):
    o_ref, stat_ref, load_refs, da_ref, delta_ref = refs[4], refs[5], refs[6:10], refs[10], refs[11]
    assemble([(ref, 0) for ref in refs[0:4]], da_ref, 0, slice(0, DH))
    lane = lax.broadcasted_iota(jnp.int32, (BLOCK, DH), 1)
    for block in range(NQ // BLOCK):
        rows = slice(block * BLOCK, (block + 1) * BLOCK)
        share = jnp.sum(o_ref[rows] * da_ref[rows].astype(F32), axis=1, keepdims=True)
        delta_ref[:, rows] = jnp.where(lane == 0, share, 0.0).T[0:8]
    none = jnp.zeros((2, NQ), F32)
    sums = jnp.concatenate(in_three(stat_ref[0:1]) + in_three(delta_ref[0:1]) + [none], axis=0)
    tiles = [sums[:, i * DH : (i + 1) * DH] for i in range(NQ // DH)] + [jnp.zeros((8, DH), F32)]
    sums = jnp.concatenate(tiles, axis=0).astype(BF16)
    for j in range(4):
        load_refs[j][0:PAIR] = take_pair(o_ref, j).astype(BF16)
        load_refs[j][PAIR:LOAD] = sums


def row_sums(load_refs):
    lses, shares = [], []
    odd = lax.broadcasted_iota(jnp.int32, (8, DH), 1) % (4 * REST) >= 2 * REST
    for s, ref in enumerate(load_refs):
        sums = ref[PAIR:LOAD].astype(F32)
        tiles = [sums[8 * i : 8 * i + 8] for i in range(9)]
        last = tiles[8]
        if s % 2 == 1:
            last = jnp.where(odd, pltpu.roll(last, 2 * REST, 1), pltpu.roll(last, FINE - 2 * REST, 1))
        if s >= 2:
            last = pltpu.roll(last, FINE // 2, 1)
        rows = jnp.concatenate([tiles[2 * (j ^ s) + k] for j in range(4) for k in range(2)] + [last], axis=1)
        lses.append(rows[0:1] + rows[1:2] + rows[2:3])
        shares.append(rows[3:4] + rows[4:5] + rows[5:6])
    top = jnp.maximum(jnp.maximum(lses[0], lses[1]), jnp.maximum(lses[2], lses[3]))
    weights = [jnp.exp2(one - top) for one in lses]
    total = weights[0] + weights[1] + weights[2] + weights[3]
    delta = sum(weights[s] * shares[s] for s in range(4)) / total
    lse = top + jnp.log2(total)
    return jnp.where(lse < -1e28, 1e30, lse), delta


def backward_kernel(base, first, last, q_ref, qm_ref, da_ref, kv_ref, km_ref, *refs):
    rows_ref, refs = refs[0], refs[1:]
    if first > 0 or base == 0:
        dq_in_ref, refs = refs[0], refs[1:]
    if first > 0:
        rows_in_ref, refs = refs[0], refs[1:]
    out_refs, dkv_ref, ds_ref = refs[:-2], refs[-2], refs[-1]
    lse, delta = rows_ref[0:1], rows_ref[1:2]
    q = q_ref[...]
    da = da_ref[...]
    q_ext = jnp.concatenate([q, qm_ref[...]], axis=1)
    if first > 0:
        dkv_ref[0 : first * BLOCK] = rows_in_ref[...]
    for block in range(first, last):
        rows = slice(block * BLOCK, (block + 1) * BLOCK)
        keys = slice(base + block * BLOCK, base + (block + 1) * BLOCK)
        k_ext = jnp.concatenate([kv_ref[keys, 0:DH], km_ref[keys]], axis=1)
        s = lax.dot_general(k_ext, q_ext, LAST, preferred_element_type=F32)
        p = jnp.exp2(s * UNIT - lse)
        dp = lax.dot_general(kv_ref[keys, DH:FEATS], da, LAST, preferred_element_type=F32)
        ds = (p * (dp - delta)).astype(BF16)
        dkv_ref[rows, DH:FEATS] = jnp.dot(p.astype(BF16), da, preferred_element_type=F32).astype(BF16)
        dkv_ref[rows, 0:DH] = (jnp.dot(ds, q, preferred_element_type=F32) * SCALE).astype(BF16)
        ds_ref[rows] = ds
    if last * BLOCK < NQ:
        out_refs[0][...] = dkv_ref[0 : last * BLOCK]
    else:
        for j in range(4):
            pair = take_pair(dkv_ref, j)
            out_refs[0][j] = pair[:, 0:DH]
            out_refs[0][4 + j] = pair[:, DH:FEATS]
    rows = slice(first * BLOCK, last * BLOCK)
    keys = slice(base + rows.start, base + rows.stop)
    dq = lax.dot_general(ds_ref[rows], kv_ref[keys, 0:DH], FIRST, preferred_element_type=F32)
    if first > 0 or base == 0:
        dq = dq + dq_in_ref[...]
    if base > 0:
        out_refs[1][...] = dq
    else:
        dq = dq * SCALE
        for at, (mine, theirs) in enumerate(((0, 1), (3, 2))):
            out_refs[1][at * PAIR : (at + 1) * PAIR] = take_pair(dq, mine)
            out_refs[2][at * PAIR : (at + 1) * PAIR] = take_pair(dq, theirs).astype(BF16)


def merge_kernel(l0_ref, l1_ref, l2_ref, l3_ref, keep_ref, send_ref, rows_ref):
    load_refs = (l0_ref, l1_ref, l2_ref, l3_ref)
    lse, delta = row_sums(load_refs)
    rows_ref[0:1] = lse
    rows_ref[1:2] = delta
    fine, last = [], []
    for s, ref in enumerate(load_refs):
        sums = ref[PAIR:LOAD].astype(F32)
        rows = sums[0:72]
        lse = [rows[8 * i : 8 * i + 1] + rows[8 * i + 1 : 8 * i + 2] + rows[8 * i + 2 : 8 * i + 3] for i in (2 * s, 2 * s + 1, 8)]
        fine += lse[0:2]
        last.append(lse[2] if s == 0 else pltpu.roll(lse[2], FINE - 2 * REST * s, 1))
    fine = jnp.concatenate(fine, axis=0).T
    last = jnp.concatenate(last + last, axis=0).T
    for k, out_ref in ((0, keep_ref), (1, send_ref)):
        for rows, columns in (
            (slice(0, FINE), [fine[:, 2 * s + k : 2 * s + k + 1] for s in range(4)]),
            (slice(FINE, PAD), [last[k * REST : (k + 1) * REST, s : s + 1] for s in range(4)]),
        ):
            source = slice(k * PAD + rows.start, k * PAD + rows.stop)
            top = jnp.maximum(jnp.maximum(columns[0], columns[1]), jnp.maximum(columns[2], columns[3]))
            weights = [jnp.exp2(one - top) for one in columns]
            total = weights[0] + weights[1] + weights[2] + weights[3]
            acc = sum(weights[s] * load_refs[s][source].astype(F32) for s in range(4))
            out_ref[rows] = (acc * jnp.where(top < -1e28, 0.0, 1.0 / total)).astype(BF16)


def project_kernel(at_ref, mine_ref, other_ref, wo_ref, dy0_ref, dy1_ref, dy2_ref, dy3_ref, *refs):
    out_refs, keep_ref, send_ref, dwo_ref = refs[0:4], *refs[4:7]
    e, h, zr, x, c = (at_ref[i] for i in range(5))
    mine, other = mine_ref[...], other_ref[...]
    even = e == 0
    attn = jnp.concatenate([jnp.where(even, mine, other), jnp.where(even, other, mine)], axis=1)
    for s in range(NH):
        at = -s % NH * WIDE
        part = jnp.dot(attn, wo_ref[:, at : at + WIDE], preferred_element_type=F32)
        out_refs[s][...] = part[0:ROWS].astype(BF16)
    for s, ref in enumerate((dy0_ref, dy1_ref, dy2_ref, dy3_ref)):
        dwo_ref[s] = lax.dot_general(ref[...], attn[0:ROWS], FIRST, preferred_element_type=F32).astype(BF16)
    for ref, core in ((keep_ref, c), (send_ref, 1 - c)):
        for i, xt in enumerate((0, 1 + 2 * core, 3 - 2 * core, 2)):
            for et in range(2):
                for t in range(4):
                    s = lax.rem(h - jnp.bitwise_xor(zr, t) + NH, NH)
                    row = lax.rem(e + et, 2) * 256 + jnp.bitwise_xor(x, xt) * 64 + core * COLS
                    to = slice((et * 4 + t) * COLS, (et * 4 + t + 1) * COLS)
                    ref[i, to] = dwo_ref[s, pl.ds(pl.multiple_of(row, COLS), COLS)]


def split_up(total, mine, theirs, keep_ref, send_ref):
    rows = total.shape[1]
    for at in range(len(mine)):
        keep_ref[at * rows : (at + 1) * rows] = total[mine[at]]
        send_ref[at * rows : (at + 1) * rows] = total[theirs[at]].astype(BF16)


def core_kernel(keep_ref, got_ref, *refs):
    total = keep_ref[...].astype(F32) + got_ref[...].astype(F32)
    split_up(total[0:4], (0, 3), (1, 2), refs[0], refs[1])
    split_up(total[4:8], (0, 1), (3, 2), refs[2], refs[3])


def dwo_kernel(keep_ref, got_ref, mine_ref, send_ref):
    total = keep_ref[...].astype(F32) + got_ref[...].astype(F32)
    split_up(total, (0, 1), (2, 3), mine_ref, send_ref)


def middle_kernel(*refs):
    count = len(refs) // 4
    for i in range(count):
        keep_ref, got_ref = refs[2 * i : 2 * i + 2]
        mine_ref, send_ref = refs[2 * (count + i) : 2 * (count + i) + 2]
        rows = mine_ref.shape[0]
        total = keep_ref[...] + got_ref[...].astype(F32)
        mine_ref[...] = total[0:rows]
        send_ref[...] = total[rows : 2 * rows].astype(BF16)


def ring_kernel(mine_ref, got_ref, keep_ref, send_ref):
    total = mine_ref[...] + got_ref[...].astype(F32)
    for et in range(2):
        at = et * 4 * COLS
        to = et * 2 * COLS
        keep_ref[to : to + 2 * COLS] = total[at : at + 2 * COLS]
        send_ref[to : to + COLS] = total[at + 3 * COLS : at + 4 * COLS].astype(BF16)
        send_ref[to + COLS : to + 2 * COLS] = total[at + 2 * COLS : at + 3 * COLS].astype(BF16)


def half_kernel(keep_ref, got_ref, out_ref, send_ref):
    total = keep_ref[...] + got_ref[...].astype(F32)
    for et in range(2):
        out_ref[et * COLS : (et + 1) * COLS] = total[et * 2 * COLS : (et * 2 + 1) * COLS]
        send_ref[et * COLS : (et + 1) * COLS] = total[(et * 2 + 1) * COLS : (et * 2 + 2) * COLS].astype(BF16)


def total_kernel(*refs):
    wkeep_ref, wgot_ref, keep_ref, wmine_ref, send_ref = refs[6:11]
    for i in range(3):
        total = (refs[2 * i][...] + refs[2 * i + 1][...].astype(F32)).astype(BF16)
        keep_ref[:, i * DH : (i + 1) * DH] = total[0:PAD]
        send_ref[i * PAD : (i + 1) * PAD] = total[PAD:PAIR]
    weights = wkeep_ref[...] + wgot_ref[...].astype(F32)
    wmine_ref[...] = weights[0:COLS]
    piece = weights[COLS : 2 * COLS].astype(BF16)
    send_ref[3 * PAD : 3 * PAD + COLS] = piece[:, 0:DH]
    send_ref[3 * PAD + COLS : 3 * PAD + 2 * COLS] = piece[:, DH:FEATS]


def place_kernel(at_ref, mine_ref, wmine_ref, got_ref, dq_ref, dk_ref, dv_ref, dwo_ref):
    even = at_ref[0] == 0
    for i, ref in enumerate((dq_ref, dk_ref, dv_ref)):
        mine = mine_ref[0:ROWS, i * DH : (i + 1) * DH]
        other = got_ref[i * PAD : i * PAD + ROWS]
        ref[:, 0:DH] = jnp.where(even, mine, other)
        ref[:, DH:FEATS] = jnp.where(even, other, mine)
    got = got_ref[3 * PAD : 3 * PAD + 2 * COLS].astype(F32)
    dwo_ref[...] = wmine_ref[...] + jnp.concatenate([got[0:COLS], got[COLS : 2 * COLS]], axis=1)


def shifted(value, axis, size, by):
    return lax.ppermute(value, axis, [(i, (i + by) % size) for i in range(size)])


def swapped(value, axis, size, mask):
    return lax.ppermute(value, axis, [(i, i ^ mask) for i in range(size)])


def by_core(value, axis, flip):
    masks = (3, 1) if flip else (1, 3)
    return lax.ppermute(value, (axis, "c"), [(i, (i // 2 ^ masks[i % 2]) * 2 + i % 2) for i in range(8)])


def around(value, axis):
    return [value] + [shifted(value, axis, 4, s) for s in (1, 2, 3)]


def local(queries, key_rows, value_rows, scale_of, wo, dy):
    axes = ("e", "head", "zr", "x", "c")
    at = jnp.stack([lax.axis_index(name) for name in axes]).astype(jnp.int32)
    ids = jnp.pad(scale_of, (0, 8 * DH - ROWS), constant_values=-1).reshape(8, DH).astype(F32)
    pair = (PAIR, DH)

    keep, send, dy = call(
        pack_kernel,
        "pack",
        [at, jnp.concatenate([queries, key_rows, value_rows, dy], axis=1), ids],
        [shape((3 * PAD, DH))] * 2 + [shape((ROWS, WIDE))],
        scalars=1,
    )
    got = swapped(send, "e", 2, 1)
    dy, send = lax.optimization_barrier((dy, send))
    k, v, q = (jnp.concatenate([keep[i : i + PAD], got[i : i + PAD]], axis=0) for i in (0, PAD, 2 * PAD))
    k = jnp.concatenate([k, swapped(k, "zr", 4, 1)], axis=0)
    v = jnp.concatenate([v, swapped(v, "zr", 4, 3)], axis=0)
    dys = around(dy, "head")
    q_one, q_three = swapped(q, "x", 4, 1), swapped(q, "x", 4, 3)
    k, v, dys = lax.optimization_barrier((k, v, dys))
    ks, vs = [k, swapped(k, "zr", 4, 3)], [v, swapped(v, "zr", 4, 1)]
    dys, q_one, q_three = lax.optimization_barrier((dys, q_one, q_three))
    wo, _ = lax.optimization_barrier((wo, dy))
    at_head = lax.axis_index("head")
    wo = jnp.concatenate(
        [lax.dynamic_slice_in_dim(wo, lax.rem(at_head - s + NH, NH) * WIDE, WIDE, 1) for s in range(NH)], axis=1
    )
    keep, send = call(dattn_kernel, "dattn", [at, *dys, wo, ids], [shape((PAD, DH))] * 2, scalars=1)
    q_late, send = lax.optimization_barrier((q, send))
    q_two = swapped(q_late, "x", 4, 2)
    da = jnp.concatenate([keep, swapped(send, "e", 2, 1)], axis=0)
    das = [da] + [swapped(da, "x", 4, s) for s in (1, 2, 3)]
    late = [ks[1], vs[1], das[1], das[3], q_two]
    ks[1], vs[1], das[1], das[3], q_two = lax.optimization_barrier(late)
    qs = [q, q_one, q_two, q_three]
    kvs = [jnp.concatenate([ks[i], vs[i]], axis=0) for i in range(2)]
    kvs = kvs + [swapped(one, "c", 2, 1) for one in kvs]

    rows = (NQ, DH)
    o, stat, q, qm, kv, km = call(
        forward_kernel,
        "forward",
        [*qs, *kvs],
        [shape(rows, F32), shape((8, NQ), F32), shape(rows), shape(rows), shape((NK, FEATS)), shape((NK, DH))],
        flops=6 * NQ * NK * DH,
    )
    *loads, da = call(
        share_kernel, "share", [*das, o, stat], [shape((LOAD, DH))] * 4 + [shape(rows)], [pltpu.VMEM((8, NQ), F32)]
    )
    loads = [loads[0]] + [swapped(loads[s], "x", 4, s) for s in (1, 2, 3)]

    keep, send, sums = call(merge_kernel, "merge", loads, [shape((PAD, DH))] * 2 + [shape((8, NQ), F32)])
    other = swapped(send, "e", 2, 1)
    q, send = lax.optimization_barrier((q, send))
    scratch = [pltpu.VMEM((NQ, FEATS), BF16), pltpu.VMEM((NQ, NQ), BF16)]
    sides = [q, qm, da, kv, km, sums]
    dkv_part, dq_part = call(
        functools.partial(backward_kernel, NQ, 0, 2),
        "backward_one",
        sides,
        [shape((2 * BLOCK, FEATS)), shape(rows, F32)],
        scratch,
        flops=4 * NQ * NK * DH,
    )
    other, dq_part = lax.optimization_barrier((other, dq_part))
    *outs, wkeep, wsend = call(
        project_kernel,
        "project",
        [at, keep, other, wo, *dys],
        [shape((ROWS, WIDE))] * 4 + [shape((4, 256, FEATS))] * 2,
        [pltpu.VMEM((4, WIDE, FEATS), BF16)],
        scalars=1,
    )
    wsend, dq_part = lax.optimization_barrier((wsend, dq_part))
    dkv_send, dq_part = call(
        functools.partial(backward_kernel, NQ, 2, 3),
        "backward_two",
        [*sides, dq_part, dkv_part],
        [shape((8, *pair)), shape(rows, F32)],
        scratch,
        flops=2 * NQ * NK * DH,
    )
    wgot, dq_part = lax.optimization_barrier((swapped(wsend, "c", 2, 1), dq_part))
    wkeep, wsend = call(
        dwo_kernel, "dwo", [wkeep, wgot], [shape((512, FEATS), F32), shape((512, FEATS))]
    )
    wsend, dq_part = lax.optimization_barrier((wsend, dq_part))
    twice = (2 * PAIR, DH)
    dkv_keep, dq_keep, dq_send = call(
        functools.partial(backward_kernel, 0, 0, 3),
        "backward_three",
        [*sides, dq_part],
        [shape((8, *pair)), shape(twice, F32), shape(twice)],
        scratch,
        flops=6 * NQ * NK * DH,
    )
    dk_keep, dk_send, dv_keep, dv_send = call(
        core_kernel, "core", [dkv_keep, swapped(dkv_send, "c", 2, 1)], [shape(twice, F32), shape(twice)] * 2
    )
    wgot, dk_send = lax.optimization_barrier((by_core(wsend, "x", 1), dk_send))
    wkeep, wsend = call(
        middle_kernel, "middle_dwo", [wkeep, wgot], [shape((256, FEATS), F32), shape((256, FEATS))]
    )
    wkeep, wsend = call(
        ring_kernel,
        "ring",
        [wkeep, by_core(wsend, "x", 0)],
        [shape((128, FEATS), F32), shape((128, FEATS))],
    )
    wsend, outs[1], outs[3] = lax.optimization_barrier((wsend, outs[1], outs[3]))
    landed = [swapped(dk_send, "zr", 4, 1), swapped(dv_send, "zr", 4, 3), swapped(dq_send, "x", 4, 1), wsend]
    landed += [shifted(outs[1], "head", NH, 1), shifted(outs[3], "head", NH, 3)]
    dk_got, dv_got, dq_got, wsend, out_one, out_three = lax.optimization_barrier(landed)
    dk, dk_send, dv, dv_send, dq, dq_send = call(
        middle_kernel,
        "middle",
        [dk_keep, dk_got, dv_keep, dv_got, dq_keep, dq_got],
        [shape(pair, F32), shape(pair)] * 3,
    )
    wgot, dq_got = swapped(wsend, "zr", 4, 3), swapped(dq_send, "x", 4, 3)
    dk_got, dv_got = swapped(dk_send, "zr", 4, 3), swapped(dv_send, "zr", 4, 1)
    wkeep, wsend = call(half_kernel, "half", [wkeep, wgot], [shape((64, FEATS), F32), shape((64, FEATS))])
    out_two = shifted(outs[2], "head", NH, 2)
    block_out = sum(one.astype(F32) for one in (outs[0], out_one, out_two, out_three)).astype(BF16)
    keep, wkeep, send = call(
        total_kernel,
        "total",
        [dq, dq_got, dk, dk_got, dv, dv_got]
        + [wkeep, swapped(wsend, "zr", 4, 1)],
        [shape((PAD, 3 * DH)), shape((COLS, FEATS), F32), shape((3 * PAD + 2 * COLS, DH))],
    )
    dq, dk, dv, dwo = call(
        place_kernel,
        "place",
        [at, keep, wkeep, swapped(send, "e", 2, 1)],
        [shape((ROWS, FEATS))] * 3 + [shape((COLS, FEATS), F32)],
        scalars=1,
    )
    return (block_out, dq, dk, dv, dwo.T)


def solution(mesh):
    fine = Mesh(mesh.devices.reshape(4, 2, 4, 2, NH), ("zr", "e", "x", "c", "head"))
    seq = ("zr", "e", "x", "c")
    placed = (
        P(seq, "head"),
        P(seq, "head"),
        P(seq, "head"),
        P(seq),
        P("head", None),
        P(seq, "head"),
    )
    return jax.shard_map(
        local,
        mesh=fine,
        in_specs=placed,
        out_specs=(
            P(seq, "head"),
            P(seq, "head"),
            P(seq, "head"),
            P(seq, "head"),
            P("head", seq),
        ),
        check_vma=False,
    )
```

```python
import functools
import math

import jax
import jax.numpy as jnp
from jax import lax
from jax.experimental import pallas as pl
from jax.experimental.pallas import tpu as pltpu
from jax.sharding import Mesh, PartitionSpec as P

DH = 128
ROWS = 136
PAD = 144
FINE = 128
REST = PAD - FINE
PAIR = 2 * PAD
NH = 4
QHALF = 8
NQ = QHALF * PAD
NK = 2 * NQ
QREST = QHALF * FINE
SUMS = 80
LOAD = PAIR + SUMS
FEATS = 2 * DH
MODEL = 2048
WIDE = MODEL // NH
COLS = 32
BLOCK = 384
BIG = -1e30
SCALE = DH ** (-0.5)
UNIT = SCALE * math.log2(math.e)
F32 = jnp.float32
BF16 = jnp.bfloat16
LAST = (((1,), (1,)), ((), ()))
FIRST = (((0,), (0,)), ((), ()))
PARAMS = pltpu.CompilerParams(vmem_limit_bytes=48 << 20)
VMEM = pl.BlockSpec(memory_space=pltpu.VMEM)
SMEM = pl.BlockSpec(memory_space=pltpu.SMEM)


def shape(dims, kind=BF16):
    return jax.ShapeDtypeStruct(dims, kind)


def call(kernel, name, ins, outs, scratch=(), scalars=0, flops=0):
    cost = pl.CostEstimate(flops=flops, bytes_accessed=1 << 20, transcendentals=0) if flops else None
    return pl.pallas_call(
        kernel,
        in_specs=[SMEM] * scalars + [VMEM] * (len(ins) - scalars),
        out_shape=outs,
        scratch_shapes=list(scratch),
        compiler_params=PARAMS,
        cost_estimate=cost,
        name=name,
    )(*ins)


def by_parity(e, first, second, keep_ref, send_ref):
    @pl.when(e == 0)
    def _():
        keep_ref[...] = first
        send_ref[...] = second

    @pl.when(e == 1)
    def _():
        keep_ref[...] = second
        send_ref[...] = first


def pack_kernel(at_ref, all_ref, ids_ref, keep_ref, send_ref, dy_ref):
    ids = ids_ref[...].astype(BF16)
    zero = jnp.zeros((8, DH), BF16)
    heads = []
    for head in range(2):
        q, k, v = (all_ref[:, i * FEATS + head * DH : i * FEATS + (head + 1) * DH] for i in range(3))
        heads.append(jnp.concatenate([k, ids, v, zero, q, ids], axis=0))
    by_parity(at_ref[0], heads[0], heads[1], keep_ref, send_ref)
    dy_ref[...] = all_ref[:, 3 * FEATS : 3 * FEATS + WIDE]


def dattn_kernel(at_ref, *refs):
    dy_refs, (wo_ref, ids_ref, keep_ref, send_ref) = refs[0:4], refs[4:]
    acc = jnp.zeros((ROWS, FEATS), F32)
    for s, ref in enumerate(dy_refs):
        block = wo_ref[:, s * WIDE : (s + 1) * WIDE]
        acc = acc + lax.dot_general(ref[...], block, LAST, preferred_element_type=F32)
    ids = ids_ref[...].T
    real = jnp.concatenate([ids[:, 0:1], ids[0:8, 1:2]], axis=0) >= 0.0
    acc = jnp.where(real, acc, 0.0).astype(BF16)
    acc = jnp.concatenate([acc, jnp.zeros((PAD - ROWS, FEATS), BF16)], axis=0)
    by_parity(at_ref[0], acc[:, 0:DH], acc[:, DH:FEATS], keep_ref, send_ref)


def pairs_of(refs, slots, top):
    found = [None] * 4
    for i, slot in enumerate(slots):
        found[slot] = (refs[i // 2], top + i % 2 * PAIR)
    return found


def assemble(pairs, all_ref, base, cols):
    rest = base + QREST
    for j, (ref, at) in enumerate(pairs):
        for k in range(2):
            half = 2 * j + k
            top = at + k * PAD
            all_ref[base + half * FINE : base + (half + 1) * FINE, cols] = ref[top : top + FINE]
            all_ref[rest + half * REST : rest + (half + 1) * REST, cols] = ref[top + FINE : top + PAD]


def take_pair(value, j):
    pieces = []
    for half in (2 * j, 2 * j + 1):
        pieces.append(value[half * FINE : (half + 1) * FINE])
        pieces.append(value[QREST + half * REST : QREST + (half + 1) * REST])
    return jnp.concatenate(pieces, axis=0)


def masks(pairs, mask_ref, base, is_query):
    fine, last = [], []
    for ref, at in pairs:
        for k in range(2):
            rows = ref[at + k * PAD + FINE : at + (k + 1) * PAD].astype(F32)
            fine.append(rows[8:9])
            last.append(rows[9:10])
    fine = jnp.concatenate(fine, axis=0).T
    last = jnp.concatenate(last, axis=0).T
    rest = base + QREST

    def encode(column):
        lane = lax.broadcasted_iota(jnp.int32, (column.shape[0], DH), 1).astype(F32)
        if is_query:
            hidden = ((lane > column) & (lane < 13.0)) | (lane == 13.0)
            return jnp.where(hidden, BIG, 0.0).astype(BF16)
        return jnp.where(lane == jnp.where(column < 0.0, 13.0, column), 1.0, 0.0).astype(BF16)

    for half in range(2 * len(pairs)):
        mask_ref[base + half * FINE : base + (half + 1) * FINE] = encode(fine[:, half : half + 1])
        mask_ref[rest + half * REST : rest + (half + 1) * REST] = encode(last[0:REST, half : half + 1])


def in_three(row):
    high = row.astype(BF16).astype(F32)
    middle = (row - high).astype(BF16).astype(F32)
    return [high, middle, row - high - middle]


def forward_kernel(*refs):
    o_ref, stat_ref, q_ref, qm_ref, kv_ref, km_ref = refs[8:14]
    left, right = slice(0, DH), slice(DH, FEATS)
    queries = [(ref, 0) for ref in refs[0:4]]
    assemble(queries, q_ref, 0, left)
    masks(queries, qm_ref, 0, True)
    for base, parts in ((0, refs[4:6]), (NQ, refs[6:8])):
        keys = pairs_of(parts, (0, 1, 3, 2), 0)
        assemble(keys, kv_ref, base, left)
        assemble(pairs_of(parts, (0, 3, 1, 2), 2 * PAIR), kv_ref, base, right)
        masks(keys, km_ref, base, False)
    k_ext = jnp.concatenate([kv_ref[:, 0:DH], km_ref[...]], axis=1)
    lane = lax.broadcasted_iota(jnp.int32, (BLOCK, DH), 1)
    for block in range(NQ // BLOCK):
        rows = slice(block * BLOCK, (block + 1) * BLOCK)
        q_ext = jnp.concatenate([q_ref[rows], qm_ref[rows]], axis=1)
        s = lax.dot_general(q_ext, k_ext, LAST, preferred_element_type=F32)
        top = jnp.max(s, axis=1, keepdims=True)
        p = jnp.exp2((s - top) * UNIT)
        total = jnp.sum(p, axis=1, keepdims=True)
        o = jnp.dot(p.astype(BF16), kv_ref[:, DH:FEATS], preferred_element_type=F32) / total
        o_ref[rows] = o
        lse = top * UNIT + jnp.log2(total)
        stat_ref[:, rows] = jnp.where(lane == 0, lse, 0.0).T[0:8]


def share_kernel(*refs):
    o_ref, stat_ref, load_refs, da_ref, delta_ref = refs[4], refs[5], refs[6:10], refs[10], refs[11]
    assemble([(ref, 0) for ref in refs[0:4]], da_ref, 0, slice(0, DH))
    lane = lax.broadcasted_iota(jnp.int32, (BLOCK, DH), 1)
    for block in range(NQ // BLOCK):
        rows = slice(block * BLOCK, (block + 1) * BLOCK)
        share = jnp.sum(o_ref[rows] * da_ref[rows].astype(F32), axis=1, keepdims=True)
        delta_ref[:, rows] = jnp.where(lane == 0, share, 0.0).T[0:8]
    none = jnp.zeros((2, NQ), F32)
    sums = jnp.concatenate(in_three(stat_ref[0:1]) + in_three(delta_ref[0:1]) + [none], axis=0)
    tiles = [sums[:, i * DH : (i + 1) * DH] for i in range(NQ // DH)] + [jnp.zeros((8, DH), F32)]
    sums = jnp.concatenate(tiles, axis=0).astype(BF16)
    for j in range(4):
        load_refs[j][0:PAIR] = take_pair(o_ref, j).astype(BF16)
        load_refs[j][PAIR:LOAD] = sums


def row_sums(load_refs):
    lses, shares = [], []
    odd = lax.broadcasted_iota(jnp.int32, (8, DH), 1) % (4 * REST) >= 2 * REST
    for s, ref in enumerate(load_refs):
        sums = ref[PAIR:LOAD].astype(F32)
        tiles = [sums[8 * i : 8 * i + 8] for i in range(9)]
        last = tiles[8]
        if s % 2 == 1:
            last = jnp.where(odd, pltpu.roll(last, 2 * REST, 1), pltpu.roll(last, FINE - 2 * REST, 1))
        if s >= 2:
            last = pltpu.roll(last, FINE // 2, 1)
        rows = jnp.concatenate([tiles[2 * (j ^ s) + k] for j in range(4) for k in range(2)] + [last], axis=1)
        lses.append(rows[0:1] + rows[1:2] + rows[2:3])
        shares.append(rows[3:4] + rows[4:5] + rows[5:6])
    top = jnp.maximum(jnp.maximum(lses[0], lses[1]), jnp.maximum(lses[2], lses[3]))
    weights = [jnp.exp2(one - top) for one in lses]
    total = weights[0] + weights[1] + weights[2] + weights[3]
    delta = sum(weights[s] * shares[s] for s in range(4)) / total
    lse = top + jnp.log2(total)
    return jnp.where(lse < -1e28, 1e30, lse), delta


def backward_kernel(base, first, last, q_ref, qm_ref, da_ref, kv_ref, km_ref, *refs):
    rows_ref, refs = refs[0], refs[1:]
    if first > 0 or base == 0:
        dq_in_ref, refs = refs[0], refs[1:]
    if first > 0:
        rows_in_ref, refs = refs[0], refs[1:]
    out_refs, dkv_ref, ds_ref = refs[:-2], refs[-2], refs[-1]
    lse, delta = rows_ref[0:1], rows_ref[1:2]
    q = q_ref[...]
    da = da_ref[...]
    q_ext = jnp.concatenate([q, qm_ref[...]], axis=1)
    if first > 0:
        dkv_ref[0 : first * BLOCK] = rows_in_ref[...]
    for block in range(first, last):
        rows = slice(block * BLOCK, (block + 1) * BLOCK)
        keys = slice(base + block * BLOCK, base + (block + 1) * BLOCK)
        k_ext = jnp.concatenate([kv_ref[keys, 0:DH], km_ref[keys]], axis=1)
        s = lax.dot_general(k_ext, q_ext, LAST, preferred_element_type=F32)
        p = jnp.exp2(s * UNIT - lse)
        dp = lax.dot_general(kv_ref[keys, DH:FEATS], da, LAST, preferred_element_type=F32)
        ds = (p * (dp - delta)).astype(BF16)
        dkv_ref[rows, DH:FEATS] = jnp.dot(p.astype(BF16), da, preferred_element_type=F32).astype(BF16)
        dkv_ref[rows, 0:DH] = (jnp.dot(ds, q, preferred_element_type=F32) * SCALE).astype(BF16)
        ds_ref[rows] = ds
    if last * BLOCK < NQ:
        out_refs[0][...] = dkv_ref[0 : last * BLOCK]
    else:
        for j in range(4):
            pair = take_pair(dkv_ref, j)
            out_refs[0][j] = pair[:, 0:DH]
            out_refs[0][4 + j] = pair[:, DH:FEATS]
    rows = slice(first * BLOCK, last * BLOCK)
    keys = slice(base + rows.start, base + rows.stop)
    dq = lax.dot_general(ds_ref[rows], kv_ref[keys, 0:DH], FIRST, preferred_element_type=F32)
    if first > 0 or base == 0:
        dq = dq + dq_in_ref[...]
    if base > 0:
        out_refs[1][...] = dq
    else:
        dq = dq * SCALE
        for at, (mine, theirs) in enumerate(((0, 1), (3, 2))):
            out_refs[1][at * PAIR : (at + 1) * PAIR] = take_pair(dq, mine)
            out_refs[2][at * PAIR : (at + 1) * PAIR] = take_pair(dq, theirs).astype(BF16)


def merge_kernel(l0_ref, l1_ref, l2_ref, l3_ref, keep_ref, send_ref, rows_ref):
    load_refs = (l0_ref, l1_ref, l2_ref, l3_ref)
    lse, delta = row_sums(load_refs)
    rows_ref[0:1] = lse
    rows_ref[1:2] = delta
    fine, last = [], []
    for s, ref in enumerate(load_refs):
        sums = ref[PAIR:LOAD].astype(F32)
        rows = sums[0:72]
        lse = [rows[8 * i : 8 * i + 1] + rows[8 * i + 1 : 8 * i + 2] + rows[8 * i + 2 : 8 * i + 3] for i in (2 * s, 2 * s + 1, 8)]
        fine += lse[0:2]
        last.append(lse[2] if s == 0 else pltpu.roll(lse[2], FINE - 2 * REST * s, 1))
    fine = jnp.concatenate(fine, axis=0).T
    last = jnp.concatenate(last + last, axis=0).T
    for k, out_ref in ((0, keep_ref), (1, send_ref)):
        for rows, columns in (
            (slice(0, FINE), [fine[:, 2 * s + k : 2 * s + k + 1] for s in range(4)]),
            (slice(FINE, PAD), [last[k * REST : (k + 1) * REST, s : s + 1] for s in range(4)]),
        ):
            source = slice(k * PAD + rows.start, k * PAD + rows.stop)
            top = jnp.maximum(jnp.maximum(columns[0], columns[1]), jnp.maximum(columns[2], columns[3]))
            weights = [jnp.exp2(one - top) for one in columns]
            total = weights[0] + weights[1] + weights[2] + weights[3]
            acc = sum(weights[s] * load_refs[s][source].astype(F32) for s in range(4))
            out_ref[rows] = (acc * jnp.where(top < -1e28, 0.0, 1.0 / total)).astype(BF16)


def project_kernel(at_ref, mine_ref, other_ref, wo_ref, dy0_ref, dy1_ref, dy2_ref, dy3_ref, *refs):
    out_refs, keep_ref, send_ref, dwo_ref = refs[0:4], *refs[4:7]
    e, h, zr, x, c = (at_ref[i] for i in range(5))
    mine, other = mine_ref[...], other_ref[...]
    even = e == 0
    attn = jnp.concatenate([jnp.where(even, mine, other), jnp.where(even, other, mine)], axis=1)
    for s in range(NH):
        at = -s % NH * WIDE
        part = jnp.dot(attn, wo_ref[:, at : at + WIDE], preferred_element_type=F32)
        out_refs[s][...] = part[0:ROWS].astype(BF16)
    for s, ref in enumerate((dy0_ref, dy1_ref, dy2_ref, dy3_ref)):
        dwo_ref[s] = lax.dot_general(ref[...], attn[0:ROWS], FIRST, preferred_element_type=F32).astype(BF16)
    for ref, core in ((keep_ref, c), (send_ref, 1 - c)):
        for i, xt in enumerate((0, 1 + 2 * core, 3 - 2 * core, 2)):
            for et in range(2):
                for t in range(4):
                    s = lax.rem(h - jnp.bitwise_xor(zr, t) + NH, NH)
                    row = lax.rem(e + et, 2) * 256 + jnp.bitwise_xor(x, xt) * 64 + core * COLS
                    to = slice((et * 4 + t) * COLS, (et * 4 + t + 1) * COLS)
                    ref[i, to] = dwo_ref[s, pl.ds(pl.multiple_of(row, COLS), COLS)]


def split_up(total, mine, theirs, keep_ref, send_ref):
    rows = total.shape[1]
    for at in range(len(mine)):
        keep_ref[at * rows : (at + 1) * rows] = total[mine[at]]
        send_ref[at * rows : (at + 1) * rows] = total[theirs[at]].astype(BF16)


def core_kernel(keep_ref, got_ref, *refs):
    total = keep_ref[...].astype(F32) + got_ref[...].astype(F32)
    split_up(total[0:4], (0, 3), (1, 2), refs[0], refs[1])
    split_up(total[4:8], (0, 1), (3, 2), refs[2], refs[3])


def dwo_kernel(keep_ref, got_ref, mine_ref, send_ref):
    total = keep_ref[...].astype(F32) + got_ref[...].astype(F32)
    split_up(total, (0, 1), (2, 3), mine_ref, send_ref)


def middle_kernel(*refs):
    count = len(refs) // 4
    for i in range(count):
        keep_ref, got_ref = refs[2 * i : 2 * i + 2]
        mine_ref, send_ref = refs[2 * (count + i) : 2 * (count + i) + 2]
        rows = mine_ref.shape[0]
        total = keep_ref[...] + got_ref[...].astype(F32)
        mine_ref[...] = total[0:rows]
        send_ref[...] = total[rows : 2 * rows].astype(BF16)


def ring_kernel(mine_ref, got_ref, keep_ref, send_ref):
    total = mine_ref[...] + got_ref[...].astype(F32)
    for et in range(2):
        at = et * 4 * COLS
        to = et * 2 * COLS
        keep_ref[to : to + 2 * COLS] = total[at : at + 2 * COLS]
        send_ref[to : to + COLS] = total[at + 3 * COLS : at + 4 * COLS].astype(BF16)
        send_ref[to + COLS : to + 2 * COLS] = total[at + 2 * COLS : at + 3 * COLS].astype(BF16)


def half_kernel(keep_ref, got_ref, out_ref, send_ref):
    total = keep_ref[...] + got_ref[...].astype(F32)
    for et in range(2):
        out_ref[et * COLS : (et + 1) * COLS] = total[et * 2 * COLS : (et * 2 + 1) * COLS]
        send_ref[et * COLS : (et + 1) * COLS] = total[(et * 2 + 1) * COLS : (et * 2 + 2) * COLS].astype(BF16)


def total_kernel(*refs):
    wkeep_ref, wgot_ref, keep_ref, wmine_ref, send_ref = refs[6:11]
    for i in range(3):
        total = (refs[2 * i][...] + refs[2 * i + 1][...].astype(F32)).astype(BF16)
        keep_ref[:, i * DH : (i + 1) * DH] = total[0:PAD]
        send_ref[i * PAD : (i + 1) * PAD] = total[PAD:PAIR]
    weights = wkeep_ref[...] + wgot_ref[...].astype(F32)
    wmine_ref[...] = weights[0:COLS]
    piece = weights[COLS : 2 * COLS].astype(BF16)
    send_ref[3 * PAD : 3 * PAD + COLS] = piece[:, 0:DH]
    send_ref[3 * PAD + COLS : 3 * PAD + 2 * COLS] = piece[:, DH:FEATS]


def place_kernel(at_ref, mine_ref, wmine_ref, got_ref, dq_ref, dk_ref, dv_ref, dwo_ref):
    even = at_ref[0] == 0
    for i, ref in enumerate((dq_ref, dk_ref, dv_ref)):
        mine = mine_ref[0:ROWS, i * DH : (i + 1) * DH]
        other = got_ref[i * PAD : i * PAD + ROWS]
        ref[:, 0:DH] = jnp.where(even, mine, other)
        ref[:, DH:FEATS] = jnp.where(even, other, mine)
    got = got_ref[3 * PAD : 3 * PAD + 2 * COLS].astype(F32)
    dwo_ref[...] = wmine_ref[...] + jnp.concatenate([got[0:COLS], got[COLS : 2 * COLS]], axis=1)


def shifted(value, axis, size, by):
    return lax.ppermute(value, axis, [(i, (i + by) % size) for i in range(size)])


def swapped(value, axis, size, mask):
    return lax.ppermute(value, axis, [(i, i ^ mask) for i in range(size)])


def by_core(value, axis, flip):
    masks = (3, 1) if flip else (1, 3)
    return lax.ppermute(value, (axis, "c"), [(i, (i // 2 ^ masks[i % 2]) * 2 + i % 2) for i in range(8)])


def around(value, axis):
    return [value] + [shifted(value, axis, 4, s) for s in (1, 2, 3)]


def local(queries, key_rows, value_rows, scale_of, wo, dy):
    axes = ("e", "head", "zr", "x", "c")
    at = jnp.stack([lax.axis_index(name) for name in axes]).astype(jnp.int32)
    ids = jnp.pad(scale_of, (0, 8 * DH - ROWS), constant_values=-1).reshape(8, DH).astype(F32)
    pair = (PAIR, DH)

    keep, send, dy = call(
        pack_kernel,
        "pack",
        [at, jnp.concatenate([queries, key_rows, value_rows, dy], axis=1), ids],
        [shape((3 * PAD, DH))] * 2 + [shape((ROWS, WIDE))],
        scalars=1,
    )
    got = swapped(send, "e", 2, 1)
    dy, send = lax.optimization_barrier((dy, send))
    k, v, q = (jnp.concatenate([keep[i : i + PAD], got[i : i + PAD]], axis=0) for i in (0, PAD, 2 * PAD))
    k = jnp.concatenate([k, swapped(k, "zr", 4, 1)], axis=0)
    v = jnp.concatenate([v, swapped(v, "zr", 4, 3)], axis=0)
    dys = [dy, shifted(dy, "head", NH, 1), None, shifted(dy, "head", NH, 3)]
    dy_late, _ = lax.optimization_barrier((dy, got))
    dys[2] = shifted(dy_late, "head", NH, 2)
    q_one, q_three = swapped(q, "x", 4, 1), swapped(q, "x", 4, 3)
    k, v, dys = lax.optimization_barrier((k, v, dys))
    ks, vs = [k, swapped(k, "zr", 4, 3)], [v, swapped(v, "zr", 4, 1)]
    dys, q_one, q_three = lax.optimization_barrier((dys, q_one, q_three))
    wo, _ = lax.optimization_barrier((wo, dy))
    at_head = lax.axis_index("head")
    wo = jnp.concatenate(
        [lax.dynamic_slice_in_dim(wo, lax.rem(at_head - s + NH, NH) * WIDE, WIDE, 1) for s in range(NH)], axis=1
    )
    keep, send = call(dattn_kernel, "dattn", [at, *dys, wo, ids], [shape((PAD, DH))] * 2, scalars=1)
    q_late, send = lax.optimization_barrier((q, send))
    q_two = swapped(q_late, "x", 4, 2)
    da_got = swapped(send, "e", 2, 1)
    ks[1], vs[1], da_got, q_two = lax.optimization_barrier((ks[1], vs[1], da_got, q_two))
    qs = [q, q_one, q_two, q_three]
    da = jnp.concatenate([keep, da_got], axis=0)
    das = [da] + [swapped(da, "x", 4, s) for s in (1, 2, 3)]
    kvs = [jnp.concatenate([ks[i], vs[i]], axis=0) for i in range(2)]
    kvs = kvs + [swapped(one, "c", 2, 1) for one in kvs]

    rows = (NQ, DH)
    o, stat, q, qm, kv, km = call(
        forward_kernel,
        "forward",
        [*qs, *kvs],
        [shape(rows, F32), shape((8, NQ), F32), shape(rows), shape(rows), shape((NK, FEATS)), shape((NK, DH))],
        flops=6 * NQ * NK * DH,
    )
    *loads, da = call(
        share_kernel, "share", [*das, o, stat], [shape((LOAD, DH))] * 4 + [shape(rows)], [pltpu.VMEM((8, NQ), F32)]
    )
    loads = [loads[0]] + [swapped(loads[s], "x", 4, s) for s in (1, 2, 3)]

    keep, send, sums = call(merge_kernel, "merge", loads, [shape((PAD, DH))] * 2 + [shape((8, NQ), F32)])
    other = swapped(send, "e", 2, 1)
    q, send = lax.optimization_barrier((q, send))
    scratch = [pltpu.VMEM((NQ, FEATS), BF16), pltpu.VMEM((NQ, NQ), BF16)]
    sides = [q, qm, da, kv, km, sums]
    dkv_part, dq_part = call(
        functools.partial(backward_kernel, NQ, 0, 2),
        "backward_one",
        sides,
        [shape((2 * BLOCK, FEATS)), shape(rows, F32)],
        scratch,
        flops=4 * NQ * NK * DH,
    )
    other, dq_part = lax.optimization_barrier((other, dq_part))
    *outs, wkeep, wsend = call(
        project_kernel,
        "project",
        [at, keep, other, wo, *dys],
        [shape((ROWS, WIDE))] * 4 + [shape((4, 256, FEATS))] * 2,
        [pltpu.VMEM((4, WIDE, FEATS), BF16)],
        scalars=1,
    )
    wsend, dq_part = lax.optimization_barrier((wsend, dq_part))
    dkv_send, dq_part = call(
        functools.partial(backward_kernel, NQ, 2, 3),
        "backward_two",
        [*sides, dq_part, dkv_part],
        [shape((8, *pair)), shape(rows, F32)],
        scratch,
        flops=2 * NQ * NK * DH,
    )
    wgot, dq_part = lax.optimization_barrier((swapped(wsend, "c", 2, 1), dq_part))
    wkeep, wsend = call(
        dwo_kernel, "dwo", [wkeep, wgot], [shape((512, FEATS), F32), shape((512, FEATS))]
    )
    wsend, dq_part = lax.optimization_barrier((wsend, dq_part))
    twice = (2 * PAIR, DH)
    dkv_keep, dq_keep, dq_send = call(
        functools.partial(backward_kernel, 0, 0, 3),
        "backward_three",
        [*sides, dq_part],
        [shape((8, *pair)), shape(twice, F32), shape(twice)],
        scratch,
        flops=6 * NQ * NK * DH,
    )
    dk_keep, dk_send, dv_keep, dv_send = call(
        core_kernel, "core", [dkv_keep, swapped(dkv_send, "c", 2, 1)], [shape(twice, F32), shape(twice)] * 2
    )
    wgot, dk_send = lax.optimization_barrier((by_core(wsend, "x", 1), dk_send))
    wkeep, wsend = call(
        middle_kernel, "middle_dwo", [wkeep, wgot], [shape((256, FEATS), F32), shape((256, FEATS))]
    )
    wsend, outs[1], outs[3] = lax.optimization_barrier((wsend, outs[1], outs[3]))
    landed = [swapped(dk_send, "zr", 4, 1), swapped(dv_send, "zr", 4, 3), swapped(dq_send, "x", 4, 1)]
    landed += [by_core(wsend, "x", 0), shifted(outs[1], "head", NH, 1), shifted(outs[3], "head", NH, 3)]
    dk_got, dv_got, dq_got, wgot, out_one, out_three = lax.optimization_barrier(landed)
    wkeep, wsend = call(
        ring_kernel,
        "ring",
        [wkeep, wgot],
        [shape((128, FEATS), F32), shape((128, FEATS))],
    )
    dk, dk_send, dv, dv_send, dq, dq_send = call(
        middle_kernel,
        "middle",
        [dk_keep, dk_got, dv_keep, dv_got, dq_keep, dq_got],
        [shape(pair, F32), shape(pair)] * 3,
    )
    wgot, dq_got = swapped(wsend, "zr", 4, 3), swapped(dq_send, "x", 4, 3)
    dk_got, dv_got = swapped(dk_send, "zr", 4, 3), swapped(dv_send, "zr", 4, 1)
    wkeep, wsend = call(half_kernel, "half", [wkeep, wgot], [shape((64, FEATS), F32), shape((64, FEATS))])
    out_two = shifted(outs[2], "head", NH, 2)
    block_out = sum(one.astype(F32) for one in (outs[0], out_one, out_two, out_three)).astype(BF16)
    keep, wkeep, send = call(
        total_kernel,
        "total",
        [dq, dq_got, dk, dk_got, dv, dv_got]
        + [wkeep, swapped(wsend, "zr", 4, 1)],
        [shape((PAD, 3 * DH)), shape((COLS, FEATS), F32), shape((3 * PAD + 2 * COLS, DH))],
    )
    dq, dk, dv, dwo = call(
        place_kernel,
        "place",
        [at, keep, wkeep, swapped(send, "e", 2, 1)],
        [shape((ROWS, FEATS))] * 3 + [shape((COLS, FEATS), F32)],
        scalars=1,
    )
    return (block_out, dq, dk, dv, dwo.T)


def solution(mesh):
    fine = Mesh(mesh.devices.reshape(4, 2, 4, 2, NH), ("zr", "e", "x", "c", "head"))
    seq = ("zr", "e", "x", "c")
    placed = (
        P(seq, "head"),
        P(seq, "head"),
        P(seq, "head"),
        P(seq),
        P("head", None),
        P(seq, "head"),
    )
    return jax.shard_map(
        local,
        mesh=fine,
        in_specs=placed,
        out_specs=(
            P(seq, "head"),
            P(seq, "head"),
            P(seq, "head"),
            P(seq, "head"),
            P("head", seq),
        ),
        check_vma=False,
    )
```

```python
import functools
import math

import jax
import jax.numpy as jnp
from jax import lax
from jax.experimental import pallas as pl
from jax.experimental.pallas import tpu as pltpu
from jax.sharding import Mesh, PartitionSpec as P

DH = 128
ROWS = 136
PAD = 144
FINE = 128
REST = PAD - FINE
PAIR = 2 * PAD
NH = 4
QHALF = 8
NQ = QHALF * PAD
NK = 2 * NQ
QREST = QHALF * FINE
SUMS = 80
LOAD = PAIR + SUMS
FEATS = 2 * DH
MODEL = 2048
WIDE = MODEL // NH
COLS = 32
BLOCK = 384
BIG = -1e30
SCALE = DH ** (-0.5)
UNIT = SCALE * math.log2(math.e)
F32 = jnp.float32
BF16 = jnp.bfloat16
LAST = (((1,), (1,)), ((), ()))
FIRST = (((0,), (0,)), ((), ()))
PARAMS = pltpu.CompilerParams(vmem_limit_bytes=48 << 20)
VMEM = pl.BlockSpec(memory_space=pltpu.VMEM)
SMEM = pl.BlockSpec(memory_space=pltpu.SMEM)


def shape(dims, kind=BF16):
    return jax.ShapeDtypeStruct(dims, kind)


def call(kernel, name, ins, outs, scratch=(), scalars=0, flops=0):
    cost = pl.CostEstimate(flops=flops, bytes_accessed=1 << 20, transcendentals=0) if flops else None
    return pl.pallas_call(
        kernel,
        in_specs=[SMEM] * scalars + [VMEM] * (len(ins) - scalars),
        out_shape=outs,
        scratch_shapes=list(scratch),
        compiler_params=PARAMS,
        cost_estimate=cost,
        name=name,
    )(*ins)


def by_parity(e, first, second, keep_ref, send_ref):
    @pl.when(e == 0)
    def _():
        keep_ref[...] = first
        send_ref[...] = second

    @pl.when(e == 1)
    def _():
        keep_ref[...] = second
        send_ref[...] = first


def pack_kernel(at_ref, all_ref, ids_ref, keep_ref, send_ref, dy_ref):
    ids = ids_ref[...].astype(BF16)
    zero = jnp.zeros((8, DH), BF16)
    heads = []
    for head in range(2):
        q, k, v = (all_ref[:, i * FEATS + head * DH : i * FEATS + (head + 1) * DH] for i in range(3))
        heads.append(jnp.concatenate([k, ids, v, zero, q, ids], axis=0))
    by_parity(at_ref[0], heads[0], heads[1], keep_ref, send_ref)
    dy_ref[...] = all_ref[:, 3 * FEATS : 3 * FEATS + WIDE]


def dattn_kernel(at_ref, *refs):
    dy_refs, (wo_ref, ids_ref, keep_ref, send_ref) = refs[0:4], refs[4:]
    acc = jnp.zeros((ROWS, FEATS), F32)
    for s, ref in enumerate(dy_refs):
        block = wo_ref[:, s * WIDE : (s + 1) * WIDE]
        acc = acc + lax.dot_general(ref[...], block, LAST, preferred_element_type=F32)
    ids = ids_ref[...].T
    real = jnp.concatenate([ids[:, 0:1], ids[0:8, 1:2]], axis=0) >= 0.0
    acc = jnp.where(real, acc, 0.0).astype(BF16)
    acc = jnp.concatenate([acc, jnp.zeros((PAD - ROWS, FEATS), BF16)], axis=0)
    by_parity(at_ref[0], acc[:, 0:DH], acc[:, DH:FEATS], keep_ref, send_ref)


def pairs_of(refs, slots, top):
    found = [None] * 4
    for i, slot in enumerate(slots):
        found[slot] = (refs[i // 2], top + i % 2 * PAIR)
    return found


def assemble(pairs, all_ref, base, cols):
    rest = base + QREST
    for j, (ref, at) in enumerate(pairs):
        for k in range(2):
            half = 2 * j + k
            top = at + k * PAD
            all_ref[base + half * FINE : base + (half + 1) * FINE, cols] = ref[top : top + FINE]
            all_ref[rest + half * REST : rest + (half + 1) * REST, cols] = ref[top + FINE : top + PAD]


def take_pair(value, j):
    pieces = []
    for half in (2 * j, 2 * j + 1):
        pieces.append(value[half * FINE : (half + 1) * FINE])
        pieces.append(value[QREST + half * REST : QREST + (half + 1) * REST])
    return jnp.concatenate(pieces, axis=0)


def masks(pairs, mask_ref, base, is_query):
    fine, last = [], []
    for ref, at in pairs:
        for k in range(2):
            rows = ref[at + k * PAD + FINE : at + (k + 1) * PAD].astype(F32)
            fine.append(rows[8:9])
            last.append(rows[9:10])
    fine = jnp.concatenate(fine, axis=0).T
    last = jnp.concatenate(last, axis=0).T
    rest = base + QREST

    def encode(column):
        lane = lax.broadcasted_iota(jnp.int32, (column.shape[0], DH), 1).astype(F32)
        if is_query:
            hidden = ((lane > column) & (lane < 13.0)) | (lane == 13.0)
            return jnp.where(hidden, BIG, 0.0).astype(BF16)
        return jnp.where(lane == jnp.where(column < 0.0, 13.0, column), 1.0, 0.0).astype(BF16)

    for half in range(2 * len(pairs)):
        mask_ref[base + half * FINE : base + (half + 1) * FINE] = encode(fine[:, half : half + 1])
        mask_ref[rest + half * REST : rest + (half + 1) * REST] = encode(last[0:REST, half : half + 1])


def in_three(row):
    high = row.astype(BF16).astype(F32)
    middle = (row - high).astype(BF16).astype(F32)
    return [high, middle, row - high - middle]


def forward_kernel(*refs):
    o_ref, stat_ref, q_ref, qm_ref, kv_ref, km_ref = refs[6:12]
    left, right = slice(0, DH), slice(DH, FEATS)
    queries = pairs_of(refs[0:2], (0, 1, 3, 2), 0)
    assemble(queries, q_ref, 0, left)
    masks(queries, qm_ref, 0, True)
    for base, parts in ((0, refs[2:4]), (NQ, refs[4:6])):
        keys = pairs_of(parts, (0, 1, 3, 2), 0)
        assemble(keys, kv_ref, base, left)
        assemble(pairs_of(parts, (0, 3, 1, 2), 2 * PAIR), kv_ref, base, right)
        masks(keys, km_ref, base, False)
    k_ext = jnp.concatenate([kv_ref[:, 0:DH], km_ref[...]], axis=1)
    lane = lax.broadcasted_iota(jnp.int32, (BLOCK, DH), 1)
    for block in range(NQ // BLOCK):
        rows = slice(block * BLOCK, (block + 1) * BLOCK)
        q_ext = jnp.concatenate([q_ref[rows], qm_ref[rows]], axis=1)
        s = lax.dot_general(q_ext, k_ext, LAST, preferred_element_type=F32)
        top = jnp.max(s, axis=1, keepdims=True)
        p = jnp.exp2((s - top) * UNIT)
        total = jnp.sum(p, axis=1, keepdims=True)
        o = jnp.dot(p.astype(BF16), kv_ref[:, DH:FEATS], preferred_element_type=F32) / total
        o_ref[rows] = o
        lse = top * UNIT + jnp.log2(total)
        stat_ref[:, rows] = jnp.where(lane == 0, lse, 0.0).T[0:8]


def share_kernel(*refs):
    o_ref, stat_ref, load_refs, da_ref, delta_ref = refs[2], refs[3], refs[4:8], refs[8], refs[9]
    assemble(pairs_of(refs[0:2], (0, 3, 1, 2), 0), da_ref, 0, slice(0, DH))
    lane = lax.broadcasted_iota(jnp.int32, (BLOCK, DH), 1)
    for block in range(NQ // BLOCK):
        rows = slice(block * BLOCK, (block + 1) * BLOCK)
        share = jnp.sum(o_ref[rows] * da_ref[rows].astype(F32), axis=1, keepdims=True)
        delta_ref[:, rows] = jnp.where(lane == 0, share, 0.0).T[0:8]
    none = jnp.zeros((2, NQ), F32)
    sums = jnp.concatenate(in_three(stat_ref[0:1]) + in_three(delta_ref[0:1]) + [none], axis=0)
    tiles = [sums[:, i * DH : (i + 1) * DH] for i in range(NQ // DH)] + [jnp.zeros((8, DH), F32)]
    sums = jnp.concatenate(tiles, axis=0).astype(BF16)
    for j in range(4):
        load_refs[j][0:PAIR] = take_pair(o_ref, j).astype(BF16)
        load_refs[j][PAIR:LOAD] = sums


def row_sums(load_refs):
    lses, shares = [], []
    odd = lax.broadcasted_iota(jnp.int32, (8, DH), 1) % (4 * REST) >= 2 * REST
    for s, ref in enumerate(load_refs):
        sums = ref[PAIR:LOAD].astype(F32)
        tiles = [sums[8 * i : 8 * i + 8] for i in range(9)]
        last = tiles[8]
        if s % 2 == 1:
            last = jnp.where(odd, pltpu.roll(last, 2 * REST, 1), pltpu.roll(last, FINE - 2 * REST, 1))
        if s >= 2:
            last = pltpu.roll(last, FINE // 2, 1)
        rows = jnp.concatenate([tiles[2 * (j ^ s) + k] for j in range(4) for k in range(2)] + [last], axis=1)
        lses.append(rows[0:1] + rows[1:2] + rows[2:3])
        shares.append(rows[3:4] + rows[4:5] + rows[5:6])
    top = jnp.maximum(jnp.maximum(lses[0], lses[1]), jnp.maximum(lses[2], lses[3]))
    weights = [jnp.exp2(one - top) for one in lses]
    total = weights[0] + weights[1] + weights[2] + weights[3]
    delta = sum(weights[s] * shares[s] for s in range(4)) / total
    lse = top + jnp.log2(total)
    return jnp.where(lse < -1e28, 1e30, lse), delta


def backward_kernel(base, first, last, q_ref, qm_ref, da_ref, kv_ref, km_ref, *refs):
    rows_ref, refs = refs[0], refs[1:]
    if first > 0 or base == 0:
        dq_in_ref, refs = refs[0], refs[1:]
    if first > 0:
        rows_in_ref, refs = refs[0], refs[1:]
    out_refs, dkv_ref, ds_ref = refs[:-2], refs[-2], refs[-1]
    lse, delta = rows_ref[0:1], rows_ref[1:2]
    q = q_ref[...]
    da = da_ref[...]
    q_ext = jnp.concatenate([q, qm_ref[...]], axis=1)
    if first > 0:
        dkv_ref[0 : first * BLOCK] = rows_in_ref[...]
    for block in range(first, last):
        rows = slice(block * BLOCK, (block + 1) * BLOCK)
        keys = slice(base + block * BLOCK, base + (block + 1) * BLOCK)
        k_ext = jnp.concatenate([kv_ref[keys, 0:DH], km_ref[keys]], axis=1)
        s = lax.dot_general(k_ext, q_ext, LAST, preferred_element_type=F32)
        p = jnp.exp2(s * UNIT - lse)
        dp = lax.dot_general(kv_ref[keys, DH:FEATS], da, LAST, preferred_element_type=F32)
        ds = (p * (dp - delta)).astype(BF16)
        dkv_ref[rows, DH:FEATS] = jnp.dot(p.astype(BF16), da, preferred_element_type=F32).astype(BF16)
        dkv_ref[rows, 0:DH] = (jnp.dot(ds, q, preferred_element_type=F32) * SCALE).astype(BF16)
        ds_ref[rows] = ds
    if last * BLOCK < NQ:
        out_refs[0][...] = dkv_ref[0 : last * BLOCK]
    else:
        for j in range(4):
            pair = take_pair(dkv_ref, j)
            out_refs[0][j] = pair[:, 0:DH]
            out_refs[0][4 + j] = pair[:, DH:FEATS]
    rows = slice(first * BLOCK, last * BLOCK)
    keys = slice(base + rows.start, base + rows.stop)
    dq = lax.dot_general(ds_ref[rows], kv_ref[keys, 0:DH], FIRST, preferred_element_type=F32)
    if first > 0 or base == 0:
        dq = dq + dq_in_ref[...]
    if base > 0:
        out_refs[1][...] = dq
    else:
        dq = dq * SCALE
        for at, (mine, theirs) in enumerate(((0, 1), (3, 2))):
            out_refs[1][at * PAIR : (at + 1) * PAIR] = take_pair(dq, mine)
            out_refs[2][at * PAIR : (at + 1) * PAIR] = take_pair(dq, theirs).astype(BF16)


def merge_kernel(l0_ref, l1_ref, l2_ref, l3_ref, keep_ref, send_ref, rows_ref):
    load_refs = (l0_ref, l1_ref, l2_ref, l3_ref)
    lse, delta = row_sums(load_refs)
    rows_ref[0:1] = lse
    rows_ref[1:2] = delta
    fine, last = [], []
    for s, ref in enumerate(load_refs):
        sums = ref[PAIR:LOAD].astype(F32)
        rows = sums[0:72]
        lse = [rows[8 * i : 8 * i + 1] + rows[8 * i + 1 : 8 * i + 2] + rows[8 * i + 2 : 8 * i + 3] for i in (2 * s, 2 * s + 1, 8)]
        fine += lse[0:2]
        last.append(lse[2] if s == 0 else pltpu.roll(lse[2], FINE - 2 * REST * s, 1))
    fine = jnp.concatenate(fine, axis=0).T
    last = jnp.concatenate(last + last, axis=0).T
    for k, out_ref in ((0, keep_ref), (1, send_ref)):
        for rows, columns in (
            (slice(0, FINE), [fine[:, 2 * s + k : 2 * s + k + 1] for s in range(4)]),
            (slice(FINE, PAD), [last[k * REST : (k + 1) * REST, s : s + 1] for s in range(4)]),
        ):
            source = slice(k * PAD + rows.start, k * PAD + rows.stop)
            top = jnp.maximum(jnp.maximum(columns[0], columns[1]), jnp.maximum(columns[2], columns[3]))
            weights = [jnp.exp2(one - top) for one in columns]
            total = weights[0] + weights[1] + weights[2] + weights[3]
            acc = sum(weights[s] * load_refs[s][source].astype(F32) for s in range(4))
            out_ref[rows] = (acc * jnp.where(top < -1e28, 0.0, 1.0 / total)).astype(BF16)


def project_kernel(at_ref, mine_ref, other_ref, wo_ref, dy0_ref, dy1_ref, dy2_ref, dy3_ref, *refs):
    out_refs, keep_ref, send_ref, dwo_ref = refs[0:4], *refs[4:7]
    e, h, zr, x, c = (at_ref[i] for i in range(5))
    mine, other = mine_ref[...], other_ref[...]
    even = e == 0
    attn = jnp.concatenate([jnp.where(even, mine, other), jnp.where(even, other, mine)], axis=1)
    for s in range(NH):
        at = -s % NH * WIDE
        part = jnp.dot(attn, wo_ref[:, at : at + WIDE], preferred_element_type=F32)
        out_refs[s][...] = part[0:ROWS].astype(BF16)
    for s, ref in enumerate((dy0_ref, dy1_ref, dy2_ref, dy3_ref)):
        dwo_ref[s] = lax.dot_general(ref[...], attn[0:ROWS], FIRST, preferred_element_type=F32).astype(BF16)
    for ref, core in ((keep_ref, c), (send_ref, 1 - c)):
        for i, xt in enumerate((0, 1 + 2 * core, 3 - 2 * core, 2)):
            for et in range(2):
                for t in range(4):
                    s = lax.rem(h - jnp.bitwise_xor(zr, t) + NH, NH)
                    row = lax.rem(e + et, 2) * 256 + jnp.bitwise_xor(x, xt) * 64 + core * COLS
                    to = slice((et * 4 + t) * COLS, (et * 4 + t + 1) * COLS)
                    ref[i, to] = dwo_ref[s, pl.ds(pl.multiple_of(row, COLS), COLS)]


def split_up(total, mine, theirs, keep_ref, send_ref):
    rows = total.shape[1]
    for at in range(len(mine)):
        keep_ref[at * rows : (at + 1) * rows] = total[mine[at]]
        send_ref[at * rows : (at + 1) * rows] = total[theirs[at]].astype(BF16)


def core_kernel(keep_ref, got_ref, *refs):
    total = keep_ref[...].astype(F32) + got_ref[...].astype(F32)
    split_up(total[0:4], (0, 3), (1, 2), refs[0], refs[1])
    split_up(total[4:8], (0, 1), (3, 2), refs[2], refs[3])


def dwo_kernel(keep_ref, got_ref, mine_ref, send_ref):
    total = keep_ref[...].astype(F32) + got_ref[...].astype(F32)
    split_up(total, (0, 1), (2, 3), mine_ref, send_ref)


def middle_kernel(*refs):
    count = len(refs) // 4
    for i in range(count):
        keep_ref, got_ref = refs[2 * i : 2 * i + 2]
        mine_ref, send_ref = refs[2 * (count + i) : 2 * (count + i) + 2]
        rows = mine_ref.shape[0]
        total = keep_ref[...] + got_ref[...].astype(F32)
        mine_ref[...] = total[0:rows]
        send_ref[...] = total[rows : 2 * rows].astype(BF16)


def ring_kernel(mine_ref, got_ref, keep_ref, send_ref):
    total = mine_ref[...] + got_ref[...].astype(F32)
    for et in range(2):
        at = et * 4 * COLS
        to = et * 2 * COLS
        keep_ref[to : to + 2 * COLS] = total[at : at + 2 * COLS]
        send_ref[to : to + COLS] = total[at + 3 * COLS : at + 4 * COLS].astype(BF16)
        send_ref[to + COLS : to + 2 * COLS] = total[at + 2 * COLS : at + 3 * COLS].astype(BF16)


def half_kernel(keep_ref, got_ref, out_ref, send_ref):
    total = keep_ref[...] + got_ref[...].astype(F32)
    for et in range(2):
        out_ref[et * COLS : (et + 1) * COLS] = total[et * 2 * COLS : (et * 2 + 1) * COLS]
        send_ref[et * COLS : (et + 1) * COLS] = total[(et * 2 + 1) * COLS : (et * 2 + 2) * COLS].astype(BF16)


def total_kernel(*refs):
    wkeep_ref, wgot_ref, keep_ref, wmine_ref, send_ref = refs[6:11]
    for i in range(3):
        total = (refs[2 * i][...] + refs[2 * i + 1][...].astype(F32)).astype(BF16)
        keep_ref[:, i * DH : (i + 1) * DH] = total[0:PAD]
        send_ref[i * PAD : (i + 1) * PAD] = total[PAD:PAIR]
    weights = wkeep_ref[...] + wgot_ref[...].astype(F32)
    wmine_ref[...] = weights[0:COLS]
    piece = weights[COLS : 2 * COLS].astype(BF16)
    send_ref[3 * PAD : 3 * PAD + COLS] = piece[:, 0:DH]
    send_ref[3 * PAD + COLS : 3 * PAD + 2 * COLS] = piece[:, DH:FEATS]


def place_kernel(at_ref, mine_ref, wmine_ref, got_ref, dq_ref, dk_ref, dv_ref, dwo_ref):
    even = at_ref[0] == 0
    for i, ref in enumerate((dq_ref, dk_ref, dv_ref)):
        mine = mine_ref[0:ROWS, i * DH : (i + 1) * DH]
        other = got_ref[i * PAD : i * PAD + ROWS]
        ref[:, 0:DH] = jnp.where(even, mine, other)
        ref[:, DH:FEATS] = jnp.where(even, other, mine)
    got = got_ref[3 * PAD : 3 * PAD + 2 * COLS].astype(F32)
    dwo_ref[...] = wmine_ref[...] + jnp.concatenate([got[0:COLS], got[COLS : 2 * COLS]], axis=1)


def shifted(value, axis, size, by):
    return lax.ppermute(value, axis, [(i, (i + by) % size) for i in range(size)])


def swapped(value, axis, size, mask):
    return lax.ppermute(value, axis, [(i, i ^ mask) for i in range(size)])


def by_core(value, axis, flip):
    masks = (3, 1) if flip else (1, 3)
    return lax.ppermute(value, (axis, "c"), [(i, (i // 2 ^ masks[i % 2]) * 2 + i % 2) for i in range(8)])


def around(value, axis):
    return [value] + [shifted(value, axis, 4, s) for s in (1, 2, 3)]


def local(queries, key_rows, value_rows, scale_of, wo, dy):
    axes = ("e", "head", "zr", "x", "c")
    at = jnp.stack([lax.axis_index(name) for name in axes]).astype(jnp.int32)
    ids = jnp.pad(scale_of, (0, 8 * DH - ROWS), constant_values=-1).reshape(8, DH).astype(F32)
    pair = (PAIR, DH)

    keep, send, dy = call(
        pack_kernel,
        "pack",
        [at, jnp.concatenate([queries, key_rows, value_rows, dy], axis=1), ids],
        [shape((3 * PAD, DH))] * 2 + [shape((ROWS, WIDE))],
        scalars=1,
    )
    got = swapped(send, "e", 2, 1)
    dy, send = lax.optimization_barrier((dy, send))
    k, v, q = (jnp.concatenate([keep[i : i + PAD], got[i : i + PAD]], axis=0) for i in (0, PAD, 2 * PAD))
    k_got, v_got = lax.optimization_barrier((swapped(k, "zr", 4, 1), swapped(v, "zr", 4, 3)))
    k, v = jnp.concatenate([k, k_got], axis=0), jnp.concatenate([v, v_got], axis=0)
    dys = [dy, shifted(dy, "head", NH, 1), None, shifted(dy, "head", NH, 3)]
    dy_late, _ = lax.optimization_barrier((dy, got))
    dys[2] = shifted(dy_late, "head", NH, 2)
    q_got = swapped(q, "x", 4, 1)
    _, _, dys, q_got = lax.optimization_barrier((k, v, dys, q_got))
    ks, vs = [k, swapped(k, "zr", 4, 3)], [v, swapped(v, "zr", 4, 1)]
    wo, _ = lax.optimization_barrier((wo, dy))
    at_head = lax.axis_index("head")
    wo = jnp.concatenate(
        [lax.dynamic_slice_in_dim(wo, lax.rem(at_head - s + NH, NH) * WIDE, WIDE, 1) for s in range(NH)], axis=1
    )
    keep, send = call(dattn_kernel, "dattn", [at, *dys, wo, ids], [shape((PAD, DH))] * 2, scalars=1)
    q, send = lax.optimization_barrier((jnp.concatenate([q, q_got], axis=0), send))
    qs = [q, swapped(q, "x", 4, 3)]
    da_got = swapped(send, "e", 2, 1)
    da = jnp.concatenate([keep, da_got], axis=0)
    late = [ks[1], vs[1], swapped(da, "x", 4, 3), qs[1]]
    ks[1], vs[1], da_got, qs[1] = lax.optimization_barrier(late)
    da = jnp.concatenate([da, da_got], axis=0)
    das = [da, swapped(da, "x", 4, 1)]
    kvs = [jnp.concatenate([ks[i], vs[i]], axis=0) for i in range(2)]
    kvs = kvs + [swapped(one, "c", 2, 1) for one in kvs]

    rows = (NQ, DH)
    o, stat, q, qm, kv, km = call(
        forward_kernel,
        "forward",
        [*qs, *kvs],
        [shape(rows, F32), shape((8, NQ), F32), shape(rows), shape(rows), shape((NK, FEATS)), shape((NK, DH))],
        flops=6 * NQ * NK * DH,
    )
    *loads, da = call(
        share_kernel, "share", [*das, o, stat], [shape((LOAD, DH))] * 4 + [shape(rows)], [pltpu.VMEM((8, NQ), F32)]
    )
    loads = [loads[0]] + [swapped(loads[s], "x", 4, s) for s in (1, 2, 3)]

    keep, send, sums = call(merge_kernel, "merge", loads, [shape((PAD, DH))] * 2 + [shape((8, NQ), F32)])
    other = swapped(send, "e", 2, 1)
    q, send = lax.optimization_barrier((q, send))
    scratch = [pltpu.VMEM((NQ, FEATS), BF16), pltpu.VMEM((NQ, NQ), BF16)]
    sides = [q, qm, da, kv, km, sums]
    dkv_part, dq_part = call(
        functools.partial(backward_kernel, NQ, 0, 2),
        "backward_one",
        sides,
        [shape((2 * BLOCK, FEATS)), shape(rows, F32)],
        scratch,
        flops=4 * NQ * NK * DH,
    )
    other, dq_part = lax.optimization_barrier((other, dq_part))
    *outs, wkeep, wsend = call(
        project_kernel,
        "project",
        [at, keep, other, wo, *dys],
        [shape((ROWS, WIDE))] * 4 + [shape((4, 256, FEATS))] * 2,
        [pltpu.VMEM((4, WIDE, FEATS), BF16)],
        scalars=1,
    )
    wsend, dq_part = lax.optimization_barrier((wsend, dq_part))
    dkv_send, dq_part = call(
        functools.partial(backward_kernel, NQ, 2, 3),
        "backward_two",
        [*sides, dq_part, dkv_part],
        [shape((8, *pair)), shape(rows, F32)],
        scratch,
        flops=2 * NQ * NK * DH,
    )
    wgot, dq_part = lax.optimization_barrier((swapped(wsend, "c", 2, 1), dq_part))
    wkeep, wsend = call(
        dwo_kernel, "dwo", [wkeep, wgot], [shape((512, FEATS), F32), shape((512, FEATS))]
    )
    wsend, dq_part = lax.optimization_barrier((wsend, dq_part))
    twice = (2 * PAIR, DH)
    dkv_keep, dq_keep, dq_send = call(
        functools.partial(backward_kernel, 0, 0, 3),
        "backward_three",
        [*sides, dq_part],
        [shape((8, *pair)), shape(twice, F32), shape(twice)],
        scratch,
        flops=6 * NQ * NK * DH,
    )
    dk_keep, dk_send, dv_keep, dv_send = call(
        core_kernel, "core", [dkv_keep, swapped(dkv_send, "c", 2, 1)], [shape(twice, F32), shape(twice)] * 2
    )
    wgot, dk_send = lax.optimization_barrier((by_core(wsend, "x", 1), dk_send))
    wkeep, wsend = call(
        middle_kernel, "middle_dwo", [wkeep, wgot], [shape((256, FEATS), F32), shape((256, FEATS))]
    )
    wsend, outs[1], outs[3] = lax.optimization_barrier((wsend, outs[1], outs[3]))
    landed = [swapped(dk_send, "zr", 4, 1), swapped(dv_send, "zr", 4, 3), swapped(dq_send, "x", 4, 1)]
    landed += [by_core(wsend, "x", 0), shifted(outs[1], "head", NH, 1), shifted(outs[3], "head", NH, 3)]
    dk_got, dv_got, dq_got, wgot, out_one, out_three = lax.optimization_barrier(landed)
    wkeep, wsend = call(
        ring_kernel,
        "ring",
        [wkeep, wgot],
        [shape((128, FEATS), F32), shape((128, FEATS))],
    )
    dk, dk_send, dv, dv_send, dq, dq_send = call(
        middle_kernel,
        "middle",
        [dk_keep, dk_got, dv_keep, dv_got, dq_keep, dq_got],
        [shape(pair, F32), shape(pair)] * 3,
    )
    wgot, dq_got = swapped(wsend, "zr", 4, 3), swapped(dq_send, "x", 4, 3)
    dk_got, dv_got = swapped(dk_send, "zr", 4, 3), swapped(dv_send, "zr", 4, 1)
    wkeep, wsend = call(half_kernel, "half", [wkeep, wgot], [shape((64, FEATS), F32), shape((64, FEATS))])
    out_two = shifted(outs[2], "head", NH, 2)
    block_out = sum(one.astype(F32) for one in (outs[0], out_one, out_two, out_three)).astype(BF16)
    keep, wkeep, send = call(
        total_kernel,
        "total",
        [dq, dq_got, dk, dk_got, dv, dv_got]
        + [wkeep, swapped(wsend, "zr", 4, 1)],
        [shape((PAD, 3 * DH)), shape((COLS, FEATS), F32), shape((3 * PAD + 2 * COLS, DH))],
    )
    dq, dk, dv, dwo = call(
        place_kernel,
        "place",
        [at, keep, wkeep, swapped(send, "e", 2, 1)],
        [shape((ROWS, FEATS))] * 3 + [shape((COLS, FEATS), F32)],
        scalars=1,
    )
    return (block_out, dq, dk, dv, dwo.T)


def solution(mesh):
    fine = Mesh(mesh.devices.reshape(4, 2, 4, 2, NH), ("zr", "e", "x", "c", "head"))
    seq = ("zr", "e", "x", "c")
    placed = (
        P(seq, "head"),
        P(seq, "head"),
        P(seq, "head"),
        P(seq),
        P("head", None),
        P(seq, "head"),
    )
    return jax.shard_map(
        local,
        mesh=fine,
        in_specs=placed,
        out_specs=(
            P(seq, "head"),
            P(seq, "head"),
            P(seq, "head"),
            P(seq, "head"),
            P("head", seq),
        ),
        check_vma=False,
    )
```

```python
import functools
import math

import jax
import jax.numpy as jnp
from jax import lax
from jax.experimental import pallas as pl
from jax.experimental.pallas import tpu as pltpu
from jax.sharding import Mesh, PartitionSpec as P

DH = 128
ROWS = 136
PAD = 144
FINE = 128
REST = PAD - FINE
PAIR = 2 * PAD
NH = 4
QHALF = 8
NQ = QHALF * PAD
NK = 2 * NQ
QREST = QHALF * FINE
SUMS = 80
LOAD = PAIR + SUMS
FEATS = 2 * DH
MODEL = 2048
WIDE = MODEL // NH
COLS = 32
BLOCK = 384
BIG = -1e30
SCALE = DH ** (-0.5)
UNIT = SCALE * math.log2(math.e)
F32 = jnp.float32
BF16 = jnp.bfloat16
LAST = (((1,), (1,)), ((), ()))
FIRST = (((0,), (0,)), ((), ()))
PARAMS = pltpu.CompilerParams(vmem_limit_bytes=48 << 20)
VMEM = pl.BlockSpec(memory_space=pltpu.VMEM)
SMEM = pl.BlockSpec(memory_space=pltpu.SMEM)


def shape(dims, kind=BF16):
    return jax.ShapeDtypeStruct(dims, kind)


def call(kernel, name, ins, outs, scratch=(), scalars=0, flops=0):
    cost = pl.CostEstimate(flops=flops, bytes_accessed=1 << 20, transcendentals=0) if flops else None
    return pl.pallas_call(
        kernel,
        in_specs=[SMEM] * scalars + [VMEM] * (len(ins) - scalars),
        out_shape=outs,
        scratch_shapes=list(scratch),
        compiler_params=PARAMS,
        cost_estimate=cost,
        name=name,
    )(*ins)


def by_parity(e, first, second, keep_ref, send_ref):
    @pl.when(e == 0)
    def _():
        keep_ref[...] = first
        send_ref[...] = second

    @pl.when(e == 1)
    def _():
        keep_ref[...] = second
        send_ref[...] = first


def pack_kernel(at_ref, all_ref, ids_ref, keep_ref, send_ref, dy_ref):
    ids = ids_ref[...].astype(BF16)
    zero = jnp.zeros((8, DH), BF16)
    heads = []
    for head in range(2):
        q, k, v = (all_ref[:, i * FEATS + head * DH : i * FEATS + (head + 1) * DH] for i in range(3))
        heads.append(jnp.concatenate([k, ids, v, zero, q, ids], axis=0))
    by_parity(at_ref[0], heads[0], heads[1], keep_ref, send_ref)
    dy_ref[...] = all_ref[:, 3 * FEATS : 3 * FEATS + WIDE]


def dattn_kernel(at_ref, *refs):
    dy_refs, (wo_ref, ids_ref, keep_ref, send_ref) = refs[0:4], refs[4:]
    acc = jnp.zeros((ROWS, FEATS), F32)
    for s, ref in enumerate(dy_refs):
        block = wo_ref[:, s * WIDE : (s + 1) * WIDE]
        acc = acc + lax.dot_general(ref[...], block, LAST, preferred_element_type=F32)
    ids = ids_ref[...].T
    real = jnp.concatenate([ids[:, 0:1], ids[0:8, 1:2]], axis=0) >= 0.0
    acc = jnp.where(real, acc, 0.0).astype(BF16)
    acc = jnp.concatenate([acc, jnp.zeros((PAD - ROWS, FEATS), BF16)], axis=0)
    by_parity(at_ref[0], acc[:, 0:DH], acc[:, DH:FEATS], keep_ref, send_ref)


def pairs_of(refs, slots, top):
    found = [None] * 4
    for i, slot in enumerate(slots):
        found[slot] = (refs[i // 2], top + i % 2 * PAIR)
    return found


def assemble(pairs, all_ref, base, cols):
    rest = base + QREST
    for j, (ref, at) in enumerate(pairs):
        for k in range(2):
            half = 2 * j + k
            top = at + k * PAD
            all_ref[base + half * FINE : base + (half + 1) * FINE, cols] = ref[top : top + FINE]
            all_ref[rest + half * REST : rest + (half + 1) * REST, cols] = ref[top + FINE : top + PAD]


def take_pair(value, j):
    pieces = []
    for half in (2 * j, 2 * j + 1):
        pieces.append(value[half * FINE : (half + 1) * FINE])
        pieces.append(value[QREST + half * REST : QREST + (half + 1) * REST])
    return jnp.concatenate(pieces, axis=0)


def masks(pairs, mask_ref, base, is_query):
    fine, last = [], []
    for ref, at in pairs:
        for k in range(2):
            rows = ref[at + k * PAD + FINE : at + (k + 1) * PAD].astype(F32)
            fine.append(rows[8:9])
            last.append(rows[9:10])
    fine = jnp.concatenate(fine, axis=0).T
    last = jnp.concatenate(last, axis=0).T
    rest = base + QREST

    def encode(column):
        lane = lax.broadcasted_iota(jnp.int32, (column.shape[0], DH), 1).astype(F32)
        if is_query:
            hidden = ((lane > column) & (lane < 13.0)) | (lane == 13.0)
            return jnp.where(hidden, BIG, 0.0).astype(BF16)
        return jnp.where(lane == jnp.where(column < 0.0, 13.0, column), 1.0, 0.0).astype(BF16)

    for half in range(2 * len(pairs)):
        mask_ref[base + half * FINE : base + (half + 1) * FINE] = encode(fine[:, half : half + 1])
        mask_ref[rest + half * REST : rest + (half + 1) * REST] = encode(last[0:REST, half : half + 1])


def in_three(row):
    high = row.astype(BF16).astype(F32)
    middle = (row - high).astype(BF16).astype(F32)
    return [high, middle, row - high - middle]


def forward_kernel(*refs):
    o_ref, stat_ref, q_ref, qm_ref, kv_ref, km_ref = refs[6:12]
    left, right = slice(0, DH), slice(DH, FEATS)
    queries = pairs_of(refs[0:2], (0, 1, 3, 2), 0)
    assemble(queries, q_ref, 0, left)
    masks(queries, qm_ref, 0, True)
    for base, parts in ((0, refs[2:4]), (NQ, refs[4:6])):
        keys = pairs_of(parts, (0, 1, 3, 2), 0)
        assemble(keys, kv_ref, base, left)
        assemble(pairs_of(parts, (0, 3, 1, 2), 2 * PAIR), kv_ref, base, right)
        masks(keys, km_ref, base, False)
    k_ext = jnp.concatenate([kv_ref[:, 0:DH], km_ref[...]], axis=1)
    lane = lax.broadcasted_iota(jnp.int32, (BLOCK, DH), 1)
    for block in range(NQ // BLOCK):
        rows = slice(block * BLOCK, (block + 1) * BLOCK)
        q_ext = jnp.concatenate([q_ref[rows], qm_ref[rows]], axis=1)
        s = lax.dot_general(q_ext, k_ext, LAST, preferred_element_type=F32)
        top = jnp.max(s, axis=1, keepdims=True)
        p = jnp.exp2((s - top) * UNIT)
        total = jnp.sum(p, axis=1, keepdims=True)
        o = jnp.dot(p.astype(BF16), kv_ref[:, DH:FEATS], preferred_element_type=F32) / total
        o_ref[rows] = o
        lse = top * UNIT + jnp.log2(total)
        stat_ref[:, rows] = jnp.where(lane == 0, lse, 0.0).T[0:8]


def share_kernel(*refs):
    o_ref, stat_ref, load_refs, da_ref, delta_ref = refs[4], refs[5], refs[6:10], refs[10], refs[11]
    assemble([(ref, 0) for ref in refs[0:4]], da_ref, 0, slice(0, DH))
    lane = lax.broadcasted_iota(jnp.int32, (BLOCK, DH), 1)
    for block in range(NQ // BLOCK):
        rows = slice(block * BLOCK, (block + 1) * BLOCK)
        share = jnp.sum(o_ref[rows] * da_ref[rows].astype(F32), axis=1, keepdims=True)
        delta_ref[:, rows] = jnp.where(lane == 0, share, 0.0).T[0:8]
    none = jnp.zeros((2, NQ), F32)
    sums = jnp.concatenate(in_three(stat_ref[0:1]) + in_three(delta_ref[0:1]) + [none], axis=0)
    tiles = [sums[:, i * DH : (i + 1) * DH] for i in range(NQ // DH)] + [jnp.zeros((8, DH), F32)]
    sums = jnp.concatenate(tiles, axis=0).astype(BF16)
    for j in range(4):
        load_refs[j][0:PAIR] = take_pair(o_ref, j).astype(BF16)
        load_refs[j][PAIR:LOAD] = sums


def row_sums(load_refs):
    lses, shares = [], []
    odd = lax.broadcasted_iota(jnp.int32, (8, DH), 1) % (4 * REST) >= 2 * REST
    for s, ref in enumerate(load_refs):
        sums = ref[PAIR:LOAD].astype(F32)
        tiles = [sums[8 * i : 8 * i + 8] for i in range(9)]
        last = tiles[8]
        if s % 2 == 1:
            last = jnp.where(odd, pltpu.roll(last, 2 * REST, 1), pltpu.roll(last, FINE - 2 * REST, 1))
        if s >= 2:
            last = pltpu.roll(last, FINE // 2, 1)
        rows = jnp.concatenate([tiles[2 * (j ^ s) + k] for j in range(4) for k in range(2)] + [last], axis=1)
        lses.append(rows[0:1] + rows[1:2] + rows[2:3])
        shares.append(rows[3:4] + rows[4:5] + rows[5:6])
    top = jnp.maximum(jnp.maximum(lses[0], lses[1]), jnp.maximum(lses[2], lses[3]))
    weights = [jnp.exp2(one - top) for one in lses]
    total = weights[0] + weights[1] + weights[2] + weights[3]
    delta = sum(weights[s] * shares[s] for s in range(4)) / total
    lse = top + jnp.log2(total)
    return jnp.where(lse < -1e28, 1e30, lse), delta


def backward_kernel(base, first, last, q_ref, qm_ref, da_ref, kv_ref, km_ref, *refs):
    rows_ref, refs = refs[0], refs[1:]
    if first > 0 or base == 0:
        dq_in_ref, refs = refs[0], refs[1:]
    if first > 0:
        rows_in_ref, refs = refs[0], refs[1:]
    out_refs, dkv_ref, ds_ref = refs[:-2], refs[-2], refs[-1]
    lse, delta = rows_ref[0:1], rows_ref[1:2]
    q = q_ref[...]
    da = da_ref[...]
    q_ext = jnp.concatenate([q, qm_ref[...]], axis=1)
    if first > 0:
        dkv_ref[0 : first * BLOCK] = rows_in_ref[...]
    for block in range(first, last):
        rows = slice(block * BLOCK, (block + 1) * BLOCK)
        keys = slice(base + block * BLOCK, base + (block + 1) * BLOCK)
        k_ext = jnp.concatenate([kv_ref[keys, 0:DH], km_ref[keys]], axis=1)
        s = lax.dot_general(k_ext, q_ext, LAST, preferred_element_type=F32)
        p = jnp.exp2(s * UNIT - lse)
        dp = lax.dot_general(kv_ref[keys, DH:FEATS], da, LAST, preferred_element_type=F32)
        ds = (p * (dp - delta)).astype(BF16)
        dkv_ref[rows, DH:FEATS] = jnp.dot(p.astype(BF16), da, preferred_element_type=F32).astype(BF16)
        dkv_ref[rows, 0:DH] = (jnp.dot(ds, q, preferred_element_type=F32) * SCALE).astype(BF16)
        ds_ref[rows] = ds
    if last * BLOCK < NQ:
        out_refs[0][...] = dkv_ref[0 : last * BLOCK]
    else:
        for j in range(4):
            pair = take_pair(dkv_ref, j)
            out_refs[0][j] = pair[:, 0:DH]
            out_refs[0][4 + j] = pair[:, DH:FEATS]
    rows = slice(first * BLOCK, last * BLOCK)
    keys = slice(base + rows.start, base + rows.stop)
    dq = lax.dot_general(ds_ref[rows], kv_ref[keys, 0:DH], FIRST, preferred_element_type=F32)
    if first > 0 or base == 0:
        dq = dq + dq_in_ref[...]
    if base > 0:
        out_refs[1][...] = dq
    else:
        dq = dq * SCALE
        for at, (mine, theirs) in enumerate(((0, 1), (3, 2))):
            out_refs[1][at * PAIR : (at + 1) * PAIR] = take_pair(dq, mine)
            out_refs[2][at * PAIR : (at + 1) * PAIR] = take_pair(dq, theirs).astype(BF16)


def merge_kernel(l0_ref, l1_ref, l2_ref, l3_ref, keep_ref, send_ref, rows_ref):
    load_refs = (l0_ref, l1_ref, l2_ref, l3_ref)
    lse, delta = row_sums(load_refs)
    rows_ref[0:1] = lse
    rows_ref[1:2] = delta
    fine, last = [], []
    for s, ref in enumerate(load_refs):
        sums = ref[PAIR:LOAD].astype(F32)
        rows = sums[0:72]
        lse = [rows[8 * i : 8 * i + 1] + rows[8 * i + 1 : 8 * i + 2] + rows[8 * i + 2 : 8 * i + 3] for i in (2 * s, 2 * s + 1, 8)]
        fine += lse[0:2]
        last.append(lse[2] if s == 0 else pltpu.roll(lse[2], FINE - 2 * REST * s, 1))
    fine = jnp.concatenate(fine, axis=0).T
    last = jnp.concatenate(last + last, axis=0).T
    for k, out_ref in ((0, keep_ref), (1, send_ref)):
        for rows, columns in (
            (slice(0, FINE), [fine[:, 2 * s + k : 2 * s + k + 1] for s in range(4)]),
            (slice(FINE, PAD), [last[k * REST : (k + 1) * REST, s : s + 1] for s in range(4)]),
        ):
            source = slice(k * PAD + rows.start, k * PAD + rows.stop)
            top = jnp.maximum(jnp.maximum(columns[0], columns[1]), jnp.maximum(columns[2], columns[3]))
            weights = [jnp.exp2(one - top) for one in columns]
            total = weights[0] + weights[1] + weights[2] + weights[3]
            acc = sum(weights[s] * load_refs[s][source].astype(F32) for s in range(4))
            out_ref[rows] = (acc * jnp.where(top < -1e28, 0.0, 1.0 / total)).astype(BF16)


def project_kernel(at_ref, mine_ref, other_ref, wo_ref, dy0_ref, dy1_ref, dy2_ref, dy3_ref, *refs):
    out_refs, keep_ref, send_ref, dwo_ref = refs[0:4], *refs[4:7]
    e, h, zr, x, c = (at_ref[i] for i in range(5))
    mine, other = mine_ref[...], other_ref[...]
    even = e == 0
    attn = jnp.concatenate([jnp.where(even, mine, other), jnp.where(even, other, mine)], axis=1)
    for s in range(NH):
        at = -s % NH * WIDE
        part = jnp.dot(attn, wo_ref[:, at : at + WIDE], preferred_element_type=F32)
        out_refs[s][...] = part[0:ROWS].astype(BF16)
    for s, ref in enumerate((dy0_ref, dy1_ref, dy2_ref, dy3_ref)):
        dwo_ref[s] = lax.dot_general(ref[...], attn[0:ROWS], FIRST, preferred_element_type=F32).astype(BF16)
    for ref, core in ((keep_ref, c), (send_ref, 1 - c)):
        for i, xt in enumerate((0, 1 + 2 * core, 3 - 2 * core, 2)):
            for et in range(2):
                for t in range(4):
                    s = lax.rem(h - jnp.bitwise_xor(zr, t) + NH, NH)
                    row = lax.rem(e + et, 2) * 256 + jnp.bitwise_xor(x, xt) * 64 + core * COLS
                    to = slice((et * 4 + t) * COLS, (et * 4 + t + 1) * COLS)
                    ref[i, to] = dwo_ref[s, pl.ds(pl.multiple_of(row, COLS), COLS)]


def split_up(total, mine, theirs, keep_ref, send_ref):
    rows = total.shape[1]
    for at in range(len(mine)):
        keep_ref[at * rows : (at + 1) * rows] = total[mine[at]]
        send_ref[at * rows : (at + 1) * rows] = total[theirs[at]].astype(BF16)


def core_kernel(keep_ref, got_ref, *refs):
    total = keep_ref[...].astype(F32) + got_ref[...].astype(F32)
    split_up(total[0:4], (0, 3), (1, 2), refs[0], refs[1])
    split_up(total[4:8], (0, 1), (3, 2), refs[2], refs[3])


def dwo_kernel(keep_ref, got_ref, mine_ref, send_ref):
    total = keep_ref[...].astype(F32) + got_ref[...].astype(F32)
    split_up(total, (0, 1), (2, 3), mine_ref, send_ref)


def middle_kernel(*refs):
    count = len(refs) // 4
    for i in range(count):
        keep_ref, got_ref = refs[2 * i : 2 * i + 2]
        mine_ref, send_ref = refs[2 * (count + i) : 2 * (count + i) + 2]
        rows = mine_ref.shape[0]
        total = keep_ref[...] + got_ref[...].astype(F32)
        mine_ref[...] = total[0:rows]
        send_ref[...] = total[rows : 2 * rows].astype(BF16)


def ring_kernel(mine_ref, got_ref, keep_ref, send_ref):
    total = mine_ref[...] + got_ref[...].astype(F32)
    for et in range(2):
        at = et * 4 * COLS
        to = et * 2 * COLS
        keep_ref[to : to + 2 * COLS] = total[at : at + 2 * COLS]
        send_ref[to : to + COLS] = total[at + 3 * COLS : at + 4 * COLS].astype(BF16)
        send_ref[to + COLS : to + 2 * COLS] = total[at + 2 * COLS : at + 3 * COLS].astype(BF16)


def half_kernel(keep_ref, got_ref, out_ref, send_ref):
    total = keep_ref[...] + got_ref[...].astype(F32)
    for et in range(2):
        out_ref[et * COLS : (et + 1) * COLS] = total[et * 2 * COLS : (et * 2 + 1) * COLS]
        send_ref[et * COLS : (et + 1) * COLS] = total[(et * 2 + 1) * COLS : (et * 2 + 2) * COLS].astype(BF16)


def total_kernel(*refs):
    wkeep_ref, wgot_ref, keep_ref, wmine_ref, send_ref = refs[6:11]
    for i in range(3):
        total = (refs[2 * i][...] + refs[2 * i + 1][...].astype(F32)).astype(BF16)
        keep_ref[:, i * DH : (i + 1) * DH] = total[0:PAD]
        send_ref[i * PAD : (i + 1) * PAD] = total[PAD:PAIR]
    weights = wkeep_ref[...] + wgot_ref[...].astype(F32)
    wmine_ref[...] = weights[0:COLS]
    piece = weights[COLS : 2 * COLS].astype(BF16)
    send_ref[3 * PAD : 3 * PAD + COLS] = piece[:, 0:DH]
    send_ref[3 * PAD + COLS : 3 * PAD + 2 * COLS] = piece[:, DH:FEATS]


def place_kernel(at_ref, mine_ref, wmine_ref, got_ref, dq_ref, dk_ref, dv_ref, dwo_ref):
    even = at_ref[0] == 0
    for i, ref in enumerate((dq_ref, dk_ref, dv_ref)):
        mine = mine_ref[0:ROWS, i * DH : (i + 1) * DH]
        other = got_ref[i * PAD : i * PAD + ROWS]
        ref[:, 0:DH] = jnp.where(even, mine, other)
        ref[:, DH:FEATS] = jnp.where(even, other, mine)
    got = got_ref[3 * PAD : 3 * PAD + 2 * COLS].astype(F32)
    dwo_ref[...] = wmine_ref[...] + jnp.concatenate([got[0:COLS], got[COLS : 2 * COLS]], axis=1)


def shifted(value, axis, size, by):
    return lax.ppermute(value, axis, [(i, (i + by) % size) for i in range(size)])


def swapped(value, axis, size, mask):
    return lax.ppermute(value, axis, [(i, i ^ mask) for i in range(size)])


def by_core(value, axis, flip):
    masks = (3, 1) if flip else (1, 3)
    return lax.ppermute(value, (axis, "c"), [(i, (i // 2 ^ masks[i % 2]) * 2 + i % 2) for i in range(8)])


def around(value, axis):
    return [value] + [shifted(value, axis, 4, s) for s in (1, 2, 3)]


def local(queries, key_rows, value_rows, scale_of, wo, dy):
    axes = ("e", "head", "zr", "x", "c")
    at = jnp.stack([lax.axis_index(name) for name in axes]).astype(jnp.int32)
    ids = jnp.pad(scale_of, (0, 8 * DH - ROWS), constant_values=-1).reshape(8, DH).astype(F32)
    pair = (PAIR, DH)

    keep, send, dy = call(
        pack_kernel,
        "pack",
        [at, jnp.concatenate([queries, key_rows, value_rows, dy], axis=1), ids],
        [shape((3 * PAD, DH))] * 2 + [shape((ROWS, WIDE))],
        scalars=1,
    )
    got = swapped(send, "e", 2, 1)
    dy, send = lax.optimization_barrier((dy, send))
    k, v, q = (jnp.concatenate([keep[i : i + PAD], got[i : i + PAD]], axis=0) for i in (0, PAD, 2 * PAD))
    k_got, v_got = lax.optimization_barrier((swapped(k, "zr", 4, 1), swapped(v, "zr", 4, 3)))
    k, v = jnp.concatenate([k, k_got], axis=0), jnp.concatenate([v, v_got], axis=0)
    dys = [dy, shifted(dy, "head", NH, 1), None, shifted(dy, "head", NH, 3)]
    dy_late, _ = lax.optimization_barrier((dy, got))
    dys[2] = shifted(dy_late, "head", NH, 2)
    q_got = swapped(q, "x", 4, 1)
    _, _, dys, q_got = lax.optimization_barrier((k, v, dys, q_got))
    ks, vs = [k, swapped(k, "zr", 4, 3)], [v, swapped(v, "zr", 4, 1)]
    wo, _ = lax.optimization_barrier((wo, dy))
    at_head = lax.axis_index("head")
    wo = jnp.concatenate(
        [lax.dynamic_slice_in_dim(wo, lax.rem(at_head - s + NH, NH) * WIDE, WIDE, 1) for s in range(NH)], axis=1
    )
    keep, send = call(dattn_kernel, "dattn", [at, *dys, wo, ids], [shape((PAD, DH))] * 2, scalars=1)
    q, send = lax.optimization_barrier((jnp.concatenate([q, q_got], axis=0), send))
    qs = [q, swapped(q, "x", 4, 3)]
    da_got = swapped(send, "e", 2, 1)
    ks[1], vs[1], da_got, qs[1] = lax.optimization_barrier((ks[1], vs[1], da_got, qs[1]))
    da = jnp.concatenate([keep, da_got], axis=0)
    das = [da] + [swapped(da, "x", 4, s) for s in (1, 2, 3)]
    kvs = [jnp.concatenate([ks[i], vs[i]], axis=0) for i in range(2)]
    kvs = kvs + [swapped(one, "c", 2, 1) for one in kvs]

    rows = (NQ, DH)
    o, stat, q, qm, kv, km = call(
        forward_kernel,
        "forward",
        [*qs, *kvs],
        [shape(rows, F32), shape((8, NQ), F32), shape(rows), shape(rows), shape((NK, FEATS)), shape((NK, DH))],
        flops=6 * NQ * NK * DH,
    )
    *loads, da = call(
        share_kernel, "share", [*das, o, stat], [shape((LOAD, DH))] * 4 + [shape(rows)], [pltpu.VMEM((8, NQ), F32)]
    )
    loads = [loads[0]] + [swapped(loads[s], "x", 4, s) for s in (1, 2, 3)]

    keep, send, sums = call(merge_kernel, "merge", loads, [shape((PAD, DH))] * 2 + [shape((8, NQ), F32)])
    other = swapped(send, "e", 2, 1)
    q, send = lax.optimization_barrier((q, send))
    scratch = [pltpu.VMEM((NQ, FEATS), BF16), pltpu.VMEM((NQ, NQ), BF16)]
    sides = [q, qm, da, kv, km, sums]
    dkv_part, dq_part = call(
        functools.partial(backward_kernel, NQ, 0, 2),
        "backward_one",
        sides,
        [shape((2 * BLOCK, FEATS)), shape(rows, F32)],
        scratch,
        flops=4 * NQ * NK * DH,
    )
    other, dq_part = lax.optimization_barrier((other, dq_part))
    *outs, wkeep, wsend = call(
        project_kernel,
        "project",
        [at, keep, other, wo, *dys],
        [shape((ROWS, WIDE))] * 4 + [shape((4, 256, FEATS))] * 2,
        [pltpu.VMEM((4, WIDE, FEATS), BF16)],
        scalars=1,
    )
    wsend, dq_part = lax.optimization_barrier((wsend, dq_part))
    dkv_send, dq_part = call(
        functools.partial(backward_kernel, NQ, 2, 3),
        "backward_two",
        [*sides, dq_part, dkv_part],
        [shape((8, *pair)), shape(rows, F32)],
        scratch,
        flops=2 * NQ * NK * DH,
    )
    wgot, dq_part = lax.optimization_barrier((swapped(wsend, "c", 2, 1), dq_part))
    wkeep, wsend = call(
        dwo_kernel, "dwo", [wkeep, wgot], [shape((512, FEATS), F32), shape((512, FEATS))]
    )
    wsend, dq_part = lax.optimization_barrier((wsend, dq_part))
    twice = (2 * PAIR, DH)
    dkv_keep, dq_keep, dq_send = call(
        functools.partial(backward_kernel, 0, 0, 3),
        "backward_three",
        [*sides, dq_part],
        [shape((8, *pair)), shape(twice, F32), shape(twice)],
        scratch,
        flops=6 * NQ * NK * DH,
    )
    dk_keep, dk_send, dv_keep, dv_send = call(
        core_kernel, "core", [dkv_keep, swapped(dkv_send, "c", 2, 1)], [shape(twice, F32), shape(twice)] * 2
    )
    wgot, dk_send = lax.optimization_barrier((by_core(wsend, "x", 1), dk_send))
    wkeep, wsend = call(
        middle_kernel, "middle_dwo", [wkeep, wgot], [shape((256, FEATS), F32), shape((256, FEATS))]
    )
    wsend, outs[1], outs[3] = lax.optimization_barrier((wsend, outs[1], outs[3]))
    landed = [swapped(dk_send, "zr", 4, 1), swapped(dv_send, "zr", 4, 3), swapped(dq_send, "x", 4, 1)]
    landed += [by_core(wsend, "x", 0), shifted(outs[1], "head", NH, 1), shifted(outs[3], "head", NH, 3)]
    dk_got, dv_got, dq_got, wgot, out_one, out_three = lax.optimization_barrier(landed)
    wkeep, wsend = call(
        ring_kernel,
        "ring",
        [wkeep, wgot],
        [shape((128, FEATS), F32), shape((128, FEATS))],
    )
    dk, dk_send, dv, dv_send, dq, dq_send = call(
        middle_kernel,
        "middle",
        [dk_keep, dk_got, dv_keep, dv_got, dq_keep, dq_got],
        [shape(pair, F32), shape(pair)] * 3,
    )
    wgot, dq_got = swapped(wsend, "zr", 4, 3), swapped(dq_send, "x", 4, 3)
    dk_got, dv_got = swapped(dk_send, "zr", 4, 3), swapped(dv_send, "zr", 4, 1)
    wkeep, wsend = call(half_kernel, "half", [wkeep, wgot], [shape((64, FEATS), F32), shape((64, FEATS))])
    out_two = shifted(outs[2], "head", NH, 2)
    block_out = sum(one.astype(F32) for one in (outs[0], out_one, out_two, out_three)).astype(BF16)
    keep, wkeep, send = call(
        total_kernel,
        "total",
        [dq, dq_got, dk, dk_got, dv, dv_got]
        + [wkeep, swapped(wsend, "zr", 4, 1)],
        [shape((PAD, 3 * DH)), shape((COLS, FEATS), F32), shape((3 * PAD + 2 * COLS, DH))],
    )
    dq, dk, dv, dwo = call(
        place_kernel,
        "place",
        [at, keep, wkeep, swapped(send, "e", 2, 1)],
        [shape((ROWS, FEATS))] * 3 + [shape((COLS, FEATS), F32)],
        scalars=1,
    )
    return (block_out, dq, dk, dv, dwo.T)


def solution(mesh):
    fine = Mesh(mesh.devices.reshape(4, 2, 4, 2, NH), ("zr", "e", "x", "c", "head"))
    seq = ("zr", "e", "x", "c")
    placed = (
        P(seq, "head"),
        P(seq, "head"),
        P(seq, "head"),
        P(seq),
        P("head", None),
        P(seq, "head"),
    )
    return jax.shard_map(
        local,
        mesh=fine,
        in_specs=placed,
        out_specs=(
            P(seq, "head"),
            P(seq, "head"),
            P(seq, "head"),
            P(seq, "head"),
            P("head", seq),
        ),
        check_vma=False,
    )
```

```python
import functools
import math

import jax
import jax.numpy as jnp
from jax import lax
from jax.experimental import pallas as pl
from jax.experimental.pallas import tpu as pltpu
from jax.sharding import Mesh, PartitionSpec as P

DH = 128
ROWS = 136
PAD = 144
FINE = 128
REST = PAD - FINE
PAIR = 2 * PAD
NH = 4
QHALF = 8
NQ = QHALF * PAD
NK = 2 * NQ
QREST = QHALF * FINE
SUMS = 80
LOAD = PAIR + SUMS
FEATS = 2 * DH
MODEL = 2048
WIDE = MODEL // NH
COLS = 32
BLOCK = 384
BIG = -1e30
SCALE = DH ** (-0.5)
UNIT = SCALE * math.log2(math.e)
F32 = jnp.float32
BF16 = jnp.bfloat16
LAST = (((1,), (1,)), ((), ()))
FIRST = (((0,), (0,)), ((), ()))
PARAMS = pltpu.CompilerParams(vmem_limit_bytes=48 << 20)
VMEM = pl.BlockSpec(memory_space=pltpu.VMEM)
SMEM = pl.BlockSpec(memory_space=pltpu.SMEM)


def shape(dims, kind=BF16):
    return jax.ShapeDtypeStruct(dims, kind)


def call(kernel, name, ins, outs, scratch=(), scalars=0, flops=0):
    cost = pl.CostEstimate(flops=flops, bytes_accessed=1 << 20, transcendentals=0) if flops else None
    return pl.pallas_call(
        kernel,
        in_specs=[SMEM] * scalars + [VMEM] * (len(ins) - scalars),
        out_shape=outs,
        scratch_shapes=list(scratch),
        compiler_params=PARAMS,
        cost_estimate=cost,
        name=name,
    )(*ins)


def by_parity(e, first, second, keep_ref, send_ref):
    @pl.when(e == 0)
    def _():
        keep_ref[...] = first
        send_ref[...] = second

    @pl.when(e == 1)
    def _():
        keep_ref[...] = second
        send_ref[...] = first


def pack_kernel(at_ref, all_ref, ids_ref, keep_ref, send_ref, dy_ref):
    ids = ids_ref[...].astype(BF16)
    zero = jnp.zeros((8, DH), BF16)
    heads = []
    for head in range(2):
        q, k, v = (all_ref[:, i * FEATS + head * DH : i * FEATS + (head + 1) * DH] for i in range(3))
        heads.append(jnp.concatenate([k, ids, v, zero, q, ids], axis=0))
    by_parity(at_ref[0], heads[0], heads[1], keep_ref, send_ref)
    dy_ref[...] = all_ref[:, 3 * FEATS : 3 * FEATS + WIDE]


def dattn_kernel(at_ref, *refs):
    dy_refs, (wo_ref, ids_ref, keep_ref, send_ref) = refs[0:4], refs[4:]
    acc = jnp.zeros((ROWS, FEATS), F32)
    for s, ref in enumerate(dy_refs):
        block = wo_ref[:, s * WIDE : (s + 1) * WIDE]
        acc = acc + lax.dot_general(ref[...], block, LAST, preferred_element_type=F32)
    ids = ids_ref[...].T
    real = jnp.concatenate([ids[:, 0:1], ids[0:8, 1:2]], axis=0) >= 0.0
    acc = jnp.where(real, acc, 0.0).astype(BF16)
    acc = jnp.concatenate([acc, jnp.zeros((PAD - ROWS, FEATS), BF16)], axis=0)
    by_parity(at_ref[0], acc[:, 0:DH], acc[:, DH:FEATS], keep_ref, send_ref)


def pairs_of(refs, slots, top):
    found = [None] * 4
    for i, slot in enumerate(slots):
        found[slot] = (refs[i // 2], top + i % 2 * PAIR)
    return found


def assemble(pairs, all_ref, base, cols):
    rest = base + QREST
    for j, (ref, at) in enumerate(pairs):
        for k in range(2):
            half = 2 * j + k
            top = at + k * PAD
            all_ref[base + half * FINE : base + (half + 1) * FINE, cols] = ref[top : top + FINE]
            all_ref[rest + half * REST : rest + (half + 1) * REST, cols] = ref[top + FINE : top + PAD]


def take_pair(value, j):
    pieces = []
    for half in (2 * j, 2 * j + 1):
        pieces.append(value[half * FINE : (half + 1) * FINE])
        pieces.append(value[QREST + half * REST : QREST + (half + 1) * REST])
    return jnp.concatenate(pieces, axis=0)


def masks(pairs, mask_ref, base, is_query):
    fine, last = [], []
    for ref, at in pairs:
        for k in range(2):
            rows = ref[at + k * PAD + FINE : at + (k + 1) * PAD].astype(F32)
            fine.append(rows[8:9])
            last.append(rows[9:10])
    fine = jnp.concatenate(fine, axis=0).T
    last = jnp.concatenate(last, axis=0).T
    rest = base + QREST

    def encode(column):
        lane = lax.broadcasted_iota(jnp.int32, (column.shape[0], DH), 1).astype(F32)
        if is_query:
            hidden = ((lane > column) & (lane < 13.0)) | (lane == 13.0)
            return jnp.where(hidden, BIG, 0.0).astype(BF16)
        return jnp.where(lane == jnp.where(column < 0.0, 13.0, column), 1.0, 0.0).astype(BF16)

    for half in range(2 * len(pairs)):
        mask_ref[base + half * FINE : base + (half + 1) * FINE] = encode(fine[:, half : half + 1])
        mask_ref[rest + half * REST : rest + (half + 1) * REST] = encode(last[0:REST, half : half + 1])


def in_three(row):
    high = row.astype(BF16).astype(F32)
    middle = (row - high).astype(BF16).astype(F32)
    return [high, middle, row - high - middle]


def forward_kernel(*refs):
    o_ref, stat_ref, q_ref, qm_ref, kv_ref, km_ref = refs[6:12]
    left, right = slice(0, DH), slice(DH, FEATS)
    queries = pairs_of(refs[0:2], (0, 1, 3, 2), 0)
    assemble(queries, q_ref, 0, left)
    masks(queries, qm_ref, 0, True)
    for base, parts in ((0, refs[2:4]), (NQ, refs[4:6])):
        keys = pairs_of(parts, (0, 1, 3, 2), 0)
        assemble(keys, kv_ref, base, left)
        assemble(pairs_of(parts, (0, 3, 1, 2), 2 * PAIR), kv_ref, base, right)
        masks(keys, km_ref, base, False)
    k_ext = jnp.concatenate([kv_ref[:, 0:DH], km_ref[...]], axis=1)
    lane = lax.broadcasted_iota(jnp.int32, (BLOCK, DH), 1)
    for block in range(NQ // BLOCK):
        rows = slice(block * BLOCK, (block + 1) * BLOCK)
        q_ext = jnp.concatenate([q_ref[rows], qm_ref[rows]], axis=1)
        s = lax.dot_general(q_ext, k_ext, LAST, preferred_element_type=F32)
        top = jnp.max(s, axis=1, keepdims=True)
        p = jnp.exp2((s - top) * UNIT)
        total = jnp.sum(p, axis=1, keepdims=True)
        o = jnp.dot(p.astype(BF16), kv_ref[:, DH:FEATS], preferred_element_type=F32) / total
        o_ref[rows] = o
        lse = top * UNIT + jnp.log2(total)
        stat_ref[:, rows] = jnp.where(lane == 0, lse, 0.0).T[0:8]


def share_kernel(*refs):
    o_ref, stat_ref, load_refs, da_ref, delta_ref = refs[4], refs[5], refs[6:10], refs[10], refs[11]
    assemble([(ref, 0) for ref in refs[0:4]], da_ref, 0, slice(0, DH))
    lane = lax.broadcasted_iota(jnp.int32, (BLOCK, DH), 1)
    for block in range(NQ // BLOCK):
        rows = slice(block * BLOCK, (block + 1) * BLOCK)
        share = jnp.sum(o_ref[rows] * da_ref[rows].astype(F32), axis=1, keepdims=True)
        delta_ref[:, rows] = jnp.where(lane == 0, share, 0.0).T[0:8]
    none = jnp.zeros((2, NQ), F32)
    sums = jnp.concatenate(in_three(stat_ref[0:1]) + in_three(delta_ref[0:1]) + [none], axis=0)
    tiles = [sums[:, i * DH : (i + 1) * DH] for i in range(NQ // DH)] + [jnp.zeros((8, DH), F32)]
    sums = jnp.concatenate(tiles, axis=0).astype(BF16)
    for j in range(4):
        load_refs[j][0:PAIR] = take_pair(o_ref, j).astype(BF16)
        load_refs[j][PAIR:LOAD] = sums


def row_sums(load_refs):
    lses, shares = [], []
    odd = lax.broadcasted_iota(jnp.int32, (8, DH), 1) % (4 * REST) >= 2 * REST
    for s, ref in enumerate(load_refs):
        sums = ref[PAIR:LOAD].astype(F32)
        tiles = [sums[8 * i : 8 * i + 8] for i in range(9)]
        last = tiles[8]
        if s % 2 == 1:
            last = jnp.where(odd, pltpu.roll(last, 2 * REST, 1), pltpu.roll(last, FINE - 2 * REST, 1))
        if s >= 2:
            last = pltpu.roll(last, FINE // 2, 1)
        rows = jnp.concatenate([tiles[2 * (j ^ s) + k] for j in range(4) for k in range(2)] + [last], axis=1)
        lses.append(rows[0:1] + rows[1:2] + rows[2:3])
        shares.append(rows[3:4] + rows[4:5] + rows[5:6])
    top = jnp.maximum(jnp.maximum(lses[0], lses[1]), jnp.maximum(lses[2], lses[3]))
    weights = [jnp.exp2(one - top) for one in lses]
    total = weights[0] + weights[1] + weights[2] + weights[3]
    delta = sum(weights[s] * shares[s] for s in range(4)) / total
    lse = top + jnp.log2(total)
    return jnp.where(lse < -1e28, 1e30, lse), delta


def backward_kernel(base, first, last, q_ref, qm_ref, da_ref, kv_ref, km_ref, *refs):
    rows_ref, refs = refs[0], refs[1:]
    if first > 0 or base == 0:
        dq_in_ref, refs = refs[0], refs[1:]
    if first > 0:
        rows_in_ref, refs = refs[0], refs[1:]
    out_refs, dkv_ref, ds_ref = refs[:-2], refs[-2], refs[-1]
    lse, delta = rows_ref[0:1], rows_ref[1:2]
    q = q_ref[...]
    da = da_ref[...]
    q_ext = jnp.concatenate([q, qm_ref[...]], axis=1)
    if first > 0:
        dkv_ref[0 : first * BLOCK] = rows_in_ref[...]
    for block in range(first, last):
        rows = slice(block * BLOCK, (block + 1) * BLOCK)
        keys = slice(base + block * BLOCK, base + (block + 1) * BLOCK)
        k_ext = jnp.concatenate([kv_ref[keys, 0:DH], km_ref[keys]], axis=1)
        s = lax.dot_general(k_ext, q_ext, LAST, preferred_element_type=F32)
        p = jnp.exp2(s * UNIT - lse)
        dp = lax.dot_general(kv_ref[keys, DH:FEATS], da, LAST, preferred_element_type=F32)
        ds = (p * (dp - delta)).astype(BF16)
        dkv_ref[rows, DH:FEATS] = jnp.dot(p.astype(BF16), da, preferred_element_type=F32).astype(BF16)
        dkv_ref[rows, 0:DH] = (jnp.dot(ds, q, preferred_element_type=F32) * SCALE).astype(BF16)
        ds_ref[rows] = ds
    if last * BLOCK < NQ:
        out_refs[0][...] = dkv_ref[0 : last * BLOCK]
    else:
        for j in range(4):
            pair = take_pair(dkv_ref, j)
            out_refs[0][j] = pair[:, 0:DH]
            out_refs[0][4 + j] = pair[:, DH:FEATS]
    rows = slice(first * BLOCK, last * BLOCK)
    keys = slice(base + rows.start, base + rows.stop)
    dq = lax.dot_general(ds_ref[rows], kv_ref[keys, 0:DH], FIRST, preferred_element_type=F32)
    if first > 0 or base == 0:
        dq = dq + dq_in_ref[...]
    if base > 0:
        out_refs[1][...] = dq
    else:
        dq = dq * SCALE
        for at, (mine, theirs) in enumerate(((0, 1), (3, 2))):
            out_refs[1][at * PAIR : (at + 1) * PAIR] = take_pair(dq, mine)
            out_refs[2][at * PAIR : (at + 1) * PAIR] = take_pair(dq, theirs).astype(BF16)


def merge_kernel(l0_ref, l1_ref, l2_ref, l3_ref, keep_ref, send_ref, rows_ref):
    load_refs = (l0_ref, l1_ref, l2_ref, l3_ref)
    lse, delta = row_sums(load_refs)
    rows_ref[0:1] = lse
    rows_ref[1:2] = delta
    fine, last = [], []
    for s, ref in enumerate(load_refs):
        sums = ref[PAIR:LOAD].astype(F32)
        rows = sums[0:72]
        lse = [rows[8 * i : 8 * i + 1] + rows[8 * i + 1 : 8 * i + 2] + rows[8 * i + 2 : 8 * i + 3] for i in (2 * s, 2 * s + 1, 8)]
        fine += lse[0:2]
        last.append(lse[2] if s == 0 else pltpu.roll(lse[2], FINE - 2 * REST * s, 1))
    fine = jnp.concatenate(fine, axis=0).T
    last = jnp.concatenate(last + last, axis=0).T
    for k, out_ref in ((0, keep_ref), (1, send_ref)):
        for rows, columns in (
            (slice(0, FINE), [fine[:, 2 * s + k : 2 * s + k + 1] for s in range(4)]),
            (slice(FINE, PAD), [last[k * REST : (k + 1) * REST, s : s + 1] for s in range(4)]),
        ):
            source = slice(k * PAD + rows.start, k * PAD + rows.stop)
            top = jnp.maximum(jnp.maximum(columns[0], columns[1]), jnp.maximum(columns[2], columns[3]))
            weights = [jnp.exp2(one - top) for one in columns]
            total = weights[0] + weights[1] + weights[2] + weights[3]
            acc = sum(weights[s] * load_refs[s][source].astype(F32) for s in range(4))
            out_ref[rows] = (acc * jnp.where(top < -1e28, 0.0, 1.0 / total)).astype(BF16)


def project_kernel(at_ref, mine_ref, other_ref, wo_ref, dy0_ref, dy1_ref, dy2_ref, dy3_ref, *refs):
    out_refs, keep_ref, send_ref, dwo_ref = refs[0:4], *refs[4:7]
    e, h, zr, x, c = (at_ref[i] for i in range(5))
    mine, other = mine_ref[...], other_ref[...]
    even = e == 0
    attn = jnp.concatenate([jnp.where(even, mine, other), jnp.where(even, other, mine)], axis=1)
    for s in range(NH):
        at = -s % NH * WIDE
        part = jnp.dot(attn, wo_ref[:, at : at + WIDE], preferred_element_type=F32)
        out_refs[s][...] = part[0:ROWS].astype(BF16)
    for s, ref in enumerate((dy0_ref, dy1_ref, dy2_ref, dy3_ref)):
        dwo_ref[s] = lax.dot_general(ref[...], attn[0:ROWS], FIRST, preferred_element_type=F32).astype(BF16)
    for ref, core in ((keep_ref, c), (send_ref, 1 - c)):
        for i, xt in enumerate((0, 1 + 2 * core, 3 - 2 * core, 2)):
            for et in range(2):
                for t in range(4):
                    s = lax.rem(h - jnp.bitwise_xor(zr, t) + NH, NH)
                    row = lax.rem(e + et, 2) * 256 + jnp.bitwise_xor(x, xt) * 64 + core * COLS
                    to = slice((et * 4 + t) * COLS, (et * 4 + t + 1) * COLS)
                    ref[i, to] = dwo_ref[s, pl.ds(pl.multiple_of(row, COLS), COLS)]


def split_up(total, mine, theirs, keep_ref, send_ref):
    rows = total.shape[1]
    for at in range(len(mine)):
        keep_ref[at * rows : (at + 1) * rows] = total[mine[at]]
        send_ref[at * rows : (at + 1) * rows] = total[theirs[at]].astype(BF16)


def core_kernel(keep_ref, got_ref, *refs):
    total = keep_ref[...].astype(F32) + got_ref[...].astype(F32)
    split_up(total[0:4], (0, 3), (1, 2), refs[0], refs[1])
    split_up(total[4:8], (0, 1), (3, 2), refs[2], refs[3])


def dwo_kernel(keep_ref, got_ref, mine_ref, send_ref):
    total = keep_ref[...].astype(F32) + got_ref[...].astype(F32)
    split_up(total, (0, 1), (2, 3), mine_ref, send_ref)


def middle_kernel(*refs):
    count = len(refs) // 4
    for i in range(count):
        keep_ref, got_ref = refs[2 * i : 2 * i + 2]
        mine_ref, send_ref = refs[2 * (count + i) : 2 * (count + i) + 2]
        rows = mine_ref.shape[0]
        total = keep_ref[...] + got_ref[...].astype(F32)
        mine_ref[...] = total[0:rows]
        send_ref[...] = total[rows : 2 * rows].astype(BF16)


def ring_kernel(mine_ref, got_ref, keep_ref, send_ref):
    total = mine_ref[...] + got_ref[...].astype(F32)
    for et in range(2):
        at = et * 4 * COLS
        to = et * 2 * COLS
        keep_ref[to : to + 2 * COLS] = total[at : at + 2 * COLS]
        send_ref[to : to + COLS] = total[at + 3 * COLS : at + 4 * COLS].astype(BF16)
        send_ref[to + COLS : to + 2 * COLS] = total[at + 2 * COLS : at + 3 * COLS].astype(BF16)


def half_kernel(keep_ref, got_ref, out_ref, send_ref):
    total = keep_ref[...] + got_ref[...].astype(F32)
    for et in range(2):
        out_ref[et * COLS : (et + 1) * COLS] = total[et * 2 * COLS : (et * 2 + 1) * COLS]
        send_ref[et * COLS : (et + 1) * COLS] = total[(et * 2 + 1) * COLS : (et * 2 + 2) * COLS].astype(BF16)


def total_kernel(*refs):
    wkeep_ref, wgot_ref, keep_ref, wmine_ref, send_ref = refs[6:11]
    for i in range(3):
        total = (refs[2 * i][...] + refs[2 * i + 1][...].astype(F32)).astype(BF16)
        keep_ref[:, i * DH : (i + 1) * DH] = total[0:PAD]
        send_ref[i * PAD : (i + 1) * PAD] = total[PAD:PAIR]
    weights = wkeep_ref[...] + wgot_ref[...].astype(F32)
    wmine_ref[...] = weights[0:COLS]
    piece = weights[COLS : 2 * COLS].astype(BF16)
    send_ref[3 * PAD : 3 * PAD + COLS] = piece[:, 0:DH]
    send_ref[3 * PAD + COLS : 3 * PAD + 2 * COLS] = piece[:, DH:FEATS]


def place_kernel(at_ref, mine_ref, wmine_ref, got_ref, dq_ref, dk_ref, dv_ref, dwo_ref):
    even = at_ref[0] == 0
    for i, ref in enumerate((dq_ref, dk_ref, dv_ref)):
        mine = mine_ref[0:ROWS, i * DH : (i + 1) * DH]
        other = got_ref[i * PAD : i * PAD + ROWS]
        ref[:, 0:DH] = jnp.where(even, mine, other)
        ref[:, DH:FEATS] = jnp.where(even, other, mine)
    got = got_ref[3 * PAD : 3 * PAD + 2 * COLS].astype(F32)
    dwo_ref[...] = wmine_ref[...] + jnp.concatenate([got[0:COLS], got[COLS : 2 * COLS]], axis=1)


def shifted(value, axis, size, by):
    return lax.ppermute(value, axis, [(i, (i + by) % size) for i in range(size)])


def swapped(value, axis, size, mask):
    return lax.ppermute(value, axis, [(i, i ^ mask) for i in range(size)])


def by_core(value, axis, flip):
    masks = (3, 1) if flip else (1, 3)
    return lax.ppermute(value, (axis, "c"), [(i, (i // 2 ^ masks[i % 2]) * 2 + i % 2) for i in range(8)])


def around(value, axis):
    return [value] + [shifted(value, axis, 4, s) for s in (1, 2, 3)]


def local(queries, key_rows, value_rows, scale_of, wo, dy):
    axes = ("e", "head", "zr", "x", "c")
    at = jnp.stack([lax.axis_index(name) for name in axes]).astype(jnp.int32)
    ids = jnp.pad(scale_of, (0, 8 * DH - ROWS), constant_values=-1).reshape(8, DH).astype(F32)
    pair = (PAIR, DH)

    keep, send, dy = call(
        pack_kernel,
        "pack",
        [at, jnp.concatenate([queries, key_rows, value_rows, dy], axis=1), ids],
        [shape((3 * PAD, DH))] * 2 + [shape((ROWS, WIDE))],
        scalars=1,
    )
    got = swapped(send, "e", 2, 1)
    dy, send = lax.optimization_barrier((dy, send))
    k, v, q = (jnp.concatenate([keep[i : i + PAD], got[i : i + PAD]], axis=0) for i in (0, PAD, 2 * PAD))
    k_got, v_got = lax.optimization_barrier((swapped(k, "zr", 4, 1), swapped(v, "zr", 4, 3)))
    k, v = jnp.concatenate([k, k_got], axis=0), jnp.concatenate([v, v_got], axis=0)
    dys = [dy, shifted(dy, "head", NH, 1), None, shifted(dy, "head", NH, 3)]
    dy_late, _ = lax.optimization_barrier((dy, got))
    dys[2] = shifted(dy_late, "head", NH, 2)
    q_got = swapped(q, "x", 4, 1)
    _, _, dys, q_got = lax.optimization_barrier((k, v, dys, q_got))
    ks, vs = [k, swapped(k, "zr", 4, 3)], [v, swapped(v, "zr", 4, 1)]
    wo, _ = lax.optimization_barrier((wo, dy))
    at_head = lax.axis_index("head")
    wo = jnp.concatenate(
        [lax.dynamic_slice_in_dim(wo, lax.rem(at_head - s + NH, NH) * WIDE, WIDE, 1) for s in range(NH)], axis=1
    )
    keep, send = call(dattn_kernel, "dattn", [at, *dys, wo, ids], [shape((PAD, DH))] * 2, scalars=1)
    q, send = lax.optimization_barrier((jnp.concatenate([q, q_got], axis=0), send))
    qs = [q, swapped(q, "x", 4, 3)]
    da_got = swapped(send, "e", 2, 1)
    ks[1], vs[1], da_got, qs[1] = lax.optimization_barrier((ks[1], vs[1], da_got, qs[1]))
    da = jnp.concatenate([keep, da_got], axis=0)
    das = [da] + [swapped(da, "x", 4, s) for s in (1, 2, 3)]
    kvs = [jnp.concatenate([ks[i], vs[i]], axis=0) for i in range(2)]
    kvs = kvs + [swapped(one, "c", 2, 1) for one in kvs]

    rows = (NQ, DH)
    o, stat, q, qm, kv, km = call(
        forward_kernel,
        "forward",
        [*qs, *kvs],
        [shape(rows, F32), shape((8, NQ), F32), shape(rows), shape(rows), shape((NK, FEATS)), shape((NK, DH))],
        flops=6 * NQ * NK * DH,
    )
    *loads, da = call(
        share_kernel, "share", [*das, o, stat], [shape((LOAD, DH))] * 4 + [shape(rows)], [pltpu.VMEM((8, NQ), F32)]
    )
    loads = [loads[0]] + [swapped(loads[s], "x", 4, s) for s in (1, 2, 3)]

    keep, send, sums = call(merge_kernel, "merge", loads, [shape((PAD, DH))] * 2 + [shape((8, NQ), F32)])
    other = swapped(send, "e", 2, 1)
    q, send = lax.optimization_barrier((q, send))
    scratch = [pltpu.VMEM((NQ, FEATS), BF16), pltpu.VMEM((NQ, NQ), BF16)]
    sides = [q, qm, da, kv, km, sums]
    dkv_part, dq_part = call(
        functools.partial(backward_kernel, NQ, 0, 2),
        "backward_one",
        sides,
        [shape((2 * BLOCK, FEATS)), shape(rows, F32)],
        scratch,
        flops=4 * NQ * NK * DH,
    )
    other, dq_part = lax.optimization_barrier((other, dq_part))
    *outs, wkeep, wsend = call(
        project_kernel,
        "project",
        [at, keep, other, wo, *dys],
        [shape((ROWS, WIDE))] * 4 + [shape((4, 256, FEATS))] * 2,
        [pltpu.VMEM((4, WIDE, FEATS), BF16)],
        scalars=1,
    )
    wsend, dq_part = lax.optimization_barrier((wsend, dq_part))
    dkv_send, dq_part = call(
        functools.partial(backward_kernel, NQ, 2, 3),
        "backward_two",
        [*sides, dq_part, dkv_part],
        [shape((8, *pair)), shape(rows, F32)],
        scratch,
        flops=2 * NQ * NK * DH,
    )
    wgot, dq_part = lax.optimization_barrier((swapped(wsend, "c", 2, 1), dq_part))
    wkeep, wsend = call(
        dwo_kernel, "dwo", [wkeep, wgot], [shape((512, FEATS), F32), shape((512, FEATS))]
    )
    wsend, dq_part = lax.optimization_barrier((wsend, dq_part))
    twice = (2 * PAIR, DH)
    dkv_keep, dq_keep, dq_send = call(
        functools.partial(backward_kernel, 0, 0, 3),
        "backward_three",
        [*sides, dq_part],
        [shape((8, *pair)), shape(twice, F32), shape(twice)],
        scratch,
        flops=6 * NQ * NK * DH,
    )
    dk_keep, dk_send, dv_keep, dv_send = call(
        core_kernel, "core", [dkv_keep, swapped(dkv_send, "c", 2, 1)], [shape(twice, F32), shape(twice)] * 2
    )
    wgot, dk_send = lax.optimization_barrier((by_core(wsend, "x", 1), dk_send))
    wkeep, wsend = call(
        middle_kernel, "middle_dwo", [wkeep, wgot], [shape((256, FEATS), F32), shape((256, FEATS))]
    )
    wsend, outs[1], outs[3] = lax.optimization_barrier((wsend, outs[1], outs[3]))
    landed = [swapped(dk_send, "zr", 4, 1), swapped(dv_send, "zr", 4, 3), swapped(dq_send, "x", 4, 1)]
    landed += [by_core(wsend, "x", 0), shifted(outs[1], "head", NH, 1), shifted(outs[3], "head", NH, 3)]
    dk_got, dv_got, dq_got, wgot, out_one, out_three = lax.optimization_barrier(landed)
    wkeep, wsend = call(
        ring_kernel,
        "ring",
        [wkeep, wgot],
        [shape((128, FEATS), F32), shape((128, FEATS))],
    )
    dk, dk_send, dv, dv_send, dq, dq_send = call(
        middle_kernel,
        "middle",
        [dk_keep, dk_got, dv_keep, dv_got, dq_keep, dq_got],
        [shape(pair, F32), shape(pair)] * 3,
    )
    wgot, out_two = lax.optimization_barrier((swapped(wsend, "zr", 4, 3), shifted(outs[2], "head", NH, 2)))
    dk_got, dv_got = swapped(dk_send, "zr", 4, 3), swapped(dv_send, "zr", 4, 1)
    wkeep, wsend = call(half_kernel, "half", [wkeep, wgot], [shape((64, FEATS), F32), shape((64, FEATS))])
    wsend, dq_send = lax.optimization_barrier((wsend, dq_send))
    dq_got = swapped(dq_send, "x", 4, 3)
    block_out = sum(one.astype(F32) for one in (outs[0], out_one, out_two, out_three)).astype(BF16)
    keep, wkeep, send = call(
        total_kernel,
        "total",
        [dq, dq_got, dk, dk_got, dv, dv_got]
        + [wkeep, swapped(wsend, "zr", 4, 1)],
        [shape((PAD, 3 * DH)), shape((COLS, FEATS), F32), shape((3 * PAD + 2 * COLS, DH))],
    )
    dq, dk, dv, dwo = call(
        place_kernel,
        "place",
        [at, keep, wkeep, swapped(send, "e", 2, 1)],
        [shape((ROWS, FEATS))] * 3 + [shape((COLS, FEATS), F32)],
        scalars=1,
    )
    return (block_out, dq, dk, dv, dwo.T)


def solution(mesh):
    fine = Mesh(mesh.devices.reshape(4, 2, 4, 2, NH), ("zr", "e", "x", "c", "head"))
    seq = ("zr", "e", "x", "c")
    placed = (
        P(seq, "head"),
        P(seq, "head"),
        P(seq, "head"),
        P(seq),
        P("head", None),
        P(seq, "head"),
    )
    return jax.shard_map(
        local,
        mesh=fine,
        in_specs=placed,
        out_specs=(
            P(seq, "head"),
            P(seq, "head"),
            P(seq, "head"),
            P(seq, "head"),
            P("head", seq),
        ),
        check_vma=False,
    )
```
